128 devices in a mesh: section: 2 (over z_hi), rep: 4 (over x), shard: 16 (over y, z_lo, core).
Axes of the slice: x: 4, y: 4, z: 4 (z_hi: 2, z_lo: 2; z = z_hi * 2 + z_lo), core: 2. Of those that a mesh axis runs over, the one named last changes fastest.
Arguments:
- inputs: bfloat16 [2, 4, 1024, 1024], P(None, 'rep', 'shard'), may hold values from -6 to 6
- cotangent: bfloat16 [2, 4, 1024, 1024], P(None, 'rep', 'shard'), may hold values from -6 to 6
- norm_in: bfloat16 [2, 1024], P('section', 'shard'), may hold values from 0.5 to 1.5
- w_in: bfloat16 [2, 1024, 3352], P('section', 'shard'), may hold values from -0.1875 to 0.1875
- conv_w: bfloat16 [2, 4, 1792], P('section', None, 'shard'), may hold values from -0.5 to 0.5
- conv_b: bfloat16 [2, 1792], P('section', 'shard'), may hold values from -0.29882812 to 0.29882812
- dt_bias: float32 [2, 24], P('section'), may hold values from -6 to -2
- a_log: float32 [2, 24], P('section'), may hold values from -1 to 2
- skip_gain: float32 [2, 24], P('section'), may hold values from 0.5 to 1.5
- norm_ssm: bfloat16 [2, 1536], P('section', 'shard'), may hold values from 0.5 to 1.5
- w_out: bfloat16 [2, 1536, 1024], P('section', 'shard'), may hold values from -0.15625 to 0.15625
- query_weight: bfloat16 [2, 1024, 512], P('section', 'shard'), may hold values from -0.1875 to 0.1875
- key_weight: bfloat16 [2, 1024, 128], P('section', 'shard'), may hold values from -0.1875 to 0.1875
- value_weight: bfloat16 [2, 1024, 128], P('section', 'shard'), may hold values from -0.1875 to 0.1875
- output_weight: bfloat16 [2, 512, 1024], P('section', 'shard'), may hold values from -0.75 to 0.75
- norm_mid: bfloat16 [2, 1024], P('section', 'shard'), may hold values from 0.5 to 1.5
- w_gate: bfloat16 [2, 1024, 2048], P('section', 'shard'), may hold values from -0.1875 to 0.1875
- w_up: bfloat16 [2, 1024, 2048], P('section', 'shard'), may hold values from -0.1875 to 0.1875
- w_down: bfloat16 [2, 2048, 1024], P('section', 'shard'), may hold values from -0.125 to 0.125
Outputs:
- section_out: bfloat16 [2, 2, 4, 1024, 1024], P('section', None, 'rep', 'shard')
- input_grad: float32 [2, 2, 4, 1024, 1024], P('section', None, 'rep', 'shard')
- grad_norm_in: float32 [2, 1024], P('section', 'shard')
- grad_w_in: float32 [2, 1024, 3352], P('section', 'shard')
- grad_conv_w: float32 [2, 4, 1792], P('section', None, 'shard')
- grad_conv_b: float32 [2, 1792], P('section', 'shard')
- grad_dt_bias: float32 [2, 24], P('section')
- grad_a_log: float32 [2, 24], P('section')
- grad_skip: float32 [2, 24], P('section')
- grad_norm_ssm: float32 [2, 1536], P('section', 'shard')
- grad_w_out: float32 [2, 1536, 1024], P('section', 'shard')
- grad_w_q: float32 [2, 1024, 512], P('section', 'shard')
- grad_w_k: float32 [2, 1024, 128], P('section', 'shard')
- grad_w_v: float32 [2, 1024, 128], P('section', 'shard')
- grad_w_o: float32 [2, 512, 1024], P('section', 'shard')
- grad_norm_mid: float32 [2, 1024], P('section', 'shard')
- grad_w_gate: float32 [2, 1024, 2048], P('section', 'shard')
- grad_w_up: float32 [2, 1024, 2048], P('section', 'shard')
- grad_w_down: float32 [2, 2048, 1024], P('section', 'shard')
The draws below stay inside these ranges and needn't reach their ends.
All inputs are finite; a program needn't handle non-finite values.
Results may differ from the reference program's by a relative error of at most 0.03.
Values may be sent and summed in bfloat16 or wider, within the bound.
No kernel may reach another device: no remote copies, remote signals or barrier semaphores. Data moves between devices by JAX's collectives and lax.ppermute only.
A program may use at most 256 MiB of HBM per device.

```python
import math
import jax
import jax.numpy as jnp
from jax import lax

MODEL_WIDTH = 1024
NH = 24
HD = 64
NS = 128
QUERY_HEADS = 8
KEY_VALUE_HEADS = 2
ATTN_HEAD_SIZE = 64
FF = 2048
CONV = 4
MB = 2
SEQ = 1024
LOCAL = 64
N_REP = 4


def block_levels(rng, extent, cuts, least, largest):
    loudness = 1.0
    for dim, blocks in cuts:
        heights = jax.random.uniform(jax.random.fold_in(jax.random.fold_in(rng, 6), dim), (blocks,), jnp.float32, least / len(cuts), largest / len(cuts))
        loudness = loudness * jnp.repeat(jnp.exp(heights), extent[dim] // blocks).reshape((-1,) + (1,) * (len(extent) - 1 - dim))
    return loudness


def scatter_about(stream_key, extent, deviation, bound, cuts=(), dtype=jnp.bfloat16):
    drawn = jax.random.normal(stream_key, extent, jnp.float32) * deviation
    if len(cuts) > 0:
        drawn = block_levels(stream_key, extent, cuts, -0.22, 0.18) * drawn
    return jnp.clip(drawn, min=-bound, max=bound).astype(dtype)


def setup_inputs(seed: int = 0) -> dict:
    key_list = jax.random.split(jax.random.key(seed), 20)
    return {
        "inputs": scatter_about(key_list[0], (MB, N_REP, SEQ, MODEL_WIDTH), 1.0, 6.0, ((1, 4), (2, 16))),
        "cotangent": scatter_about(key_list[1], (MB, N_REP, SEQ, MODEL_WIDTH), 1.0, 6.0, ((1, 4), (2, 16))),
        "norm_in": jnp.clip(1.0 + 0.1 * jax.random.normal(key_list[2], (2, MODEL_WIDTH), jnp.float32), 0.5, 1.5).astype(jnp.bfloat16),
        "w_in": scatter_about(key_list[3], (2, MODEL_WIDTH, 2 * NH * HD + 2 * NS + NH), MODEL_WIDTH ** -0.5, 0.1875, ((0, 2), (1, 16))),
        "conv_w": jnp.clip(jax.random.uniform(key_list[4], (2, CONV, NH * HD + 2 * NS), jnp.float32, -0.5, 0.5) * block_levels(key_list[4], (2, CONV, NH * HD + 2 * NS), ((0, 2), (2, 16)), -0.4, 0.0), -0.5, 0.5).astype(jnp.bfloat16),
        "conv_b": jnp.clip(jax.random.uniform(key_list[5], (2, NH * HD + 2 * NS), jnp.float32, -0.29882812, 0.29882812) * block_levels(key_list[5], (2, NH * HD + 2 * NS), ((0, 2), (1, 16)), -0.4, 0.0), -0.29882812, 0.29882812).astype(jnp.bfloat16),
        "dt_bias": jnp.clip(-6.0 + 4.0 * jax.random.uniform(key_list[6], (2, NH), jnp.float32) ** block_levels(key_list[6], (2, NH), ((0, 2),), -0.2, 0.2), -6.0, -2.0),
        "a_log": jnp.clip(-1.0 + 3.0 * jax.random.uniform(key_list[7], (2, NH), jnp.float32) ** block_levels(key_list[7], (2, NH), ((0, 2),), -0.2, 0.2), -1.0, 2.0),
        "skip_gain": jnp.clip(0.5 + 1.0 * jax.random.uniform(key_list[8], (2, NH), jnp.float32) ** block_levels(key_list[8], (2, NH), ((0, 2),), -0.2, 0.2), 0.5, 1.5),
        "norm_ssm": jnp.clip(1.0 + 0.1 * jax.random.normal(key_list[9], (2, NH * HD), jnp.float32), 0.5, 1.5).astype(jnp.bfloat16),
        "w_out": scatter_about(key_list[10], (2, NH * HD, MODEL_WIDTH), (NH * HD) ** -0.5, 0.15625, ((0, 2), (1, 16))),
        "query_weight": scatter_about(key_list[11], (2, MODEL_WIDTH, QUERY_HEADS * ATTN_HEAD_SIZE), MODEL_WIDTH ** -0.5, 0.1875, ((0, 2), (1, 16))),
        "key_weight": scatter_about(key_list[12], (2, MODEL_WIDTH, KEY_VALUE_HEADS * ATTN_HEAD_SIZE), MODEL_WIDTH ** -0.5, 0.1875, ((0, 2), (1, 16))),
        "value_weight": scatter_about(key_list[13], (2, MODEL_WIDTH, KEY_VALUE_HEADS * ATTN_HEAD_SIZE), MODEL_WIDTH ** -0.5, 0.1875, ((0, 2), (1, 16))),
        "output_weight": scatter_about(key_list[14], (2, QUERY_HEADS * ATTN_HEAD_SIZE, MODEL_WIDTH), (QUERY_HEADS * ATTN_HEAD_SIZE // 8) ** -0.5, 0.75, ((0, 2), (1, 16))),
        "norm_mid": jnp.clip(1.0 + 0.1 * jax.random.normal(key_list[15], (2, MODEL_WIDTH), jnp.float32), 0.5, 1.5).astype(jnp.bfloat16),
        "w_gate": scatter_about(key_list[16], (2, MODEL_WIDTH, FF), MODEL_WIDTH ** -0.5, 0.1875, ((0, 2), (1, 16))),
        "w_up": scatter_about(key_list[17], (2, MODEL_WIDTH, FF), MODEL_WIDTH ** -0.5, 0.1875, ((0, 2), (1, 16))),
        "w_down": scatter_about(key_list[18], (2, FF, MODEL_WIDTH), FF ** -0.5, 0.125, ((0, 2), (1, 16))),
    }


EPSILON = 1e-05

@jax.custom_vjp
def reduced_precision(v):
    return lax.optimization_barrier(v.astype(jnp.bfloat16)).astype(jnp.float32)

@jax.custom_vjp
def reduced_backward(v):
    return v

def low_keep(v):
    return (reduced_precision(v), None)

def low_pass(kept, grad):
    return (grad,)

def back_keep(v):
    return (v, None)

def back_low(kept, grad):
    return (reduced_precision(grad),)
reduced_precision.defvjp(low_keep, low_pass)
reduced_backward.defvjp(back_keep, back_low)

def matrix_product(former, latter):
    return jnp.dot(former, latter, precision=lax.Precision.HIGHEST)

def rms_scale(values, norm_gain):
    return values * lax.rsqrt(lax.optimization_barrier(jnp.mean(values * values, axis=-1, keepdims=True)) + EPSILON) * norm_gain

def mixer_block(state_in, pieces):
    states_in, input_map, output_map, step_size, log_decay = pieces
    sequence_length = states_in.shape[0]
    cumulative = jnp.cumsum(log_decay, axis=0)
    from_start = jnp.einsum('tn,hdn->thd', output_map, state_in, precision=lax.Precision.HIGHEST) * jnp.exp(cumulative)[:, :, None]
    rows_index = lax.broadcasted_iota(jnp.int32, (sequence_length, sequence_length), 0)
    cols_index = lax.broadcasted_iota(jnp.int32, (sequence_length, sequence_length), 1)
    causal = (cols_index <= rows_index)[:, :, None]
    spread = jnp.where(causal, cumulative[:, None, :] - cumulative[None, :, :], 0.0)
    within = jnp.where(causal, jnp.exp(spread), 0.0)
    coupling = jnp.dot(output_map, input_map.T, precision=lax.Precision.HIGHEST)
    mixing = within * coupling[:, :, None] * step_size[None, :, :]
    local_part = jnp.einsum('tsh,shd->thd', mixing, states_in, precision=lax.Precision.HIGHEST)
    weights_tail = jnp.exp(cumulative[-1][None, :] - cumulative) * step_size
    state_end = jnp.einsum('sh,shd,sn->hdn', weights_tail, states_in, input_map, precision=lax.Precision.HIGHEST)
    state_out = jnp.exp(cumulative[-1])[:, None, None] * state_in + state_end
    return (state_out, from_start + local_part)

def hybrid_layer(hidden_in, params):
    norm_in, w_in, conv_w, conv_b, dt_shift, log_rate, skip_gain, norm_ssm, w_out, query_weight, key_weight, value_weight, output_weight, norm_mid, w_gate, w_up, w_down = params
    sequence_length = hidden_in.shape[0]
    inner_width = NH * HD
    conv_width = inner_width + 2 * NS
    normalized_input = reduced_precision(rms_scale(hidden_in, norm_in))
    project = reduced_backward(matrix_product(normalized_input, w_in))
    gate_raw = project[:, :inner_width]
    conv_in = project[:, inner_width:inner_width + conv_width]
    dt_raw = project[:, inner_width + conv_width:]
    padded = jnp.concatenate([jnp.zeros((CONV - 1, conv_width), jnp.float32), conv_in], axis=0)
    convolved = conv_b[None, :] + sum((conv_w[shift_index][None, :] * padded[shift_index:shift_index + sequence_length] for shift_index in range(CONV)))
    activated = jax.nn.silu(convolved)
    states_in = activated[:, :inner_width].reshape(sequence_length, NH, HD)
    input_map = activated[:, inner_width:inner_width + NS]
    output_map = activated[:, inner_width + NS:]
    step_size = jax.nn.softplus(dt_raw + dt_shift[None, :])
    log_decay = -step_size * jnp.exp(log_rate)[None, :]
    blocks = sequence_length // LOCAL
    pieces = (states_in.reshape(blocks, LOCAL, NH, HD), input_map.reshape(blocks, LOCAL, NS), output_map.reshape(blocks, LOCAL, NS), step_size.reshape(blocks, LOCAL, NH), log_decay.reshape(blocks, LOCAL, NH))
    _, mixed_out = lax.scan(mixer_block, jnp.zeros((NH, HD, NS), jnp.float32), pieces)
    mixed_out = mixed_out.reshape(sequence_length, NH, HD) + skip_gain[None, :, None] * states_in
    gated = mixed_out.reshape(sequence_length, inner_width) * jax.nn.silu(gate_raw)
    mixer_val = reduced_precision(rms_scale(gated, norm_ssm))
    mamba_val = reduced_backward(matrix_product(mixer_val, w_out))
    query_groups = QUERY_HEADS // KEY_VALUE_HEADS
    query_head_count = reduced_precision(reduced_backward(matrix_product(normalized_input, query_weight))).reshape(sequence_length, KEY_VALUE_HEADS, query_groups, ATTN_HEAD_SIZE)
    key_head_count = reduced_precision(reduced_backward(matrix_product(normalized_input, key_weight))).reshape(sequence_length, KEY_VALUE_HEADS, ATTN_HEAD_SIZE)
    value_head_count = reduced_precision(reduced_backward(matrix_product(normalized_input, value_weight))).reshape(sequence_length, KEY_VALUE_HEADS, ATTN_HEAD_SIZE)
    scores = reduced_backward(jnp.einsum('qkgd,skd->kgqs', query_head_count, key_head_count, precision=lax.Precision.HIGHEST) * (1.0 / math.sqrt(ATTN_HEAD_SIZE)))
    visible = lax.broadcasted_iota(jnp.int32, (sequence_length, sequence_length), 1) <= lax.broadcasted_iota(jnp.int32, (sequence_length, sequence_length), 0)
    soft_out = reduced_precision(jax.nn.softmax(jnp.where(visible, scores, -1e+30), axis=-1))
    attended = jnp.einsum('kgqs,skd->qkgd', soft_out, value_head_count, precision=lax.Precision.HIGHEST).reshape(sequence_length, QUERY_HEADS * ATTN_HEAD_SIZE)
    attended = reduced_precision(reduced_backward(attended))
    attn_val = reduced_backward(matrix_product(attended, output_weight))
    hidden = hidden_in + mamba_val + attn_val
    normed_mid = reduced_precision(rms_scale(hidden, norm_mid))
    gate_val = reduced_backward(matrix_product(normed_mid, w_gate))
    up_val = reduced_backward(matrix_product(normed_mid, w_up))
    swish_out = reduced_precision(jax.nn.silu(gate_val) * up_val)
    return hidden + reduced_backward(matrix_product(swish_out, w_down))

def reference(inputs, cotangent, norm_in, w_in, conv_w, conv_b, dt_bias, a_log, skip_gain, norm_ssm, w_out, query_weight, key_weight, value_weight, output_weight, norm_mid, w_gate, w_up, w_down):
    params = tuple((array_in.astype(jnp.float32) for array_in in (norm_in, w_in, conv_w, conv_b, dt_bias, a_log, skip_gain, norm_ssm, w_out, query_weight, key_weight, value_weight, output_weight, norm_mid, w_gate, w_up, w_down)))
    sequence_count = MB * N_REP
    start_rows = inputs.astype(jnp.float32).reshape(sequence_count, SEQ, MODEL_WIDTH)
    target = cotangent.astype(jnp.float32).reshape(sequence_count, SEQ, MODEL_WIDTH)
    zero_gap = jnp.zeros_like(start_rows)

    def two_sections(params, start_rows, zero_gap):
        first_params = tuple((array_in[0] for array_in in params))
        second_params = tuple((array_in[1] for array_in in params))

        def per_sequence(carry_in, item_pair):
            sequence, gap_rows = item_pair
            middle = hybrid_layer(sequence, first_params)
            handed = reduced_backward(reduced_precision(middle)) + gap_rows
            return (carry_in, (middle, hybrid_layer(handed, second_params)))
        _, outputs = lax.scan(jax.checkpoint(per_sequence), jnp.zeros((), jnp.float32), (start_rows, zero_gap))
        return outputs
    outputs, pullback = jax.vjp(two_sections, params, start_rows, zero_gap)
    grads, grad_start, grad_gap = pullback((jnp.zeros_like(outputs[0]), target))
    section_out = jnp.stack([outputs[0], outputs[1]]).astype(jnp.bfloat16).reshape(2, MB, N_REP, SEQ, MODEL_WIDTH)
    input_grad = jnp.stack([grad_start, grad_gap]).reshape(2, MB, N_REP, SEQ, MODEL_WIDTH)
    return (section_out, input_grad, grads[0], grads[1], grads[2], grads[3], grads[4], grads[5], grads[6], grads[7], grads[8], grads[9], grads[10], grads[11], grads[12], grads[13], grads[14], grads[15], grads[16])
```

```python
import jax
import jax.numpy as jnp
from jax import lax
from jax.experimental import pallas as pl
from jax.experimental.pallas import tpu as pltpu
from jax.sharding import PartitionSpec as P

MODEL_WIDTH = 1024
NH = 24
HD = 64
NS = 128
QUERY_HEADS = 8
KEY_VALUE_HEADS = 2
ATTN_HEAD_SIZE = 64
FF = 2048
CONV = 4
MB = 2

EPSILON = 1e-05

SHARDS = 16
CORES = 2
CHIPS = SHARDS // CORES
INNER = NH * HD
NARROW = INNER // SHARDS
LANES = 128
HALF_HEAD = ATTN_HEAD_SIZE // 2
IN_COLS = 4 * LANES
WIDE_COLS = 2 * LANES
CONVED = 3 * LANES
CHUNK = 128
BLOCK = 64
FF_CORE = FF // SHARDS
RATIO = ATTN_HEAD_SIZE ** (-0.5)

BF = jnp.bfloat16
F32 = jnp.float32


def dot_plain(former, latter):
    return jnp.dot(former, latter, preferred_element_type=F32)


def dot_rows(former, latter):
    return lax.dot_general(former, latter, (((0,), (0,)), ((), ())), preferred_element_type=F32)


def dot_back(former, latter):
    return lax.dot_general(former, latter, (((1,), (1,)), ((), ())), preferred_element_type=F32)


def exact(former, latter, dims):
    return lax.dot_general(
        former,
        latter,
        ((dims[:1], dims[1:]), ((), ())),
        precision=lax.Precision.HIGHEST,
        preferred_element_type=F32,
    )


def swap_cores(x):
    return lax.ppermute(x, "shard", [(i, i ^ 1) for i in range(SHARDS)])


def swap_sections(x):
    return lax.ppermute(x, "section", [(0, 1), (1, 0)])


def same_core():
    return [list(range(core, SHARDS, CORES)) for core in range(CORES)]


def spread(rows):
    count, width = rows.shape
    copies = jnp.broadcast_to(rows[None], (CHIPS, count, width)).reshape(CHIPS * count, width)
    return lax.all_to_all(copies, "shard", 0, 0, axis_index_groups=same_core(), tiled=True)


def collect(partial):
    rows = partial.shape[0] // CHIPS
    met = lax.all_to_all(
        partial.astype(BF), "shard", 0, 0, axis_index_groups=same_core(), tiled=True
    )
    return jnp.sum(met.reshape(CHIPS, rows, partial.shape[1]).astype(F32), axis=0)


def two_parts(x):
    high = x.astype(BF)
    return high, (x - high.astype(F32)).astype(BF)


def by_place(core, own, other, axis):
    return jnp.where(
        core == 0,
        jnp.concatenate([own, other], axis=axis),
        jnp.concatenate([other, own], axis=axis),
    )


def normalize(x):
    scale = lax.rsqrt(jnp.mean(x * x, axis=-1, keepdims=True) + EPSILON)
    return x * scale, scale


def normalize_back(unit, scale, grad):
    return scale * (grad - unit * jnp.mean(grad * unit, axis=-1, keepdims=True))


def whole_vmem(count):
    return [pl.BlockSpec(memory_space=pltpu.VMEM)] * count


def scalar_first(count):
    return [pl.BlockSpec(memory_space=pltpu.SMEM)] + whole_vmem(count)


def params():
    return pltpu.CompilerParams(vmem_limit_bytes=48 * 2**20)


def softplus(v):
    return jnp.maximum(v, 0.0) + jnp.log1p(jnp.exp(-jnp.abs(v)))


def chunk_rows(core, own_ref, recv_ref, k):
    at = pl.ds(pl.multiple_of(k * BLOCK, BLOCK), BLOCK)
    own = jnp.concatenate([own_ref[at, 0:LANES], own_ref[at, 3 * LANES : 5 * LANES]], axis=1)
    own = own.astype(F32)
    recv = recv_ref[at, 0:CONVED].astype(F32)
    return jnp.where(core == 0, own, recv), jnp.where(core == 0, recv, own)


def chunk_parts(ext, conv_ref, cols_ref, sel_ref):
    conv = conv_ref[CONV : CONV + 1, :]
    for j in range(CONV):
        start = 8 - (CONV - 1) + j
        conv = conv + conv_ref[j : j + 1, :] * ext[start : start + CHUNK, :]
    sig = 1.0 / (1.0 + jnp.exp(-conv))
    activated = conv * sig
    states_in = activated[:, 0:LANES]
    input_map = activated[:, LANES : 2 * LANES]
    output_map = activated[:, 2 * LANES :]
    raw = dot_plain(ext[8 : 8 + CHUNK, 0:LANES].astype(BF), sel_ref[...]) + cols_ref[0:1, :]
    step = softplus(raw)
    log_decay = -step * cols_ref[1:2, :]
    rows = lax.broadcasted_iota(jnp.int32, (CHUNK, CHUNK), 0)
    cols = lax.broadcasted_iota(jnp.int32, (CHUNK, CHUNK), 1)
    causal = cols <= rows
    lower = jnp.where(causal, 1.0, 0.0)
    cumulative = exact(lower, log_decay, (1, 0))
    turned = exact(log_decay, lower, (0, 1))
    weighted = states_in * step
    coupling = dot_back(output_map.astype(BF), input_map.astype(BF))
    within = []
    for lane in (0, NARROW - 1):
        gap = cumulative[:, lane : lane + 1] - turned[lane : lane + 1, :]
        within.append(jnp.where(causal, jnp.exp(jnp.where(causal, gap, 0.0)), 0.0))
    last = cumulative[CHUNK - 1 : CHUNK, :]
    tail = jnp.exp(last - cumulative)
    decay = jnp.exp(turned[:, CHUNK - 1 : CHUNK])
    return (
        conv,
        sig,
        states_in,
        input_map.astype(BF),
        output_map.astype(BF),
        raw,
        step,
        log_decay,
        lower,
        cumulative,
        weighted,
        coupling,
        within,
        last,
        tail,
        decay,
    )


def mixer_kernel(
    core_ref, own_ref, recv_ref, conv_ref, cols_ref, sel_ref, mine_ref, theirs_ref, starts_ref, ext
):
    core = core_ref[0]
    ext[0:8, :] = jnp.zeros((8, CONVED), F32)

    def chunk(k, state):
        first, second = chunk_rows(core, own_ref, recv_ref, k)
        ext[8 : 8 + BLOCK, :] = first
        ext[8 + BLOCK : 8 + CHUNK, :] = second
        (
            conv,
            sig,
            states_in,
            input_map,
            output_map,
            raw,
            step,
            log_decay,
            lower,
            cumulative,
            weighted,
            coupling,
            within,
            last,
            tail,
            decay,
        ) = chunk_parts(ext, conv_ref, cols_ref, sel_ref)
        starts_ref[k] = state
        mixed = dot_back(output_map, state.astype(BF)) * jnp.exp(cumulative)
        mixed = mixed + cols_ref[2:3, :] * states_in
        for head in range(2):
            mixed = mixed + dot_plain(
                (within[head] * coupling).astype(BF),
                (weighted * cols_ref[3 + head : 4 + head, :]).astype(BF),
            )
        state = decay * state + dot_rows((weighted * tail).astype(BF), input_map)
        at = pl.ds(pl.multiple_of(k * BLOCK, BLOCK), BLOCK)
        low, high = mixed[:BLOCK, :], mixed[BLOCK:, :]
        mine_ref[at, :] = jnp.where(core == 0, low, high).astype(BF)
        theirs_ref[at, :] = jnp.where(core == 0, high, low).astype(BF)
        ext[0:8, :] = ext[CHUNK : CHUNK + 8, :]
        return state

    lax.fori_loop(0, CHIPS, chunk, jnp.zeros((LANES, NS), F32))


def mixer(core, own, recv, layer):
    rows = own.shape[0]
    return pl.pallas_call(
        mixer_kernel,
        out_shape=(
            jax.ShapeDtypeStruct((rows, LANES), BF),
            jax.ShapeDtypeStruct((rows, LANES), BF),
            jax.ShapeDtypeStruct((CHIPS, LANES, NS), F32),
        ),
        in_specs=scalar_first(5),
        out_specs=tuple(whole_vmem(3)),
        scratch_shapes=[pltpu.VMEM((CHUNK + 8, CONVED), F32)],
        compiler_params=params(),
        cost_estimate=pl.CostEstimate(
            flops=8 * 10**9, bytes_accessed=2 * 10**6, transcendentals=10**6
        ),
    )(core, own, recv, layer["conv"], layer["cols"], layer["sel"])


def mixer_back_kernel(
    core_ref,
    own_ref,
    recv_ref,
    conv_ref,
    cols_ref,
    sel_ref,
    starts_ref,
    grad_own_ref,
    grad_recv_ref,
    mine_ref,
    theirs_ref,
    conv_grad_ref,
    cols_grad_ref,
    ext,
    later,
):
    core = core_ref[0]
    later[...] = jnp.zeros((CHUNK + 8, CONVED), F32)
    conv_grad_ref[...] = jnp.zeros((8, CONVED), F32)
    cols_grad_ref[...] = jnp.zeros((8, LANES), F32)
    ones = jnp.ones((CHUNK, LANES), BF)
    lanes = lax.broadcasted_iota(jnp.int32, (CHUNK, LANES), 1)

    def chunk(turn, grad_state):
        k = CHIPS - 1 - turn
        first, second = chunk_rows(core, own_ref, recv_ref, k)
        ext[8 : 8 + BLOCK, :] = first
        ext[8 + BLOCK : 8 + CHUNK, :] = second
        before = jnp.maximum(k - 1, 0)
        at_end = pl.ds(pl.multiple_of(before * BLOCK + BLOCK - 16, 16), 16)
        own_end = jnp.concatenate(
            [own_ref[at_end, 0:LANES], own_ref[at_end, 3 * LANES : 5 * LANES]], axis=1
        ).astype(F32)
        recv_end = recv_ref[at_end, 0:CONVED].astype(F32)
        end = jnp.where(core == 0, recv_end, own_end)[8:16, :]
        ext[0:8, :] = jnp.where(k > 0, end, 0.0)
        (
            conv,
            sig,
            states_in,
            input_map,
            output_map,
            raw,
            step,
            log_decay,
            lower,
            cumulative,
            weighted,
            coupling,
            within,
            last,
            tail,
            decay,
        ) = chunk_parts(ext, conv_ref, cols_ref, sel_ref)
        start = starts_ref[k]
        start_low = start.astype(BF)
        at = pl.ds(pl.multiple_of(k * BLOCK, BLOCK), BLOCK)
        grad_mine = grad_own_ref[at, :].astype(F32)
        grad_theirs = grad_recv_ref[at, :].astype(F32)
        grad = jnp.concatenate(
            [
                jnp.where(core == 0, grad_mine, grad_theirs),
                jnp.where(core == 0, grad_theirs, grad_mine),
            ],
            axis=0,
        )
        grad_states = cols_ref[2:3, :] * grad
        grad_skip = jnp.sum(grad * states_in, axis=0, keepdims=True)
        grown = grad * jnp.exp(cumulative)
        grown_low = grown.astype(BF)
        grad_out_map = dot_plain(grown_low, start_low)
        grad_start = dot_rows(grown_low, output_map)
        grad_cum = grown * dot_back(output_map, start_low)
        grad_coupling = jnp.zeros((CHUNK, CHUNK), F32)
        grad_weighted = jnp.zeros((CHUNK, LANES), F32)
        for head in range(2):
            member = cols_ref[3 + head : 4 + head, :]
            grad_head = (grad * member).astype(BF)
            grad_mixing = dot_back(grad_head, weighted.astype(BF))
            mixing = within[head] * coupling
            grad_weighted = grad_weighted + dot_rows(mixing.astype(BF), grad_head)
            grad_coupling = grad_coupling + grad_mixing * within[head]
            pairs = (grad_mixing * mixing).astype(BF)
            change = dot_plain(pairs, ones) - dot_rows(pairs, ones)
            grad_cum = grad_cum + jnp.where(lanes == head * (NARROW - 1), change, 0.0)
        coupling_low = grad_coupling.astype(BF)
        grad_out_map = grad_out_map + dot_plain(coupling_low, input_map)
        grad_in_map = dot_rows(coupling_low, output_map)
        state_low = grad_state.astype(BF)
        tailed = weighted * tail
        grad_in_map = grad_in_map + dot_plain(tailed.astype(BF), state_low)
        reach = dot_back(input_map, state_low)
        grad_weighted = grad_weighted + reach * tail
        moved = reach * tailed
        grad_cum = grad_cum - moved
        kept = exact(jnp.ones((8, NS), F32), grad_state * start, (1, 1))[0:1, :]
        grad_last = jnp.sum(moved, axis=0, keepdims=True) + kept * jnp.exp(last)
        grad_log = exact(lower, grad_cum, (0, 0)) + grad_last
        grad_step = grad_weighted * states_in - cols_ref[1:2, :] * grad_log
        grad_states = grad_states + grad_weighted * step
        grad_raw = grad_step / (1.0 + jnp.exp(-raw))
        cols_grad_ref[0:1, :] += jnp.sum(grad_raw, axis=0, keepdims=True)
        cols_grad_ref[1:2, :] += jnp.sum(grad_log * log_decay, axis=0, keepdims=True)
        cols_grad_ref[2:3, :] += grad_skip
        grad_dt = exact(grad_raw, sel_ref[...].astype(F32), (1, 1))
        slope = sig * (1.0 + conv * (1.0 - sig))
        grad_conv = jnp.concatenate([grad_states, grad_in_map, grad_out_map], axis=1) * slope
        later[CHUNK : CHUNK + 8, :] = later[0:8, :]
        later[0:CHUNK, :] = grad_conv
        conv_grad_ref[CONV : CONV + 1, :] += jnp.sum(grad_conv, axis=0, keepdims=True)
        grad_in = jnp.zeros((CHUNK, CONVED), F32)
        for j in range(CONV):
            low = 8 - (CONV - 1) + j
            conv_grad_ref[j : j + 1, :] += jnp.sum(
                grad_conv * ext[low : low + CHUNK, :], axis=0, keepdims=True
            )
            ahead = CONV - 1 - j
            grad_in = grad_in + conv_ref[j : j + 1, :] * later[ahead : ahead + CHUNK, :]
        grad_in = jnp.concatenate([grad_in[:, 0:LANES] + grad_dt, grad_in[:, LANES:]], axis=1)
        low, high = grad_in[:BLOCK, :], grad_in[BLOCK:, :]
        mine_ref[at, :] = jnp.where(core == 0, low, high)
        theirs_ref[at, :] = jnp.where(core == 0, high, low).astype(BF)
        return decay * grad_state + grad_start

    lax.fori_loop(0, CHIPS, chunk, jnp.zeros((LANES, NS), F32))


def mixer_back(core, own, recv, layer, starts, grad_own, grad_recv):
    rows = own.shape[0]
    return pl.pallas_call(
        mixer_back_kernel,
        out_shape=(
            jax.ShapeDtypeStruct((rows, CONVED), F32),
            jax.ShapeDtypeStruct((rows, CONVED), BF),
            jax.ShapeDtypeStruct((8, CONVED), F32),
            jax.ShapeDtypeStruct((8, LANES), F32),
        ),
        in_specs=scalar_first(8),
        out_specs=tuple(whole_vmem(4)),
        scratch_shapes=[pltpu.VMEM((CHUNK + 8, CONVED), F32)] * 2,
        compiler_params=params(),
        cost_estimate=pl.CostEstimate(
            flops=16 * 10**9, bytes_accessed=4 * 10**6, transcendentals=10**6
        ),
    )(core, own, recv, layer["conv"], layer["cols"], layer["sel"], starts, grad_own, grad_recv)


def seen(core, part, rows, columns):
    row = lax.broadcasted_iota(jnp.int32, (rows, columns), 0) + part * rows
    col = lax.broadcasted_iota(jnp.int32, (rows, columns), 1)
    half = columns // 2
    query_at = (row // BLOCK * 2 + core) * BLOCK + row % BLOCK
    other = col // half
    key = col - other * half
    key_at = (key // BLOCK * 2 + jnp.where(other == 0, core, 1 - core)) * BLOCK + key % BLOCK
    return key_at <= query_at


def keys_values(own_ref, recv_ref):
    both = jnp.concatenate([own_ref[:, 5 * LANES :], recv_ref[:, CONVED:]], axis=0)
    return both[:, :ATTN_HEAD_SIZE], both[:, ATTN_HEAD_SIZE:]


def attend_kernel(core_ref, own_ref, recv_ref, out_ref, stat_ref):
    core = core_ref[0]
    keys, values = keys_values(own_ref, recv_ref)
    for part in range(own_ref.shape[0] // CHUNK):
        at = slice(part * CHUNK, (part + 1) * CHUNK)
        query = own_ref[at, LANES : LANES + ATTN_HEAD_SIZE]
        scores = dot_back(query, keys) * RATIO
        scores = jnp.where(seen(core, part, *scores.shape), scores, -1e30)
        top = jnp.max(scores, axis=1, keepdims=True)
        grown = jnp.exp(scores - top)
        total = jnp.sum(grown, axis=1, keepdims=True)
        soft = grown / total
        out_ref[at, :] = dot_plain(soft.astype(BF), values).astype(BF)
        stat_ref[at, :] = jnp.broadcast_to(top + jnp.log(total), (CHUNK, LANES))


def attend(core, own, recv):
    rows = own.shape[0]
    return pl.pallas_call(
        attend_kernel,
        out_shape=(
            jax.ShapeDtypeStruct((rows, ATTN_HEAD_SIZE), BF),
            jax.ShapeDtypeStruct((rows, LANES), F32),
        ),
        in_specs=scalar_first(2),
        out_specs=tuple(whole_vmem(2)),
        compiler_params=params(),
        cost_estimate=pl.CostEstimate(
            flops=3 * 10**9, bytes_accessed=2 * 10**6, transcendentals=10**6
        ),
    )(core, own, recv)


def attend_back_kernel(
    core_ref, own_ref, recv_ref, stat_ref, grad_ref, query_ref, mine_ref, theirs_ref, total
):
    core = core_ref[0]
    keys, values = keys_values(own_ref, recv_ref)
    total[...] = jnp.zeros(total.shape, F32)
    half = own_ref.shape[0]
    for part in range(half // CHUNK):
        at = slice(part * CHUNK, (part + 1) * CHUNK)
        query = own_ref[at, LANES : LANES + ATTN_HEAD_SIZE]
        grad = grad_ref[at, :]
        scores = dot_back(query, keys) * RATIO
        visible = seen(core, part, *scores.shape)
        soft = jnp.where(visible, jnp.exp(scores - stat_ref[at, 0:1]), 0.0)
        grad_soft = dot_back(grad, values)
        row_total = jnp.sum(soft * grad_soft, axis=1, keepdims=True)
        grad_scores = (soft * (grad_soft - row_total)).astype(BF)
        query_grad = dot_plain(grad_scores, keys) * RATIO
        query_ref[at, :] = jnp.concatenate([query_grad, jnp.zeros_like(query_grad)], axis=1)
        key_grad = dot_rows(grad_scores, query) * RATIO
        value_grad = dot_rows(soft.astype(BF), grad)
        total[...] += jnp.concatenate([key_grad, value_grad], axis=1)
    mine_ref[...] = total[:half, :]
    theirs_ref[...] = total[half:, :].astype(BF)


def attend_back(core, own, recv, stat, grad):
    rows = own.shape[0]
    return pl.pallas_call(
        attend_back_kernel,
        out_shape=(
            jax.ShapeDtypeStruct((rows, LANES), F32),
            jax.ShapeDtypeStruct((rows, LANES), F32),
            jax.ShapeDtypeStruct((rows, LANES), BF),
        ),
        in_specs=scalar_first(4),
        out_specs=tuple(whole_vmem(3)),
        scratch_shapes=[pltpu.VMEM((2 * rows, LANES), F32)],
        compiler_params=params(),
        cost_estimate=pl.CostEstimate(
            flops=6 * 10**9, bytes_accessed=2 * 10**6, transcendentals=10**6
        ),
    )(core, own, recv, stat, grad)


def forward_mixer(x, layer, core):
    unit, scale = normalize(x)
    own_unit = spread(unit.astype(BF))
    weights = layer["in"]
    own = dot_plain(own_unit, weights[:, 2 * LANES :]).astype(BF)
    recv = swap_cores(own[:, 2 * LANES :])
    gate_raw = dot_plain(own_unit, weights[:, : 2 * LANES])
    attended, stat = attend(core, own, recv)
    attention = collect(dot_plain(attended, layer["out"]))
    mine, theirs, starts = mixer(core, own, recv, layer)
    mixed = jnp.concatenate([mine, swap_cores(theirs)], axis=1).astype(F32)
    gated = mixed * jax.nn.silu(gate_raw)
    squares = jnp.sum(gated * gated, axis=-1, keepdims=True)
    gained = (gated * layer["gain"]).astype(BF)
    high, low = two_parts(squares)
    lanes = lax.broadcasted_iota(jnp.int32, (gated.shape[0], LANES), 1)
    marks = jnp.where(lanes == 0, high, jnp.where(lanes == 1, low, jnp.zeros((), BF)))
    partial = jnp.concatenate([dot_plain(gained, layer["mamba"]).astype(BF), marks], axis=1)
    total = collect(partial)
    mamba = total[:, :MODEL_WIDTH]
    square = total[:, MODEL_WIDTH : MODEL_WIDTH + 1] + total[:, MODEL_WIDTH + 1 : MODEL_WIDTH + 2]
    ssm_scale = lax.rsqrt(square / INNER + EPSILON)
    hidden = x + ssm_scale * mamba + attention
    kept = (
        unit,
        scale,
        own_unit,
        own,
        recv,
        gate_raw,
        attended,
        stat,
        starts,
        mixed,
        gated,
        gained,
        mamba,
        ssm_scale,
    )
    return hidden, kept


def forward_wide(hidden, layer):
    unit, scale = normalize(hidden)
    own_unit = spread(unit.astype(BF))
    both = dot_plain(own_unit, layer["wide"])
    gate_val = both[:, : 2 * FF_CORE]
    up_val = both[:, 2 * FF_CORE :]
    swish = (jax.nn.silu(gate_val) * up_val).astype(BF)
    return dot_plain(swish, layer["down"]), (unit, scale, own_unit, gate_val, up_val, swish)


def backward_wide(grad_out, grad_out_own, kept, layer):
    unit, scale, own_unit, gate_val, up_val, swish = kept
    grad_swish = dot_back(grad_out_own, layer["down"])
    sig = jax.nn.sigmoid(gate_val)
    grad_gate = grad_swish * up_val * (sig * (1.0 + gate_val * (1.0 - sig)))
    grad_up = grad_swish * (gate_val * sig)
    grad_both = jnp.concatenate([grad_gate, grad_up], axis=1).astype(BF)
    grad_unit = collect(dot_back(grad_both, layer["wide"]))
    grad_hidden = grad_out + normalize_back(unit, scale, grad_unit)
    return grad_hidden, dot_rows(own_unit, grad_both), dot_rows(swish, grad_out_own)


def backward_mixer(grad_hidden, kept, layer, core):
    (
        unit,
        scale,
        own_unit,
        own,
        recv,
        gate_raw,
        attended,
        stat,
        starts,
        mixed,
        gated,
        gained,
        mamba,
        ssm_scale,
    ) = kept
    grad_low = grad_hidden.astype(BF)
    inner = jnp.sum(grad_low.astype(F32) * mamba, axis=-1, keepdims=True)
    pull_back = ssm_scale * ssm_scale * ssm_scale * inner / INNER
    rows = grad_low.shape[0]
    sent = jnp.concatenate(
        [grad_low, *two_parts(ssm_scale), *two_parts(pull_back), jnp.zeros((rows, 124), BF)],
        axis=1,
    )
    met = spread(sent)
    grad_own = met[:, :MODEL_WIDTH]
    extra = met[:, MODEL_WIDTH : MODEL_WIDTH + 4].astype(F32)
    scale_own = extra[:, 0:1] + extra[:, 1:2]
    pull_own = extra[:, 2:3] + extra[:, 3:4]
    grad_mixer = dot_back(grad_own, layer["mamba"])
    grad_attended = dot_back(grad_own, layer["out"]).astype(BF)
    grad_gated = scale_own * layer["gain"] * grad_mixer - gated * pull_own
    sig = jax.nn.sigmoid(gate_raw)
    grad_mixed = (grad_gated * gate_raw * sig).astype(BF)
    grad_gate_raw = grad_gated * mixed * (sig * (1.0 + gate_raw * (1.0 - sig)))
    grad_recv = swap_cores(grad_mixed[:, LANES:])
    grad_query, key_mine, key_theirs = attend_back(core, own, recv, stat, grad_attended)
    mine, theirs, conv_grad, cols_grad = mixer_back(
        core, own, recv, layer, starts, grad_mixed[:, :LANES], grad_recv
    )
    other = swap_cores(jnp.concatenate([theirs, key_theirs], axis=1)).astype(F32)
    mixer_low = (gained.astype(F32) * scale_own).astype(BF)
    grad_mamba = dot_rows(mixer_low, grad_own)
    grad_out = dot_rows(attended, grad_own)
    grad_gain = jnp.sum(grad_mixer * gated * scale_own, axis=0)
    grad_project = jnp.concatenate(
        [
            grad_gate_raw,
            mine[:, :LANES],
            grad_query,
            other[:, :LANES],
            mine[:, LANES:] + other[:, LANES:CONVED],
            key_mine + other[:, CONVED:],
        ],
        axis=1,
    ).astype(BF)
    grad_unit = collect(dot_back(grad_project, layer["in"]))
    grad_x = grad_hidden + normalize_back(unit, scale, grad_unit)
    grad_in = dot_rows(own_unit, grad_project)
    return grad_x, grad_in, grad_mamba, grad_out, grad_gain, conv_grad, cols_grad


def cut_in(w_in, query_weight, key_weight, value_weight, first_spare, second_spare):
    rows = w_in.shape[0]

    def even(w):
        return w.reshape(rows, SHARDS, -1).transpose(1, 0, 2)

    def by_core(w):
        return jnp.tile(w.reshape(rows, CORES, -1).transpose(1, 0, 2), (CHIPS, 1, 1))

    def by_key_head(w):
        groups = CHIPS // KEY_VALUE_HEADS
        cut = w.reshape(rows, KEY_VALUE_HEADS, CORES, -1).transpose(1, 2, 0, 3)
        cut = jnp.broadcast_to(cut[:, None], (KEY_VALUE_HEADS, groups) + cut.shape[1:])
        return cut.reshape((SHARDS,) + cut.shape[3:])

    maps = 2 * INNER + 2 * NS
    steps = jnp.broadcast_to(w_in[None, :, maps:], (SHARDS, rows, NH))
    return jnp.concatenate(
        [
            even(w_in[:, :INNER]),
            first_spare,
            even(w_in[:, INNER : 2 * INNER]),
            steps,
            jnp.zeros((SHARDS, rows, LANES - NARROW - NH), BF),
            by_core(w_in[:, 2 * INNER : maps]),
            even(query_weight),
            by_key_head(key_weight),
            by_key_head(value_weight),
            second_spare,
        ],
        axis=2,
    )


def cut_wide(w_gate, w_up):
    rows = w_gate.shape[0]
    both = [w.reshape(rows, SHARDS, FF_CORE).transpose(1, 0, 2) for w in (w_gate, w_up)]
    return jnp.concatenate(both, axis=2)


def body(
    inputs,
    cotangent,
    norm_in,
    w_in,
    conv_w,
    conv_b,
    dt_bias,
    a_log,
    skip_gain,
    norm_ssm,
    w_out,
    query_weight,
    key_weight,
    value_weight,
    output_weight,
    norm_mid,
    w_gate,
    w_up,
    w_down,
):
    place = lax.axis_index("shard")
    core = place % CORES
    core_word = core.reshape(1).astype(jnp.int32)
    section = lax.axis_index("section")
    reps = lax.axis_size("rep")
    local = inputs.shape[2]
    spare = LANES - NARROW

    gain_in = norm_in[0].astype(F32)[:, None]
    gain_mid = norm_mid[0].astype(F32)[:, None]

    def scaled(w, gain):
        return (w[0].astype(F32) * gain).astype(BF)

    conv_all = jnp.concatenate([conv_w[0], conv_b], axis=0)
    conv_count = conv_all.size
    conv_cols = jnp.concatenate(
        [conv_all.reshape(-1), jnp.zeros((spare * local - conv_count,), BF)]
    ).reshape(1, local, spare)
    cut = cut_in(
        scaled(w_in, gain_in),
        scaled(query_weight, gain_in),
        scaled(key_weight, gain_in),
        scaled(value_weight, gain_in),
        jnp.broadcast_to(conv_cols, (SHARDS, local, spare)),
        jnp.zeros((SHARDS, local, LANES - 3 * HALF_HEAD), BF),
    )
    everywhere = ("section", "shard")
    met = lax.all_to_all(jnp.concatenate([cut, cut], axis=0), everywhere, 0, 0, tiled=True)
    met = met.reshape(2, SHARDS, local, IN_COLS)
    conv_met = met[:, :, :, NARROW:LANES].reshape(2, SHARDS, spare * local)[:, :, :conv_count]
    conv_met = conv_met.reshape(2, SHARDS, CONV + 1, -1).transpose(0, 2, 1, 3)
    conv_met = conv_met.reshape(2, CONV + 1, INNER + 2 * NS).astype(F32)
    own_cols = met.reshape(2, SHARDS * local, IN_COLS)
    other_cols = swap_cores(own_cols)
    cut = cut_wide(scaled(w_gate, gain_mid), scaled(w_up, gain_mid))
    wide_cols = lax.all_to_all(jnp.concatenate([cut, cut], axis=0), everywhere, 0, 0, tiled=True)
    wide_cols = wide_cols.reshape(2, SHARDS * local, WIDE_COLS)
    other_wide = swap_cores(wide_cols)

    def both_layers(own):
        other = swap_sections(own)
        return jnp.where(section == 0, jnp.stack([own, other]), jnp.stack([other, own]))

    row_weights = both_layers(jnp.concatenate([w_out[0], output_weight[0], w_down[0]], axis=0))
    other_rows = swap_cores(row_weights)
    out_row, down_row = NARROW, NARROW + HALF_HEAD
    per_head = jnp.concatenate([dt_bias[0], a_log[0], skip_gain[0], norm_ssm[0].astype(F32)])
    per_head = both_layers(per_head)
    own_gain = per_head[:, 3 * NH :]
    other_gain = swap_cores(own_gain)
    lane = lax.broadcasted_iota(jnp.int32, (NH, LANES), 1)
    head_of = jnp.where(lane < NARROW, (lane + place * NARROW) // HD, -1)
    member = (head_of == lax.broadcasted_iota(jnp.int32, (NH, LANES), 0)).astype(F32)
    sel = jnp.concatenate(
        [jnp.zeros((NARROW, LANES), F32), member, jnp.zeros((LANES - NARROW - NH, LANES), F32)]
    ).astype(BF)
    in_first = (head_of[0:1] == head_of[0:1, 0:1]).astype(F32)
    in_second = (head_of[0:1] == head_of[0:1, NARROW - 1 : NARROW]).astype(F32)

    def to_columns(values):
        return jnp.sum(values[:, None] * member, axis=0, keepdims=True)

    def padded(g):
        return jnp.concatenate([g, jnp.zeros((spare,), F32)])

    no_rows = jnp.zeros((spare, MODEL_WIDTH), BF)
    layers = []
    for layer in range(2):
        mine, theirs = own_cols[layer], other_cols[layer]
        block = [slice(k * LANES, (k + 1) * LANES) for k in range(4)]

        def paired(at):
            low = 3 * LANES + at * HALF_HEAD
            cols = slice(low, low + HALF_HEAD)
            return by_place(core, mine[:, cols], theirs[:, cols], 1)

        head_values = per_head[layer]
        cols = jnp.concatenate(
            [
                to_columns(head_values[:NH]),
                to_columns(jnp.exp(head_values[NH : 2 * NH])),
                to_columns(head_values[2 * NH : 3 * NH]),
                in_first,
                in_second,
                jnp.zeros((3, LANES), F32),
            ]
        )
        conv_own = jnp.concatenate(
            [
                lax.dynamic_slice_in_dim(conv_met[layer], place * NARROW, NARROW, axis=1),
                jnp.zeros((CONV + 1, spare), F32),
                conv_met[layer, :, INNER:],
            ],
            axis=1,
        )
        rows, others = row_weights[layer], other_rows[layer]
        layers.append(
            {
                "in": jnp.concatenate(
                    [
                        mine[:, block[0]],
                        theirs[:, block[0]],
                        mine[:, block[1]],
                        paired(0),
                        jnp.zeros((SHARDS * local, LANES - ATTN_HEAD_SIZE), BF),
                        theirs[:, block[1]],
                        by_place(core, mine[:, block[2]], theirs[:, block[2]], 1),
                        paired(1),
                        paired(2),
                    ],
                    axis=1,
                ),
                "wide": jnp.concatenate(
                    [
                        wide_cols[layer, :, :FF_CORE],
                        other_wide[layer, :, :FF_CORE],
                        wide_cols[layer, :, FF_CORE:],
                        other_wide[layer, :, FF_CORE:],
                    ],
                    axis=1,
                ),
                "mamba": jnp.concatenate([rows[:out_row], no_rows, others[:out_row], no_rows]),
                "out": by_place(core, rows[out_row:down_row], others[out_row:down_row], 0),
                "down": jnp.concatenate([rows[down_row:], others[down_row:]]),
                "conv": jnp.concatenate([conv_own, jnp.zeros((7 - CONV, CONVED), F32)]),
                "cols": cols,
                "sel": sel,
                "gain": jnp.concatenate([padded(own_gain[layer]), padded(other_gain[layer])])[None],
            }
        )

    own_input = lax.dynamic_index_in_dim(inputs[:, 0], section, 0, False).astype(F32)
    own_target = lax.dynamic_index_in_dim(cotangent[:, 0], section, 0, False)
    x = own_input
    outs = []
    kept_mixer, kept_wide = [], []
    for layer in range(2):
        hidden, kept = forward_mixer(x, layers[layer], core_word)
        kept_mixer.append(kept)
        partial, kept = forward_wide(hidden, layers[layer])
        kept_wide.append(kept)
        outs.append((hidden + collect(partial)).astype(BF))
        x = outs[layer].astype(F32)

    grad = own_target.astype(F32)
    grads = [None, None]
    input_grads = [None, None]
    for layer in (1, 0):
        grad_own = spread(grad.astype(BF))
        grad_hidden, grad_wide, grad_down = backward_wide(
            grad, grad_own, kept_wide[layer], layers[layer]
        )
        grad_x, *rest = backward_mixer(grad_hidden, kept_mixer[layer], layers[layer], core_word)
        input_grads[layer] = grad_x
        grad = grad_x.astype(BF).astype(F32)
        grads[layer] = (grad_wide, grad_down, *rest)

    def exchanged(first, second):
        own = jnp.where(section == 0, first, second)
        other = swap_sections(jnp.where(section == 0, second, first).astype(BF))
        other = other.astype(own.dtype)
        return jnp.where(section == 0, jnp.stack([own, other]), jnp.stack([other, own]))

    section_out = exchanged(*outs)[None, :, None]
    input_grad = exchanged(*input_grads)[None, :, None]

    row_grads = []
    for layer in range(2):
        _, grad_down, _, grad_mamba, grad_out, _, _, _ = grads[layer]
        out_first, out_second = grad_out[:HALF_HEAD], grad_out[HALF_HEAD:]
        mine = jnp.concatenate(
            [
                grad_mamba[:NARROW],
                jnp.where(core == 0, out_first, out_second),
                grad_down[:FF_CORE],
            ]
        )
        theirs = jnp.concatenate(
            [
                grad_mamba[LANES : LANES + NARROW],
                jnp.where(core == 0, out_second, out_first),
                grad_down[FF_CORE:],
            ]
        )
        row_grads.append((mine + swap_cores(theirs.astype(BF)).astype(F32)).astype(BF))
    met = lax.all_to_all(jnp.concatenate(row_grads), ("section", "rep"), 0, 0, tiled=True)
    row_total = jnp.sum(met.reshape(2 * reps, -1, MODEL_WIDTH).astype(F32), axis=0).astype(BF)
    copies = jnp.broadcast_to(row_total[None], (reps,) + row_total.shape)
    row_total = lax.all_to_all(copies, "rep", 0, 0, tiled=True)
    row_total = row_total.reshape(-1, MODEL_WIDTH).astype(F32)

    part = local // reps
    all_cols = IN_COLS + WIDE_COLS
    sent = []
    for layer in range(2):
        grad_wide, _, grad_in, _, _, grad_gain, conv_grad, cols_grad = grads[layer]
        blocks = [grad_in[:, k * LANES : (k + 1) * LANES].astype(BF) for k in range(8)]
        wide = [grad_wide[:, k * LANES : (k + 1) * LANES].astype(BF) for k in range(4)]
        heads = [
            jnp.concatenate(
                [
                    blocks[3][:, low : low + HALF_HEAD],
                    blocks[7][:, low : low + HALF_HEAD],
                    blocks[7][:, low + ATTN_HEAD_SIZE : low + ATTN_HEAD_SIZE + HALF_HEAD],
                    jnp.zeros((blocks[3].shape[0], LANES - 3 * HALF_HEAD), BF),
                ],
                axis=1,
            )
            for low in (0, HALF_HEAD)
        ]
        mine = jnp.concatenate(
            [
                blocks[0],
                blocks[2],
                jnp.where(core == 0, blocks[5], blocks[6]),
                jnp.where(core == 0, heads[0], heads[1]),
                wide[0],
                wide[2],
            ],
            axis=1,
        )
        theirs = jnp.concatenate(
            [
                blocks[1],
                blocks[4],
                jnp.where(core == 0, blocks[6], blocks[5]),
                jnp.where(core == 0, heads[1], heads[0]),
                wide[1],
                wide[3],
            ],
            axis=1,
        )
        mine = (mine.astype(F32) + swap_cores(theirs).astype(F32)).astype(BF)
        mine = mine.reshape(SHARDS, reps, part, all_cols).transpose(1, 0, 2, 3)
        conv_grad = conv_grad[: CONV + 1]
        conv_grad = jnp.concatenate(
            [
                lax.dynamic_update_slice_in_dim(
                    jnp.zeros((CONV + 1, INNER), F32), conv_grad[:, :NARROW], place * NARROW, axis=1
                ),
                conv_grad[:, LANES:],
            ],
            axis=1,
        )
        conv_grad = conv_grad.reshape(CONV + 1, SHARDS, -1).transpose(1, 0, 2).reshape(SHARDS, -1)
        gain_halves = by_place(core, grad_gain[:NARROW], grad_gain[LANES : LANES + NARROW], 0)
        gain_grad = lax.dynamic_update_slice_in_dim(
            jnp.zeros((INNER,), F32), gain_halves, (place // CORES) * CORES * NARROW, axis=0
        ).reshape(SHARDS, -1)
        head_grad = jnp.sum(cols_grad[:3, None, :] * member[None], axis=2).reshape(-1)
        head_high, head_low = two_parts(head_grad)
        extra = jnp.concatenate(
            [
                conv_grad.astype(BF),
                gain_grad.astype(BF),
                jnp.broadcast_to(head_high[None], (SHARDS, 3 * NH)),
                jnp.broadcast_to(head_low[None], (SHARDS, 3 * NH)),
            ],
            axis=1,
        )
        room = part * spare
        extra_count = extra.shape[1]
        extra = jnp.concatenate([extra, jnp.zeros((SHARDS, 2 * room - extra_count), BF)], axis=1)
        extra = extra.reshape(1, SHARDS, 2, part, spare)
        extra = jnp.broadcast_to(extra, (reps,) + extra.shape[1:])
        sent.append(
            jnp.concatenate(
                [
                    mine[..., :NARROW],
                    extra[:, :, 0],
                    mine[..., LANES : 3 * LANES + 3 * HALF_HEAD],
                    extra[:, :, 1],
                    mine[..., IN_COLS:],
                ],
                axis=3,
            )
        )
    sent = jnp.stack(sent).reshape(2 * reps * SHARDS, part, all_cols)
    met = lax.all_to_all(sent, ("section", "rep", "shard"), 0, 0, tiled=True)
    total = jnp.sum(met.reshape(2 * reps, SHARDS, part, all_cols).astype(F32), axis=0)
    tail_at = 3 * LANES + 3 * HALF_HEAD
    extra = jnp.concatenate(
        [
            jnp.sum(total[:, :, NARROW:LANES], axis=0).reshape(room),
            jnp.sum(total[:, :, tail_at:IN_COLS], axis=0).reshape(room),
        ]
    )
    conv_total = extra[:conv_count].reshape(CONV + 1, -1)
    gain_total = extra[conv_count : conv_count + NARROW]
    head_total = extra[conv_count + NARROW : extra_count]
    head_total = (head_total[: 3 * NH] + head_total[3 * NH :]).reshape(3, NH)

    def even(g):
        return g.transpose(1, 0, 2).reshape(part, -1)

    def by_key_head(g):
        groups = CHIPS // KEY_VALUE_HEADS
        g = jnp.sum(g.reshape(KEY_VALUE_HEADS, groups, CORES, part, -1), axis=1)
        return even(g.reshape(KEY_VALUE_HEADS * CORES, part, -1))

    maps = total[:, :, 2 * LANES : 3 * LANES].reshape(CHIPS, CORES, part, LANES)
    heads = [
        total[:, :, 3 * LANES + k * HALF_HEAD : 3 * LANES + (k + 1) * HALF_HEAD] for k in range(3)
    ]
    column_grads = jnp.concatenate(
        [
            even(total[:, :, :NARROW]),
            even(total[:, :, LANES : LANES + NARROW]),
            even(jnp.sum(maps, axis=0)),
            jnp.sum(total[:, :, LANES + NARROW : LANES + NARROW + NH], axis=0),
            even(heads[0]),
            by_key_head(heads[1]),
            by_key_head(heads[2]),
            even(total[:, :, IN_COLS : IN_COLS + FF_CORE]),
            even(total[:, :, IN_COLS + FF_CORE :]),
        ],
        axis=1,
    ).astype(BF)
    copies = jnp.broadcast_to(column_grads[None], (reps,) + column_grads.shape)
    column_grads = lax.all_to_all(copies, "rep", 0, 0, tiled=True)
    column_grads = column_grads.reshape(local, -1).astype(F32)
    raw = (w_in, query_weight, key_weight, value_weight, w_gate, w_up)
    plain, at = [], 0
    for w in raw:
        plain.append(column_grads[:, at : at + w.shape[2]])
        at += w.shape[2]
    dots = [jnp.sum(g * w[0].astype(F32), axis=1) for g, w in zip(plain, raw)]
    grad_norm_in = dots[0] + dots[1] + dots[2] + dots[3]
    grad_norm_mid = dots[4] + dots[5]
    by_rows = [g * gain for g, gain in zip(plain, (gain_in,) * 4 + (gain_mid,) * 2)]
    return (
        section_out,
        input_grad,
        grad_norm_in[None],
        by_rows[0][None],
        conv_total[:CONV][None],
        conv_total[CONV][None],
        head_total[0][None],
        head_total[1][None],
        head_total[2][None],
        gain_total[None],
        row_total[:out_row][None],
        by_rows[1][None],
        by_rows[2][None],
        by_rows[3][None],
        row_total[out_row:down_row][None],
        grad_norm_mid[None],
        by_rows[4][None],
        by_rows[5][None],
        row_total[down_row:][None],
    )


def solution(mesh):
    return jax.shard_map(
        body,
        mesh=mesh,
        in_specs=(
            P(None, "rep", "shard", None),
            P(None, "rep", "shard", None),
            P("section", "shard"),
            P("section", "shard", None),
            P("section", None, "shard"),
            P("section", "shard"),
            P("section", None),
            P("section", None),
            P("section", None),
            P("section", "shard"),
            P("section", "shard", None),
            P("section", "shard", None),
            P("section", "shard", None),
            P("section", "shard", None),
            P("section", "shard", None),
            P("section", "shard"),
            P("section", "shard", None),
            P("section", "shard", None),
            P("section", "shard", None),
        ),
        out_specs=(
            P("section", None, "rep", "shard", None),
            P("section", None, "rep", "shard", None),
            P("section", "shard"),
            P("section", "shard", None),
            P("section", None, "shard"),
            P("section", "shard"),
            P("section", None),
            P("section", None),
            P("section", None),
            P("section", "shard"),
            P("section", "shard", None),
            P("section", "shard", None),
            P("section", "shard", None),
            P("section", "shard", None),
            P("section", "shard", None),
            P("section", "shard"),
            P("section", "shard", None),
            P("section", "shard", None),
            P("section", "shard", None),
        ),
        check_vma=False,
    )
```

```python
import functools

import jax
import jax.numpy as jnp
from jax import lax
from jax.experimental import pallas as pl
from jax.experimental.pallas import tpu as pltpu
from jax.sharding import PartitionSpec as P

MODEL_WIDTH = 1024
NH = 24
HD = 64
NS = 128
QUERY_HEADS = 8
KEY_VALUE_HEADS = 2
ATTN_HEAD_SIZE = 64
FF = 2048
CONV = 4
MB = 2

EPSILON = 1e-05

SHARDS = 16
CORES = 2
CHIPS = SHARDS // CORES
INNER = NH * HD
NARROW = INNER // SHARDS
LANES = 128
HALF_HEAD = ATTN_HEAD_SIZE // 2
IN_COLS = 4 * LANES
WIDE_COLS = 2 * LANES
CONVED = 3 * LANES
CHUNK = 128
BLOCK = 64
FF_CORE = FF // SHARDS
RATIO = ATTN_HEAD_SIZE ** (-0.5)

BF = jnp.bfloat16
F32 = jnp.float32


def dot_plain(former, latter):
    return jnp.dot(former, latter, preferred_element_type=F32)


def dot_rows(former, latter):
    return lax.dot_general(former, latter, (((0,), (0,)), ((), ())), preferred_element_type=F32)


def dot_back(former, latter):
    return lax.dot_general(former, latter, (((1,), (1,)), ((), ())), preferred_element_type=F32)


def exact(former, latter, dims):
    return lax.dot_general(
        former,
        latter,
        ((dims[:1], dims[1:]), ((), ())),
        precision=lax.Precision.HIGHEST,
        preferred_element_type=F32,
    )


def swap_cores(x):
    return lax.ppermute(x, "shard", [(i, i ^ 1) for i in range(SHARDS)])


def swap_sections(x):
    return lax.ppermute(x, "section", [(0, 1), (1, 0)])


def same_core():
    return [list(range(core, SHARDS, CORES)) for core in range(CORES)]


def joined(x, *met):
    zero = sum((m[(0,) * m.ndim] * 0).astype(F32) for m in met)
    return x + zero.astype(x.dtype)


def spread(rows):
    count, width = rows.shape
    copies = jnp.broadcast_to(rows[None], (CHIPS, count, width)).reshape(CHIPS * count, width)
    return lax.all_to_all(copies, "shard", 0, 0, axis_index_groups=same_core(), tiled=True)


def collect(partial, *beside):
    rows = partial.shape[0] // CHIPS
    met = lax.all_to_all(
        partial.astype(BF), "shard", 0, 0, axis_index_groups=same_core(), tiled=True
    )
    total = jnp.sum(met.reshape(CHIPS, rows, partial.shape[1]).astype(F32), axis=0)
    return joined(total, *beside) if beside else total


def chip_sums(x, *beside):
    ones = jnp.ones((8, x.shape[1]), F32)
    sums = exact(ones, x, (1, 1))
    copies = jnp.broadcast_to(sums[None], (CHIPS,) + sums.shape).reshape(8 * CHIPS, -1)
    met = lax.all_to_all(copies, "shard", 0, 0, axis_index_groups=same_core(), tiled=True)
    share = joined(jnp.full((8 * CHIPS, LANES), 0.125, F32), *beside)
    return exact(met, share, (0, 0))[:, :1]


def by_place(core, own, other, axis):
    return jnp.where(
        core == 0,
        jnp.concatenate([own, other], axis=axis),
        jnp.concatenate([other, own], axis=axis),
    )


def normalize(x):
    scale = lax.rsqrt(jnp.mean(x * x, axis=-1, keepdims=True) + EPSILON)
    return x * scale, scale


def normalize_back(unit, scale, grad):
    return scale * (grad - unit * jnp.mean(grad * unit, axis=-1, keepdims=True))


def whole_vmem(count):
    return [pl.BlockSpec(memory_space=pltpu.VMEM)] * count


def scalar_first(count):
    return [pl.BlockSpec(memory_space=pltpu.SMEM)] + whole_vmem(count)


def params():
    return pltpu.CompilerParams(vmem_limit_bytes=48 * 2**20)


def small_cost():
    return pl.CostEstimate(flops=10**6, bytes_accessed=10**4, transcendentals=0)


def softplus(v):
    return jnp.maximum(v, 0.0) + jnp.log1p(jnp.exp(-jnp.abs(v)))


def row_parts(refs, at):
    states, first, second = refs
    parts = [ref[at, low : low + LANES] for ref, low in (states, first, second)]
    return jnp.concatenate(parts, axis=1).astype(F32)


def sources(near_ref, maps_ref, far_ref, recv_maps_ref, recv_far_ref):
    own = ((near_ref, LANES), (maps_ref, 0), (far_ref, 2 * LANES))
    recv = ((recv_far_ref, LANES), (recv_far_ref, 2 * LANES), (recv_maps_ref, 0))
    return own, recv


def chunk_rows(core, own_refs, recv_refs, k):
    at = pl.ds(pl.multiple_of(k * BLOCK, BLOCK), BLOCK)
    own = row_parts(own_refs, at)
    recv = row_parts(recv_refs, at)
    return jnp.where(core == 0, own, recv), jnp.where(core == 0, recv, own)


def chunk_parts(core, ext, conv_ref, cols_ref, sel_ref):
    conv = conv_ref[CONV : CONV + 1, :]
    for j in range(CONV):
        start = 8 - (CONV - 1) + j
        conv = conv + conv_ref[j : j + 1, :] * ext[start : start + CHUNK, :]
    sig = 1.0 / (1.0 + jnp.exp(-conv))
    activated = conv * sig
    states_in = activated[:, 0:LANES]
    first, second = activated[:, LANES : 2 * LANES], activated[:, 2 * LANES :]
    input_map = jnp.where(core == 0, first, second)
    output_map = jnp.where(core == 0, second, first)
    raw = dot_plain(ext[8 : 8 + CHUNK, 0:LANES].astype(BF), sel_ref[...]) + cols_ref[0:1, :]
    step = softplus(raw)
    log_decay = -step * cols_ref[1:2, :]
    rows = lax.broadcasted_iota(jnp.int32, (CHUNK, CHUNK), 0)
    cols = lax.broadcasted_iota(jnp.int32, (CHUNK, CHUNK), 1)
    causal = cols <= rows
    lower = jnp.where(causal, 1.0, 0.0)
    cumulative = exact(lower, log_decay, (1, 0))
    turned = exact(log_decay, lower, (0, 1))
    weighted = states_in * step
    coupling = dot_back(output_map.astype(BF), input_map.astype(BF))
    within = []
    for lane in (0, NARROW - 1):
        gap = cumulative[:, lane : lane + 1] - turned[lane : lane + 1, :]
        within.append(jnp.where(causal, jnp.exp(jnp.where(causal, gap, 0.0)), 0.0))
    last = cumulative[CHUNK - 1 : CHUNK, :]
    tail = jnp.exp(last - cumulative)
    decay = jnp.exp(turned[:, CHUNK - 1 : CHUNK])
    return (
        conv,
        sig,
        states_in,
        input_map.astype(BF),
        output_map.astype(BF),
        raw,
        step,
        log_decay,
        lower,
        cumulative,
        weighted,
        coupling,
        within,
        last,
        tail,
        decay,
    )


def mixer_kernel(
    core_ref,
    near_ref,
    maps_ref,
    far_ref,
    recv_maps_ref,
    recv_far_ref,
    conv_ref,
    cols_ref,
    sel_ref,
    mine_ref,
    theirs_ref,
    starts_ref,
    ext,
):
    core = core_ref[0]
    own_refs, recv_refs = sources(near_ref, maps_ref, far_ref, recv_maps_ref, recv_far_ref)
    ext[0:8, :] = jnp.zeros((8, CONVED), F32)

    def chunk(k, state):
        first, second = chunk_rows(core, own_refs, recv_refs, k)
        ext[8 : 8 + BLOCK, :] = first
        ext[8 + BLOCK : 8 + CHUNK, :] = second
        (
            conv,
            sig,
            states_in,
            input_map,
            output_map,
            raw,
            step,
            log_decay,
            lower,
            cumulative,
            weighted,
            coupling,
            within,
            last,
            tail,
            decay,
        ) = chunk_parts(core, ext, conv_ref, cols_ref, sel_ref)
        starts_ref[k] = state
        mixed = dot_back(output_map, state.astype(BF)) * jnp.exp(cumulative)
        mixed = mixed + cols_ref[2:3, :] * states_in
        for head in range(2):
            mixed = mixed + dot_plain(
                (within[head] * coupling).astype(BF),
                (weighted * cols_ref[3 + head : 4 + head, :]).astype(BF),
            )
        state = decay * state + dot_rows((weighted * tail).astype(BF), input_map)
        at = pl.ds(pl.multiple_of(k * BLOCK, BLOCK), BLOCK)
        low, high = mixed[:BLOCK, :], mixed[BLOCK:, :]
        mine_ref[at, :] = jnp.where(core == 0, low, high).astype(BF)
        theirs_ref[at, :] = jnp.where(core == 0, high, low).astype(BF)
        ext[0:8, :] = ext[CHUNK : CHUNK + 8, :]
        return state

    lax.fori_loop(0, CHIPS, chunk, jnp.zeros((LANES, NS), F32), unroll=4)


def anywhere(count):
    return [pl.BlockSpec(memory_space=pl.ANY)] * count


def mixer(core, own, layer):
    rows = own[0].shape[0]
    return pl.pallas_call(
        mixer_kernel,
        out_shape=(
            jax.ShapeDtypeStruct((rows, LANES), BF),
            jax.ShapeDtypeStruct((rows, LANES), BF),
            jax.ShapeDtypeStruct((CHIPS, LANES, NS), F32),
        ),
        in_specs=scalar_first(8),
        out_specs=tuple(whole_vmem(3)),
        scratch_shapes=[pltpu.VMEM((CHUNK + 8, CONVED), F32)],
        compiler_params=params(),
        cost_estimate=small_cost(),
    )(core, *own, layer["conv"], layer["cols"], layer["sel"])


def mixer_back_kernel(
    core_ref,
    near_ref,
    maps_ref,
    far_ref,
    recv_maps_ref,
    recv_far_ref,
    conv_ref,
    cols_ref,
    sel_ref,
    starts_ref,
    grad_own_ref,
    grad_recv_ref,
    *refs,
):
    mine_ref, theirs_ref, conv_grad_ref, cols_grad_ref, ext, later = refs[-6:]
    core = core_ref[0]
    own_refs, recv_refs = sources(near_ref, maps_ref, far_ref, recv_maps_ref, recv_far_ref)
    later[...] = jnp.zeros((CHUNK + 8, CONVED), F32)
    conv_grad_ref[...] = jnp.zeros((8, CONVED), F32)
    cols_grad_ref[...] = jnp.zeros((8, LANES), F32)
    ones = jnp.ones((CHUNK, LANES), BF)
    lanes = lax.broadcasted_iota(jnp.int32, (CHUNK, LANES), 1)

    def chunk(turn, grad_state):
        k = CHIPS - 1 - turn
        first, second = chunk_rows(core, own_refs, recv_refs, k)
        ext[8 : 8 + BLOCK, :] = first
        ext[8 + BLOCK : 8 + CHUNK, :] = second
        before = jnp.maximum(k - 1, 0)
        at_end = pl.ds(pl.multiple_of(before * BLOCK + BLOCK - 16, 16), 16)
        own_end = row_parts(own_refs, at_end)
        recv_end = row_parts(recv_refs, at_end)
        end = jnp.where(core == 0, recv_end, own_end)[8:16, :]
        ext[0:8, :] = jnp.where(k > 0, end, 0.0)
        (
            conv,
            sig,
            states_in,
            input_map,
            output_map,
            raw,
            step,
            log_decay,
            lower,
            cumulative,
            weighted,
            coupling,
            within,
            last,
            tail,
            decay,
        ) = chunk_parts(core, ext, conv_ref, cols_ref, sel_ref)
        start = starts_ref[k]
        start_low = start.astype(BF)
        at = pl.ds(pl.multiple_of(k * BLOCK, BLOCK), BLOCK)
        grad_mine = grad_own_ref[at, :].astype(F32)
        grad_theirs = grad_recv_ref[at, :].astype(F32)
        grad = jnp.concatenate(
            [
                jnp.where(core == 0, grad_mine, grad_theirs),
                jnp.where(core == 0, grad_theirs, grad_mine),
            ],
            axis=0,
        )
        grad_states = cols_ref[2:3, :] * grad
        grad_skip = jnp.sum(grad * states_in, axis=0, keepdims=True)
        grown = grad * jnp.exp(cumulative)
        grown_low = grown.astype(BF)
        grad_out_map = dot_plain(grown_low, start_low)
        grad_start = dot_rows(grown_low, output_map)
        grad_cum = grown * dot_back(output_map, start_low)
        grad_coupling = jnp.zeros((CHUNK, CHUNK), F32)
        grad_weighted = jnp.zeros((CHUNK, LANES), F32)
        for head in range(2):
            member = cols_ref[3 + head : 4 + head, :]
            grad_head = (grad * member).astype(BF)
            grad_mixing = dot_back(grad_head, weighted.astype(BF))
            mixing = within[head] * coupling
            grad_weighted = grad_weighted + dot_rows(mixing.astype(BF), grad_head)
            grad_coupling = grad_coupling + grad_mixing * within[head]
            pairs = (grad_mixing * mixing).astype(BF)
            change = dot_plain(pairs, ones) - dot_rows(pairs, ones)
            grad_cum = grad_cum + jnp.where(lanes == head * (NARROW - 1), change, 0.0)
        coupling_low = grad_coupling.astype(BF)
        grad_out_map = grad_out_map + dot_plain(coupling_low, input_map)
        grad_in_map = dot_rows(coupling_low, output_map)
        state_low = grad_state.astype(BF)
        tailed = weighted * tail
        grad_in_map = grad_in_map + dot_plain(tailed.astype(BF), state_low)
        reach = dot_back(input_map, state_low)
        grad_weighted = grad_weighted + reach * tail
        moved = reach * tailed
        grad_cum = grad_cum - moved
        kept = exact(jnp.ones((8, NS), F32), grad_state * start, (1, 1))[0:1, :]
        grad_last = jnp.sum(moved, axis=0, keepdims=True) + kept * jnp.exp(last)
        grad_log = exact(lower, grad_cum, (0, 0)) + grad_last
        grad_step = grad_weighted * states_in - cols_ref[1:2, :] * grad_log
        grad_states = grad_states + grad_weighted * step
        grad_raw = grad_step / (1.0 + jnp.exp(-raw))
        cols_grad_ref[0:1, :] += jnp.sum(grad_raw, axis=0, keepdims=True)
        cols_grad_ref[1:2, :] += jnp.sum(grad_log * log_decay, axis=0, keepdims=True)
        cols_grad_ref[2:3, :] += grad_skip
        grad_dt = exact(grad_raw, sel_ref[...].astype(F32), (1, 1))
        slope = sig * (1.0 + conv * (1.0 - sig))
        grad_first = jnp.where(core == 0, grad_in_map, grad_out_map)
        grad_second = jnp.where(core == 0, grad_out_map, grad_in_map)
        grad_conv = jnp.concatenate([grad_states, grad_first, grad_second], axis=1) * slope
        later[CHUNK : CHUNK + 8, :] = later[0:8, :]
        later[0:CHUNK, :] = grad_conv
        conv_grad_ref[CONV : CONV + 1, :] += jnp.sum(grad_conv, axis=0, keepdims=True)
        grad_in = jnp.zeros((CHUNK, CONVED), F32)
        for j in range(CONV):
            low = 8 - (CONV - 1) + j
            conv_grad_ref[j : j + 1, :] += jnp.sum(
                grad_conv * ext[low : low + CHUNK, :], axis=0, keepdims=True
            )
            ahead = CONV - 1 - j
            grad_in = grad_in + conv_ref[j : j + 1, :] * later[ahead : ahead + CHUNK, :]
        grad_in = jnp.concatenate([grad_in[:, 0:LANES] + grad_dt, grad_in[:, LANES:]], axis=1)
        low, high = grad_in[:BLOCK, :], grad_in[BLOCK:, :]
        mine_ref[at, :] = jnp.where(core == 0, low, high)
        theirs_ref[at, :] = jnp.where(core == 0, high, low).astype(BF)
        return decay * grad_state + grad_start

    lax.fori_loop(0, CHIPS, chunk, jnp.zeros((LANES, NS), F32), unroll=4)


def mixer_back(core, own, layer, starts, grad_own, grad_recv):
    rows = own[0].shape[0]
    return pl.pallas_call(
        mixer_back_kernel,
        out_shape=(
            jax.ShapeDtypeStruct((rows, CONVED), F32),
            jax.ShapeDtypeStruct((rows, CONVED), BF),
            jax.ShapeDtypeStruct((8, CONVED), F32),
            jax.ShapeDtypeStruct((8, LANES), F32),
        ),
        in_specs=scalar_first(11),
        out_specs=tuple(whole_vmem(4)),
        scratch_shapes=[pltpu.VMEM((CHUNK + 8, CONVED), F32)] * 2,
        compiler_params=params(),
        cost_estimate=small_cost(),
    )(core, *own, layer["conv"], layer["cols"], layer["sel"], starts, grad_own, grad_recv)


def seen(core, part, rows, columns):
    row = lax.broadcasted_iota(jnp.int32, (rows, columns), 0) + part * rows
    col = lax.broadcasted_iota(jnp.int32, (rows, columns), 1)
    half = columns // 2
    query_at = (row // BLOCK * 2 + core) * BLOCK + row % BLOCK
    other = col // half
    key = col - other * half
    key_at = (key // BLOCK * 2 + jnp.where(other == 0, core, 1 - core)) * BLOCK + key % BLOCK
    return key_at <= query_at


def head_part(near, far, part):
    at = slice(part * HALF_HEAD, (part + 1) * HALF_HEAD)
    return jnp.concatenate([near[:, at], far[:, at]], axis=1)


def heads_of(maps_ref, far_ref, recv_maps_ref, recv_far_ref):
    near, far = maps_ref[:, LANES:], far_ref[:, 3 * LANES :]
    recv_near, recv_far = recv_far_ref[:, 3 * LANES :], recv_maps_ref[:, LANES:]
    keys, values = (
        jnp.concatenate([head_part(near, far, k), head_part(recv_near, recv_far, k)], axis=0)
        for k in (1, 2)
    )
    return head_part(near, far, 0), keys, values


def attend_kernel(
    core_ref, maps_ref, far_ref, recv_maps_ref, recv_far_ref, also_ref, out_ref, stat_ref
):
    core = core_ref[0]
    queries, keys, values = heads_of(maps_ref, far_ref, recv_maps_ref, recv_far_ref)
    for part in range(maps_ref.shape[0] // CHUNK):
        at = slice(part * CHUNK, (part + 1) * CHUNK)
        scores = dot_back(queries[at], keys) * RATIO
        scores = jnp.where(seen(core, part, *scores.shape), scores, -1e30)
        top = jnp.max(scores, axis=1, keepdims=True)
        grown = jnp.exp(scores - top)
        total = jnp.sum(grown, axis=1, keepdims=True)
        soft = grown / total
        out_ref[at, :] = dot_plain(soft.astype(BF), values).astype(BF)
        stat_ref[at, :] = jnp.broadcast_to(top + jnp.log(total), (CHUNK, LANES))


def attend(core, own, also):
    rows = own[0].shape[0]
    return pl.pallas_call(
        attend_kernel,
        out_shape=(
            jax.ShapeDtypeStruct((rows, ATTN_HEAD_SIZE), BF),
            jax.ShapeDtypeStruct((rows, LANES), F32),
        ),
        in_specs=scalar_first(4) + anywhere(1),
        out_specs=tuple(whole_vmem(2)),
        compiler_params=params(),
        cost_estimate=small_cost(),
    )(core, *own[1:], also)


def attend_back_kernel(
    core_ref,
    maps_ref,
    far_ref,
    recv_maps_ref,
    recv_far_ref,
    stat_ref,
    grad_ref,
    *refs,
):
    near_grad_ref, far_grad_ref, theirs_ref, total, query_total = refs[-5:]
    core = core_ref[0]
    queries, keys, values = heads_of(maps_ref, far_ref, recv_maps_ref, recv_far_ref)
    total[...] = jnp.zeros(total.shape, F32)
    half = maps_ref.shape[0]
    for part in range(half // CHUNK):
        at = slice(part * CHUNK, (part + 1) * CHUNK)
        query = queries[at]
        grad = grad_ref[at, :]
        scores = dot_back(query, keys) * RATIO
        visible = seen(core, part, *scores.shape)
        soft = jnp.where(visible, jnp.exp(scores - stat_ref[at, 0:1]), 0.0)
        grad_soft = dot_back(grad, values)
        row_total = jnp.sum(soft * grad_soft, axis=1, keepdims=True)
        grad_scores = (soft * (grad_soft - row_total)).astype(BF)
        query_total[at, :] = dot_plain(grad_scores, keys) * RATIO
        key_grad = dot_rows(grad_scores, query) * RATIO
        value_grad = dot_rows(soft.astype(BF), grad)
        total[...] += jnp.concatenate([key_grad, value_grad], axis=1)
    empty = jnp.zeros((half, HALF_HEAD), F32)
    mine, theirs = total[:half, :], total[half:, :]

    def cut(x, at):
        return x[:, at * HALF_HEAD : (at + 1) * HALF_HEAD]

    query = query_total[...]
    near_grad_ref[...] = jnp.concatenate([cut(query, 0), cut(mine, 0), cut(mine, 2), empty], axis=1)
    far_grad_ref[...] = jnp.concatenate([cut(query, 1), cut(mine, 1), cut(mine, 3), empty], axis=1)
    theirs_ref[:, :LANES] = jnp.concatenate(
        [empty, cut(theirs, 0), cut(theirs, 2), empty], axis=1
    ).astype(BF)
    theirs_ref[:, LANES:] = jnp.concatenate(
        [empty, cut(theirs, 1), cut(theirs, 3), empty], axis=1
    ).astype(BF)


def attend_back(core, own, stat, grad):
    rows = own[0].shape[0]
    return pl.pallas_call(
        attend_back_kernel,
        out_shape=(
            jax.ShapeDtypeStruct((rows, LANES), F32),
            jax.ShapeDtypeStruct((rows, LANES), F32),
            jax.ShapeDtypeStruct((rows, 2 * LANES), BF),
        ),
        in_specs=scalar_first(6),
        out_specs=tuple(whole_vmem(3)),
        scratch_shapes=[
            pltpu.VMEM((2 * rows, LANES), F32),
            pltpu.VMEM((rows, ATTN_HEAD_SIZE), F32),
        ],
        compiler_params=params(),
        cost_estimate=small_cost(),
    )(core, *own[1:], stat, grad)


def gather_later(rows):
    return lax.all_gather(rows, "shard", axis=0, tiled=True, axis_index_groups=same_core())


def collect_later(partial):
    return lax.psum_scatter(
        partial.astype(BF),
        "shard",
        scatter_dimension=0,
        tiled=True,
        axis_index_groups=same_core(),
    ).astype(F32)


def forward_mixer(x, unit, scale, own_unit, layer, core, also, row_weights):
    far = dot_plain(own_unit, layer["far"]).astype(BF)
    maps = dot_plain(own_unit, layer["near"][:, 2 * LANES :]).astype(BF)
    near = dot_plain(own_unit, layer["near"][:, : 2 * LANES]).astype(BF)
    own = (near, maps, far, swap_cores(maps), swap_cores(far))
    gate_raw = jnp.concatenate([near[:, :LANES], far[:, :LANES]], axis=1).astype(F32)
    mine, theirs, starts = mixer(core, own, layer)
    mixed = jnp.concatenate([mine, swap_cores(theirs)], axis=1).astype(F32)
    gated = mixed * jax.nn.silu(gate_raw)
    attended, stat = attend(core, own, own[0] if also is None else also)
    rows = row_weights(mine)
    squares = joined(gated * gated, layer["wide"])
    ssm_scale = lax.rsqrt(chip_sums(squares, attended) / INNER + EPSILON)
    mixer_low = (gated * ssm_scale * layer["gain"]).astype(BF)
    hidden = x + collect(dot_plain(mixer_low, rows["mamba"]) + dot_plain(attended, rows["out"]))
    kept = (
        unit,
        scale,
        own_unit,
        own,
        gate_raw,
        attended,
        stat,
        starts,
        mixed,
        gated,
        mixer_low,
        ssm_scale,
    )
    return hidden, kept, rows


def forward_wide(hidden, layer, rows):
    unit, scale = normalize(hidden)
    own_unit = spread(unit.astype(BF))
    near = dot_plain(own_unit, layer["wide"])
    far = dot_plain(own_unit, layer["wide_far"])
    gate_val = jnp.concatenate([near[:, :FF_CORE], far[:, :FF_CORE]], axis=1)
    up_val = jnp.concatenate([near[:, FF_CORE:], far[:, FF_CORE:]], axis=1)
    swish = (jax.nn.silu(gate_val) * up_val).astype(BF)
    return dot_plain(swish, rows["down"]), (unit, scale, own_unit, gate_val, up_val, swish)


def backward_wide(grad_out, grad_out_own, kept, layer, rows):
    unit, scale, own_unit, gate_val, up_val, swish = kept
    grad_swish = dot_back(grad_out_own, rows["down"])
    sig = jax.nn.sigmoid(gate_val)
    grad_gate = grad_swish * up_val * (sig * (1.0 + gate_val * (1.0 - sig)))
    grad_up = grad_swish * (gate_val * sig)
    grad_near = jnp.concatenate([grad_gate[:, :FF_CORE], grad_up[:, :FF_CORE]], axis=1).astype(BF)
    grad_far = jnp.concatenate([grad_gate[:, FF_CORE:], grad_up[:, FF_CORE:]], axis=1).astype(BF)
    grads = (
        dot_rows(own_unit, grad_near),
        dot_rows(own_unit, grad_far).astype(BF),
        dot_rows(swish, grad_out_own),
    )
    grad_unit = dot_back(grad_near, layer["wide"]) + dot_back(grad_far, layer["wide_far"])
    grad_unit = collect(grad_unit, *grads)
    grad_hidden = grad_out + normalize_back(unit, scale, grad_unit)
    return grad_hidden, *grads


def backward_mixer(grad_hidden, kept, layer, rows, core, reduce_rows):
    (
        unit,
        scale,
        own_unit,
        own,
        gate_raw,
        attended,
        stat,
        starts,
        mixed,
        gated,
        mixer_low,
        ssm_scale,
    ) = kept
    grad_low = grad_hidden.astype(BF)
    grad_own = spread(grad_low)
    grad_mixer = dot_back(grad_own, rows["mamba"])
    grad_attended = dot_back(grad_own, rows["out"]).astype(BF)
    grad_scaled = grad_mixer * layer["gain"]
    near_heads, far_heads, heads_theirs = attend_back(core, own, stat, grad_attended)
    if reduce_rows is not None:
        grad_mamba, grad_out = dot_rows(mixer_low, grad_own), dot_rows(attended, grad_own)
        inner = chip_sums(grad_scaled * gated, near_heads, grad_mamba, grad_out)
    else:
        inner = chip_sums(grad_scaled * gated, near_heads)
    pull_back = ssm_scale * ssm_scale * ssm_scale * inner / INNER
    grad_gated = ssm_scale * grad_scaled - gated * pull_back
    sig = jax.nn.sigmoid(gate_raw)
    grad_mixed = (grad_gated * gate_raw * sig).astype(BF)
    grad_gate_raw = grad_gated * mixed * (sig * (1.0 + gate_raw * (1.0 - sig)))
    grad_recv = swap_cores(grad_mixed[:, LANES:])
    grad_gain = jnp.sum(grad_mixer * gated * ssm_scale, axis=0)
    mine, theirs, conv_grad, cols_grad = mixer_back(
        core, own, layer, starts, grad_mixed[:, :LANES], grad_recv
    )
    other = swap_cores(jnp.concatenate([theirs, heads_theirs], axis=1)).astype(F32)
    block = [slice(k * LANES, (k + 1) * LANES) for k in range(5)]
    if reduce_rows is not None:
        row_total = reduce_rows(grad_mamba, grad_out)
        mine = joined(mine, row_total)
    grad_near = jnp.concatenate(
        [
            grad_gate_raw[:, :LANES],
            mine[:, block[0]],
            mine[:, block[1]] + other[:, block[2]],
            near_heads + other[:, block[4]],
        ],
        axis=1,
    )
    grad_far = jnp.concatenate(
        [
            grad_gate_raw[:, LANES:],
            other[:, block[0]],
            mine[:, block[2]] + other[:, block[1]],
            far_heads + other[:, block[3]],
        ],
        axis=1,
    )
    grad_near, grad_far = grad_near.astype(BF), grad_far.astype(BF)
    near, far = dot_rows(own_unit, grad_near), dot_rows(own_unit, grad_far).astype(BF)
    if reduce_rows is None:
        low = joined(mixer_low, grad_near)
        grad_mamba = dot_rows(low, grad_own)
        grad_out = dot_rows(joined(attended, grad_near), grad_own)
        beside = near, far, grad_mamba, grad_out
        row_total = grad_mamba, grad_out
    else:
        beside = near, far
    grad_unit = dot_back(grad_near, layer["near"]) + dot_back(grad_far, layer["far"])
    grad_x = grad_hidden + normalize_back(unit, scale, collect(grad_unit, *beside))
    return grad_x, near, far, row_total, grad_gain, conv_grad, cols_grad


def section_pair(section, own, other):
    return jnp.where(section == 0, jnp.stack([own, other]), jnp.stack([other, own]))


def cut_in_kernel(w_ref, query_ref, key_ref, value_ref, gain_ref, conv_ref, out_ref):
    rows = w_ref.shape[0]
    gain = gain_ref[...]
    maps = 2 * INNER

    def piece(ref, at, width):
        return (ref[:, at : at + width].astype(F32) * gain).astype(BF)

    steps = piece(w_ref, maps + 2 * NS, NH)
    filler = jnp.zeros((rows, LANES - NARROW - NH), BF)
    rest = jnp.zeros((rows, LANES - 3 * HALF_HEAD), BF)
    for device in range(SHARDS):
        chip, core = device // CORES, device % CORES
        head = (chip // (CHIPS // KEY_VALUE_HEADS) * CORES + core) * HALF_HEAD
        cut = jnp.concatenate(
            [
                piece(w_ref, device * NARROW, NARROW),
                conv_ref[...],
                piece(w_ref, INNER + device * NARROW, NARROW),
                steps,
                filler,
                piece(w_ref, maps + core * NS, NS),
                piece(query_ref, device * HALF_HEAD, HALF_HEAD),
                piece(key_ref, head, HALF_HEAD),
                piece(value_ref, head, HALF_HEAD),
                rest,
            ],
            axis=1,
        )
        out_ref[device] = cut
        out_ref[SHARDS + device] = cut


def cut_wide_kernel(gate_ref, up_ref, gain_ref, out_ref):
    gain = gain_ref[...]
    for device in range(SHARDS):
        at = slice(device * FF_CORE, (device + 1) * FF_CORE)
        for k, ref in enumerate((gate_ref, up_ref)):
            cut = (ref[:, at].astype(F32) * gain).astype(BF)
            low = slice(k * FF_CORE, (k + 1) * FF_CORE)
            out_ref[device, :, low] = cut
            out_ref[SHARDS + device, :, low] = cut


def cut_call(kernel, columns, *operands):
    return pl.pallas_call(
        kernel,
        out_shape=jax.ShapeDtypeStruct((2 * SHARDS, operands[0].shape[0], columns), BF),
        in_specs=whole_vmem(len(operands)),
        out_specs=whole_vmem(1)[0],
        compiler_params=params(),
        cost_estimate=small_cost(),
    )(*operands)


def finish_kernel(in_width, total_ref, gain_ref, mid_ref, *refs):
    raw, outs, norms_ref = refs[:6], refs[6:12], refs[12]
    sums = []
    at = 0
    for k in range(6):
        width = raw[k].shape[1]
        part = slice(at, at + width)
        grad = total_ref[:, part].astype(F32)
        sums.append(jnp.sum(grad * raw[k][...].astype(F32), axis=1, keepdims=True))
        outs[k][...] = grad * (gain_ref if k < 4 else mid_ref)[...]
        at += in_width if k == 0 else width
    lane = lax.broadcasted_iota(jnp.int32, norms_ref.shape, 1)
    norm_in = sums[0] + sums[1] + sums[2] + sums[3]
    norms_ref[...] = jnp.where(lane == 0, norm_in, sums[4] + sums[5])


def finish(in_width, total, gain_in, gain_mid, raw):
    rows = total.shape[0]
    return pl.pallas_call(
        functools.partial(finish_kernel, in_width),
        out_shape=tuple(jax.ShapeDtypeStruct(w.shape, F32) for w in raw)
        + (jax.ShapeDtypeStruct((rows, LANES), F32),),
        in_specs=whole_vmem(9),
        out_specs=tuple(whole_vmem(7)),
        compiler_params=params(),
        cost_estimate=small_cost(),
    )(total, gain_in, gain_mid, *raw)


def body(
    inputs,
    cotangent,
    norm_in,
    w_in,
    conv_w,
    conv_b,
    dt_bias,
    a_log,
    skip_gain,
    norm_ssm,
    w_out,
    query_weight,
    key_weight,
    value_weight,
    output_weight,
    norm_mid,
    w_gate,
    w_up,
    w_down,
):
    place = lax.axis_index("shard")
    core = place % CORES
    core_word = core.reshape(1).astype(jnp.int32)
    section = lax.axis_index("section")
    reps = lax.axis_size("rep")
    local = inputs.shape[2]
    spare = LANES - NARROW

    gain_in = norm_in[0].astype(F32)[:, None]
    gain_mid = norm_mid[0].astype(F32)[:, None]

    own_input = lax.dynamic_index_in_dim(inputs[:, 0], section, 0, False).astype(F32)
    own_target = lax.dynamic_index_in_dim(cotangent[:, 0], section, 0, False)
    unit, scale = normalize(own_input)
    own_unit = spread(unit.astype(BF))
    conv_all = jnp.concatenate([conv_w[0], conv_b], axis=0)
    conv_count = conv_all.size
    conv_cols = jnp.concatenate(
        [conv_all.reshape(-1), jnp.zeros((spare * local - conv_count,), BF)]
    ).reshape(local, spare)
    cut = cut_call(
        cut_in_kernel,
        IN_COLS,
        w_in[0],
        query_weight[0],
        key_weight[0],
        value_weight[0],
        gain_in,
        conv_cols,
    )
    everywhere = ("section", "shard")
    met = lax.all_to_all(cut, everywhere, 0, 0, tiled=True)
    met = met.reshape(2, SHARDS, local, IN_COLS)
    conv_met = met[:, :, :, NARROW:LANES].reshape(2, SHARDS, spare * local)[:, :, :conv_count]
    conv_met = conv_met.reshape(2, SHARDS, CONV + 1, -1).transpose(0, 2, 1, 3)
    conv_met = conv_met.reshape(2, CONV + 1, INNER + 2 * NS).astype(F32)
    own_cols = met.reshape(2, SHARDS * local, IN_COLS)
    other_cols = swap_cores(own_cols)
    cut = cut_call(cut_wide_kernel, WIDE_COLS, w_gate[0], w_up[0], gain_mid)
    wide_cols = lax.all_to_all(cut, everywhere, 0, 0, tiled=True)
    wide_cols = wide_cols.reshape(2, SHARDS * local, WIDE_COLS)
    other_wide = swap_cores(wide_cols)

    def both_layers(own):
        return section_pair(section, own, swap_sections(own))

    raw_rows = jnp.concatenate([w_out[0], output_weight[0], w_down[0]], axis=0)
    raw_rows = joined(raw_rows, met)
    sent_rows = swap_sections(raw_rows)
    row_store = {}

    def rows_at(layer):
        def make(token):
            if not row_store:
                rows = section_pair(section, raw_rows, joined(sent_rows, token))
                row_store["pair"] = rows, swap_cores(rows)
            rows, others = (x[layer] for x in row_store["pair"])
            return {
                "mamba": jnp.concatenate([rows[:out_row], no_rows, others[:out_row], no_rows]),
                "out": jnp.concatenate([rows[out_row:down_row], others[out_row:down_row]]),
                "down": jnp.concatenate([rows[down_row:], others[down_row:]]),
            }

        return make

    out_row, down_row = NARROW, NARROW + HALF_HEAD
    per_head = jnp.concatenate([dt_bias[0], a_log[0], skip_gain[0], norm_ssm[0].astype(F32)])
    per_head = both_layers(per_head)
    own_gain = per_head[:, 3 * NH :]
    other_gain = swap_cores(own_gain)
    lane = lax.broadcasted_iota(jnp.int32, (NH, LANES), 1)
    head_of = jnp.where(lane < NARROW, (lane + place * NARROW) // HD, -1)
    member = (head_of == lax.broadcasted_iota(jnp.int32, (NH, LANES), 0)).astype(F32)
    sel = jnp.concatenate(
        [jnp.zeros((NARROW, LANES), F32), member, jnp.zeros((LANES - NARROW - NH, LANES), F32)]
    ).astype(BF)
    in_first = (head_of[0:1] == head_of[0:1, 0:1]).astype(F32)
    in_second = (head_of[0:1] == head_of[0:1, NARROW - 1 : NARROW]).astype(F32)

    def to_columns(values):
        return jnp.sum(values[:, None] * member, axis=0, keepdims=True)

    def padded(g):
        return jnp.concatenate([g, jnp.zeros((spare,), F32)])

    no_rows = jnp.zeros((spare, MODEL_WIDTH), BF)
    layers = []
    for layer in range(2):
        head_values = per_head[layer]
        cols = jnp.concatenate(
            [
                to_columns(head_values[:NH]),
                to_columns(jnp.exp(head_values[NH : 2 * NH])),
                to_columns(head_values[2 * NH : 3 * NH]),
                in_first,
                in_second,
                jnp.zeros((3, LANES), F32),
            ]
        )
        conv_own = jnp.concatenate(
            [
                lax.dynamic_slice_in_dim(conv_met[layer], place * NARROW, NARROW, axis=1),
                jnp.zeros((CONV + 1, spare), F32),
                by_place(core, conv_met[layer, :, INNER : INNER + NS], conv_met[layer, :, INNER + NS :], 1),
            ],
            axis=1,
        )
        layers.append(
            {
                "near": own_cols[layer],
                "far": other_cols[layer],
                "wide": wide_cols[layer],
                "wide_far": other_wide[layer],
                "conv": jnp.concatenate([conv_own, jnp.zeros((7 - CONV, CONVED), F32)]),
                "cols": cols,
                "sel": sel,
                "gain": jnp.concatenate([padded(own_gain[layer]), padded(other_gain[layer])])[None],
            }
        )

    x = own_input
    outs = []
    target_own = None
    kept_mixer, kept_wide, row_weights = [], [], []
    for layer in range(2):
        if layer == 1:
            unit, scale = normalize(x)
            own_unit = spread(unit.astype(BF))
        hidden, kept, rows = forward_mixer(
            x, unit, scale, own_unit, layers[layer], core_word, target_own, rows_at(layer)
        )
        if layer == 0:
            target_own = gather_later(joined(own_target, hidden))
        row_weights.append(rows)
        kept_mixer.append(kept)
        partial, kept = forward_wide(hidden, layers[layer], rows)
        kept_wide.append(kept)
        total = collect(partial) if layer == 0 else collect_later(partial)
        outs.append((hidden + total).astype(BF))
        x = outs[layer].astype(F32)

    def exchanged(first, second):
        own = jnp.where(section == 0, first, second)
        other = swap_sections(jnp.where(section == 0, second, first).astype(BF))
        return section_pair(section, own, other.astype(own.dtype))

    part = local // reps

    def by_parts(columns):
        cut = columns.reshape(SHARDS, reps, part, columns.shape[1])
        return cut.transpose(1, 0, 2, 3).reshape(reps * SHARDS, part, columns.shape[1])

    def over_all(sent):
        met = lax.all_to_all(sent, ("section", "rep", "shard"), 0, 0, tiled=True)
        met = met.reshape(2 * reps, SHARDS, part, sent.shape[2])
        return jnp.sum(met.astype(F32), axis=0)

    extra_width = -(-(conv_count + NARROW + 3 * NH) // (reps * part))
    in_width = -(-(2 * INNER + 2 * NS + NH + extra_width) // LANES) * LANES

    def to_all(rows, axes, count):
        copies = jnp.broadcast_to(rows[None], (count,) + rows.shape)
        met = lax.all_to_all(copies, axes, 0, 0, tiled=True)
        return met.reshape(count * rows.shape[0], rows.shape[1])

    def even(g):
        return g.transpose(1, 0, 2).reshape(part, -1)

    def by_key_head(g):
        groups = CHIPS // KEY_VALUE_HEADS
        g = jnp.sum(g.reshape(KEY_VALUE_HEADS, groups, CORES, part, -1), axis=1)
        return even(g.reshape(KEY_VALUE_HEADS * CORES, part, -1))

    def by_weight(total):
        maps = total[:, :, 2 * LANES : 3 * LANES].reshape(CHIPS, CORES, part, LANES)
        heads = [
            total[:, :, 3 * LANES + k * HALF_HEAD : 3 * LANES + (k + 1) * HALF_HEAD]
            for k in range(3)
        ]
        columns = [
            even(total[:, :, :NARROW]),
            even(total[:, :, LANES : LANES + NARROW]),
            even(jnp.sum(maps, axis=0)),
            jnp.sum(total[:, :, LANES + NARROW : LANES + NARROW + NH], axis=0),
            jnp.sum(total[:, :, NARROW : NARROW + extra_width], axis=0),
            jnp.zeros((part, in_width - 2 * INNER - 2 * NS - NH - extra_width), F32),
            even(heads[0]),
            by_key_head(heads[1]),
            by_key_head(heads[2]),
            even(total[:, :, IN_COLS : IN_COLS + FF_CORE]),
            even(total[:, :, IN_COLS + FF_CORE :]),
        ]
        return jnp.concatenate(columns, axis=1).astype(BF)

    def pair_total(near, far):
        return (near + swap_cores(far).astype(F32)).astype(BF)

    def small_parts(grad_gain, conv_grad, cols_grad):
        conv_grad = conv_grad[: CONV + 1]
        maps_grad = by_place(core, conv_grad[:, LANES : 2 * LANES], conv_grad[:, 2 * LANES :], 1)
        conv_grad = jnp.concatenate(
            [
                lax.dynamic_update_slice_in_dim(
                    jnp.zeros((CONV + 1, INNER), F32), conv_grad[:, :NARROW], place * NARROW, axis=1
                ),
                maps_grad,
            ],
            axis=1,
        )
        conv_grad = conv_grad.reshape(CONV + 1, SHARDS, -1).transpose(1, 0, 2).reshape(SHARDS, -1)
        gain_halves = by_place(core, grad_gain[:NARROW], grad_gain[LANES : LANES + NARROW], 0)
        gain_grad = lax.dynamic_update_slice_in_dim(
            jnp.zeros((INNER,), F32), gain_halves, (place // CORES) * CORES * NARROW, axis=0
        ).reshape(SHARDS, -1)
        head_grad = jnp.sum(cols_grad[:3, None, :] * member[None], axis=2).reshape(1, -1)
        extra = jnp.concatenate(
            [conv_grad, gain_grad, jnp.broadcast_to(head_grad, (SHARDS, 3 * NH))], axis=1
        )
        width = -(-extra.shape[1] // (reps * part))
        missing = reps * part * width - extra.shape[1]
        extra = jnp.concatenate([extra, jnp.zeros((SHARDS, missing), F32)], axis=1)
        extra = extra.reshape(SHARDS, reps, part, width).transpose(1, 0, 2, 3)
        return extra.reshape(reps * SHARDS, part, width).astype(BF)

    def with_small(sent, extra):
        room = spare - extra.shape[2]
        extra = jnp.pad(extra, ((0, 0), (0, 0), (0, room)))
        return jnp.concatenate([sent[:, :, :NARROW], extra, sent[:, :, LANES:]], axis=2)

    def rows_of(grad_mamba, grad_out, grad_down):
        mine = jnp.concatenate([grad_mamba[:NARROW], grad_out[:HALF_HEAD], grad_down[:FF_CORE]])
        theirs = jnp.concatenate(
            [grad_mamba[LANES : LANES + NARROW], grad_out[HALF_HEAD:], grad_down[FF_CORE:]]
        )
        return pair_total(mine, theirs.astype(BF))

    def reduce_rows(grad_mamba, grad_out):
        first_rows = rows_of(grad_mamba, grad_out, grad_down)
        met = lax.all_to_all(
            jnp.concatenate([first_rows, last_rows]), ("section", "rep"), 0, 0, tiled=True
        )
        met = met.reshape(2 * reps, -1, MODEL_WIDTH).astype(F32)
        return joined(jnp.sum(met, axis=0), outs[1]).astype(BF)

    sent = [None, None]
    grad = own_target.astype(F32)
    input_grads = [None, None]
    for layer in (1, 0):
        grad_own = target_own if layer == 1 else spread(grad.astype(BF))
        grad_hidden, grad_wide, grad_wide_far, grad_down = backward_wide(
            grad, grad_own, kept_wide[layer], layers[layer], row_weights[layer]
        )
        grad_x, grad_near, grad_far, row_total, *small = backward_mixer(
            grad_hidden,
            kept_mixer[layer],
            layers[layer],
            row_weights[layer],
            core_word,
            reduce_rows if layer == 0 else None,
        )
        if layer == 1:
            last_rows = rows_of(*row_total, grad_down)
        input_grads[layer] = grad_x
        grad = grad_x.astype(BF).astype(F32)
        columns = [pair_total(grad_near, grad_far), pair_total(grad_wide, grad_wide_far)]
        columns = jnp.concatenate(columns, axis=1)
        sent[layer] = with_small(by_parts(columns), small_parts(*small))

    section_out = exchanged(outs[0], joined(outs[1], grad_near))[None, :, None]
    input_grad = exchanged(*input_grads)[None, :, None]
    columns = by_weight(over_all(jnp.concatenate(sent)))
    totals = to_all(jnp.concatenate([columns, row_total.reshape(part, -1)], axis=1), "rep", reps)
    columns = totals[:, : columns.shape[1]]
    row_total = totals[:, columns.shape[1] :].reshape(-1, MODEL_WIDTH).astype(F32)
    used = 2 * INNER + 2 * NS + NH
    extra = columns[:, used : used + extra_width].astype(F32).reshape(-1)
    conv_total = extra[:conv_count].reshape(CONV + 1, -1)
    gain_total = extra[conv_count : conv_count + NARROW]
    head_total = extra[conv_count + NARROW : conv_count + NARROW + 3 * NH].reshape(3, NH)
    raw = [w[0] for w in (w_in, query_weight, key_weight, value_weight, w_gate, w_up)]
    *by_rows, norms = finish(in_width, totals, gain_in, gain_mid, raw)
    grad_norm_in, grad_norm_mid = norms[:, 0], norms[:, 1]
    return (
        section_out,
        input_grad,
        grad_norm_in[None],
        by_rows[0][None],
        conv_total[:CONV][None],
        conv_total[CONV][None],
        head_total[0][None],
        head_total[1][None],
        head_total[2][None],
        gain_total[None],
        row_total[:out_row][None],
        by_rows[1][None],
        by_rows[2][None],
        by_rows[3][None],
        row_total[out_row:down_row][None],
        grad_norm_mid[None],
        by_rows[4][None],
        by_rows[5][None],
        row_total[down_row:][None],
    )


def solution(mesh):
    return jax.shard_map(
        body,
        mesh=mesh,
        in_specs=(
            P(None, "rep", "shard", None),
            P(None, "rep", "shard", None),
            P("section", "shard"),
            P("section", "shard", None),
            P("section", None, "shard"),
            P("section", "shard"),
            P("section", None),
            P("section", None),
            P("section", None),
            P("section", "shard"),
            P("section", "shard", None),
            P("section", "shard", None),
            P("section", "shard", None),
            P("section", "shard", None),
            P("section", "shard", None),
            P("section", "shard"),
            P("section", "shard", None),
            P("section", "shard", None),
            P("section", "shard", None),
        ),
        out_specs=(
            P("section", None, "rep", "shard", None),
            P("section", None, "rep", "shard", None),
            P("section", "shard"),
            P("section", "shard", None),
            P("section", None, "shard"),
            P("section", "shard"),
            P("section", None),
            P("section", None),
            P("section", None),
            P("section", "shard"),
            P("section", "shard", None),
            P("section", "shard", None),
            P("section", "shard", None),
            P("section", "shard", None),
            P("section", "shard", None),
            P("section", "shard"),
            P("section", "shard", None),
            P("section", "shard", None),
            P("section", "shard", None),
        ),
        check_vma=False,
    )
```

```python
import functools

import jax
import jax.numpy as jnp
from jax import lax
from jax.experimental import pallas as pl
from jax.experimental.pallas import tpu as pltpu
from jax.sharding import PartitionSpec as P

MODEL_WIDTH = 1024
NH = 24
HD = 64
NS = 128
QUERY_HEADS = 8
KEY_VALUE_HEADS = 2
ATTN_HEAD_SIZE = 64
FF = 2048
CONV = 4
MB = 2

EPSILON = 1e-05

SHARDS = 16
CORES = 2
CHIPS = SHARDS // CORES
INNER = NH * HD
NARROW = INNER // SHARDS
LANES = 128
HALF_HEAD = ATTN_HEAD_SIZE // 2
IN_COLS = 4 * LANES
WIDE_COLS = 2 * LANES
CONVED = 3 * LANES
CHUNK = 128
BLOCK = 64
FF_CORE = FF // SHARDS
RATIO = ATTN_HEAD_SIZE ** (-0.5)

BF = jnp.bfloat16
F32 = jnp.float32


def dot_plain(former, latter):
    return jnp.dot(former, latter, preferred_element_type=F32)


def dot_rows(former, latter):
    return lax.dot_general(former, latter, (((0,), (0,)), ((), ())), preferred_element_type=F32)


def dot_back(former, latter):
    return lax.dot_general(former, latter, (((1,), (1,)), ((), ())), preferred_element_type=F32)


def exact(former, latter, dims):
    return lax.dot_general(
        former,
        latter,
        ((dims[:1], dims[1:]), ((), ())),
        precision=lax.Precision.HIGHEST,
        preferred_element_type=F32,
    )


def swap_cores(x):
    return lax.ppermute(x, "shard", [(i, i ^ 1) for i in range(SHARDS)])


def swap_sections(x):
    return lax.ppermute(x, "section", [(0, 1), (1, 0)])


def same_core():
    return [list(range(core, SHARDS, CORES)) for core in range(CORES)]


def joined(x, *met):
    zero = sum((m[(0,) * m.ndim] * 0).astype(F32) for m in met)
    return x + zero.astype(x.dtype)


def spread(rows):
    count, width = rows.shape
    copies = jnp.broadcast_to(rows[None], (CHIPS, count, width)).reshape(CHIPS * count, width)
    return lax.all_to_all(copies, "shard", 0, 0, axis_index_groups=same_core(), tiled=True)


def collect(partial, *beside):
    rows = partial.shape[0] // CHIPS
    met = lax.all_to_all(
        partial.astype(BF), "shard", 0, 0, axis_index_groups=same_core(), tiled=True
    )
    total = jnp.sum(met.reshape(CHIPS, rows, partial.shape[1]).astype(F32), axis=0)
    return joined(total, *beside) if beside else total


def chip_sums(x, *beside):
    ones = jnp.ones((8, x.shape[1]), F32)
    sums = exact(ones, x, (1, 1))
    copies = jnp.broadcast_to(sums[None], (CHIPS,) + sums.shape).reshape(8 * CHIPS, -1)
    met = lax.all_to_all(copies, "shard", 0, 0, axis_index_groups=same_core(), tiled=True)
    share = joined(jnp.full((8 * CHIPS, LANES), 0.125, F32), *beside)
    return exact(met, share, (0, 0))[:, :1]


def by_place(core, own, other, axis):
    return jnp.where(
        core == 0,
        jnp.concatenate([own, other], axis=axis),
        jnp.concatenate([other, own], axis=axis),
    )


def normalize(x):
    scale = lax.rsqrt(jnp.mean(x * x, axis=-1, keepdims=True) + EPSILON)
    return x * scale, scale


def normalize_back(unit, scale, grad):
    return scale * (grad - unit * jnp.mean(grad * unit, axis=-1, keepdims=True))


def whole_vmem(count):
    return [pl.BlockSpec(memory_space=pltpu.VMEM)] * count


def scalar_first(count):
    return [pl.BlockSpec(memory_space=pltpu.SMEM)] + whole_vmem(count)


def params():
    return pltpu.CompilerParams(vmem_limit_bytes=48 * 2**20)


def small_cost():
    return pl.CostEstimate(flops=10**6, bytes_accessed=10**4, transcendentals=0)


def softplus(v):
    return jnp.maximum(v, 0.0) + jnp.log1p(jnp.exp(-jnp.abs(v)))


def row_parts(refs, at):
    states, first, second = refs
    parts = [ref[at, low : low + LANES] for ref, low in (states, first, second)]
    return jnp.concatenate(parts, axis=1).astype(F32)


def sources(near_ref, maps_ref, far_ref, recv_maps_ref, recv_far_ref):
    own = ((near_ref, LANES), (maps_ref, 0), (far_ref, 2 * LANES))
    recv = ((recv_far_ref, LANES), (recv_far_ref, 2 * LANES), (recv_maps_ref, 0))
    return own, recv


def chunk_rows(core, own_refs, recv_refs, k):
    at = pl.ds(pl.multiple_of(k * BLOCK, BLOCK), BLOCK)
    own = row_parts(own_refs, at)
    recv = row_parts(recv_refs, at)
    return jnp.where(core == 0, own, recv), jnp.where(core == 0, recv, own)


def chunk_parts(core, ext, conv_ref, cols_ref, sel_ref):
    conv = conv_ref[CONV : CONV + 1, :]
    for j in range(CONV):
        start = 8 - (CONV - 1) + j
        conv = conv + conv_ref[j : j + 1, :] * ext[start : start + CHUNK, :]
    sig = 1.0 / (1.0 + jnp.exp(-conv))
    activated = conv * sig
    states_in = activated[:, 0:LANES]
    first, second = activated[:, LANES : 2 * LANES], activated[:, 2 * LANES :]
    input_map = jnp.where(core == 0, first, second)
    output_map = jnp.where(core == 0, second, first)
    raw = dot_plain(ext[8 : 8 + CHUNK, 0:LANES].astype(BF), sel_ref[...]) + cols_ref[0:1, :]
    step = softplus(raw)
    log_decay = -step * cols_ref[1:2, :]
    rows = lax.broadcasted_iota(jnp.int32, (CHUNK, CHUNK), 0)
    cols = lax.broadcasted_iota(jnp.int32, (CHUNK, CHUNK), 1)
    causal = cols <= rows
    lower = jnp.where(causal, 1.0, 0.0)
    cumulative = exact(lower, log_decay, (1, 0))
    turned = exact(log_decay, lower, (0, 1))
    weighted = states_in * step
    coupling = dot_back(output_map.astype(BF), input_map.astype(BF))
    within = []
    for lane in (0, NARROW - 1):
        gap = cumulative[:, lane : lane + 1] - turned[lane : lane + 1, :]
        within.append(jnp.where(causal, jnp.exp(jnp.where(causal, gap, 0.0)), 0.0))
    last = cumulative[CHUNK - 1 : CHUNK, :]
    tail = jnp.exp(last - cumulative)
    decay = jnp.exp(turned[:, CHUNK - 1 : CHUNK])
    return (
        conv,
        sig,
        states_in,
        input_map.astype(BF),
        output_map.astype(BF),
        raw,
        step,
        log_decay,
        lower,
        cumulative,
        weighted,
        coupling,
        within,
        last,
        tail,
        decay,
    )


def mixer_kernel(
    core_ref,
    near_ref,
    maps_ref,
    far_ref,
    recv_maps_ref,
    recv_far_ref,
    conv_ref,
    cols_ref,
    sel_ref,
    mine_ref,
    theirs_ref,
    starts_ref,
    ext,
):
    core = core_ref[0]
    own_refs, recv_refs = sources(near_ref, maps_ref, far_ref, recv_maps_ref, recv_far_ref)
    ext[0:8, :] = jnp.zeros((8, CONVED), F32)

    def chunk(k, state):
        first, second = chunk_rows(core, own_refs, recv_refs, k)
        ext[8 : 8 + BLOCK, :] = first
        ext[8 + BLOCK : 8 + CHUNK, :] = second
        (
            conv,
            sig,
            states_in,
            input_map,
            output_map,
            raw,
            step,
            log_decay,
            lower,
            cumulative,
            weighted,
            coupling,
            within,
            last,
            tail,
            decay,
        ) = chunk_parts(core, ext, conv_ref, cols_ref, sel_ref)
        starts_ref[k] = state
        mixed = dot_back(output_map, state.astype(BF)) * jnp.exp(cumulative)
        mixed = mixed + cols_ref[2:3, :] * states_in
        for head in range(2):
            mixed = mixed + dot_plain(
                (within[head] * coupling).astype(BF),
                (weighted * cols_ref[3 + head : 4 + head, :]).astype(BF),
            )
        state = decay * state + dot_rows((weighted * tail).astype(BF), input_map)
        at = pl.ds(pl.multiple_of(k * BLOCK, BLOCK), BLOCK)
        low, high = mixed[:BLOCK, :], mixed[BLOCK:, :]
        mine_ref[at, :] = jnp.where(core == 0, low, high).astype(BF)
        theirs_ref[at, :] = jnp.where(core == 0, high, low).astype(BF)
        ext[0:8, :] = ext[CHUNK : CHUNK + 8, :]
        return state

    lax.fori_loop(0, CHIPS, chunk, jnp.zeros((LANES, NS), F32), unroll=4)


def anywhere(count):
    return [pl.BlockSpec(memory_space=pl.ANY)] * count


def mixer(core, own, layer):
    rows = own[0].shape[0]
    return pl.pallas_call(
        mixer_kernel,
        out_shape=(
            jax.ShapeDtypeStruct((rows, LANES), BF),
            jax.ShapeDtypeStruct((rows, LANES), BF),
            jax.ShapeDtypeStruct((CHIPS, LANES, NS), F32),
        ),
        in_specs=scalar_first(8),
        out_specs=tuple(whole_vmem(3)),
        scratch_shapes=[pltpu.VMEM((CHUNK + 8, CONVED), F32)],
        compiler_params=params(),
        cost_estimate=small_cost(),
    )(core, *own, layer["conv"], layer["cols"], layer["sel"])


def mixer_back_kernel(
    core_ref,
    near_ref,
    maps_ref,
    far_ref,
    recv_maps_ref,
    recv_far_ref,
    conv_ref,
    cols_ref,
    sel_ref,
    starts_ref,
    grad_own_ref,
    grad_recv_ref,
    *refs,
):
    mine_ref, theirs_ref, conv_grad_ref, cols_grad_ref, ext, later = refs[-6:]
    core = core_ref[0]
    own_refs, recv_refs = sources(near_ref, maps_ref, far_ref, recv_maps_ref, recv_far_ref)
    later[...] = jnp.zeros((CHUNK + 8, CONVED), F32)
    conv_grad_ref[...] = jnp.zeros((8, CONVED), F32)
    cols_grad_ref[...] = jnp.zeros((8, LANES), F32)
    ones = jnp.ones((CHUNK, LANES), BF)
    lanes = lax.broadcasted_iota(jnp.int32, (CHUNK, LANES), 1)

    def chunk(turn, grad_state):
        k = CHIPS - 1 - turn
        first, second = chunk_rows(core, own_refs, recv_refs, k)
        ext[8 : 8 + BLOCK, :] = first
        ext[8 + BLOCK : 8 + CHUNK, :] = second
        before = jnp.maximum(k - 1, 0)
        at_end = pl.ds(pl.multiple_of(before * BLOCK + BLOCK - 16, 16), 16)
        own_end = row_parts(own_refs, at_end)
        recv_end = row_parts(recv_refs, at_end)
        end = jnp.where(core == 0, recv_end, own_end)[8:16, :]
        ext[0:8, :] = jnp.where(k > 0, end, 0.0)
        (
            conv,
            sig,
            states_in,
            input_map,
            output_map,
            raw,
            step,
            log_decay,
            lower,
            cumulative,
            weighted,
            coupling,
            within,
            last,
            tail,
            decay,
        ) = chunk_parts(core, ext, conv_ref, cols_ref, sel_ref)
        start = starts_ref[k]
        start_low = start.astype(BF)
        at = pl.ds(pl.multiple_of(k * BLOCK, BLOCK), BLOCK)
        grad_mine = grad_own_ref[at, :].astype(F32)
        grad_theirs = grad_recv_ref[at, :].astype(F32)
        grad = jnp.concatenate(
            [
                jnp.where(core == 0, grad_mine, grad_theirs),
                jnp.where(core == 0, grad_theirs, grad_mine),
            ],
            axis=0,
        )
        grad_states = cols_ref[2:3, :] * grad
        grad_skip = jnp.sum(grad * states_in, axis=0, keepdims=True)
        grown = grad * jnp.exp(cumulative)
        grown_low = grown.astype(BF)
        grad_out_map = dot_plain(grown_low, start_low)
        grad_start = dot_rows(grown_low, output_map)
        grad_cum = grown * dot_back(output_map, start_low)
        grad_coupling = jnp.zeros((CHUNK, CHUNK), F32)
        grad_weighted = jnp.zeros((CHUNK, LANES), F32)
        for head in range(2):
            member = cols_ref[3 + head : 4 + head, :]
            grad_head = (grad * member).astype(BF)
            grad_mixing = dot_back(grad_head, weighted.astype(BF))
            mixing = within[head] * coupling
            grad_weighted = grad_weighted + dot_rows(mixing.astype(BF), grad_head)
            grad_coupling = grad_coupling + grad_mixing * within[head]
            pairs = (grad_mixing * mixing).astype(BF)
            change = dot_plain(pairs, ones) - dot_rows(pairs, ones)
            grad_cum = grad_cum + jnp.where(lanes == head * (NARROW - 1), change, 0.0)
        coupling_low = grad_coupling.astype(BF)
        grad_out_map = grad_out_map + dot_plain(coupling_low, input_map)
        grad_in_map = dot_rows(coupling_low, output_map)
        state_low = grad_state.astype(BF)
        tailed = weighted * tail
        grad_in_map = grad_in_map + dot_plain(tailed.astype(BF), state_low)
        reach = dot_back(input_map, state_low)
        grad_weighted = grad_weighted + reach * tail
        moved = reach * tailed
        grad_cum = grad_cum - moved
        kept = exact(jnp.ones((8, NS), F32), grad_state * start, (1, 1))[0:1, :]
        grad_last = jnp.sum(moved, axis=0, keepdims=True) + kept * jnp.exp(last)
        grad_log = exact(lower, grad_cum, (0, 0)) + grad_last
        grad_step = grad_weighted * states_in - cols_ref[1:2, :] * grad_log
        grad_states = grad_states + grad_weighted * step
        grad_raw = grad_step / (1.0 + jnp.exp(-raw))
        cols_grad_ref[0:1, :] += jnp.sum(grad_raw, axis=0, keepdims=True)
        cols_grad_ref[1:2, :] += jnp.sum(grad_log * log_decay, axis=0, keepdims=True)
        cols_grad_ref[2:3, :] += grad_skip
        grad_dt = exact(grad_raw, sel_ref[...].astype(F32), (1, 1))
        slope = sig * (1.0 + conv * (1.0 - sig))
        grad_first = jnp.where(core == 0, grad_in_map, grad_out_map)
        grad_second = jnp.where(core == 0, grad_out_map, grad_in_map)
        grad_conv = jnp.concatenate([grad_states, grad_first, grad_second], axis=1) * slope
        later[CHUNK : CHUNK + 8, :] = later[0:8, :]
        later[0:CHUNK, :] = grad_conv
        conv_grad_ref[CONV : CONV + 1, :] += jnp.sum(grad_conv, axis=0, keepdims=True)
        grad_in = jnp.zeros((CHUNK, CONVED), F32)
        for j in range(CONV):
            low = 8 - (CONV - 1) + j
            conv_grad_ref[j : j + 1, :] += jnp.sum(
                grad_conv * ext[low : low + CHUNK, :], axis=0, keepdims=True
            )
            ahead = CONV - 1 - j
            grad_in = grad_in + conv_ref[j : j + 1, :] * later[ahead : ahead + CHUNK, :]
        grad_in = jnp.concatenate([grad_in[:, 0:LANES] + grad_dt, grad_in[:, LANES:]], axis=1)
        low, high = grad_in[:BLOCK, :], grad_in[BLOCK:, :]
        mine_ref[at, :] = jnp.where(core == 0, low, high)
        theirs_ref[at, :] = jnp.where(core == 0, high, low).astype(BF)
        return decay * grad_state + grad_start

    lax.fori_loop(0, CHIPS, chunk, jnp.zeros((LANES, NS), F32), unroll=4)


def mixer_back(core, own, layer, starts, grad_own, grad_recv):
    rows = own[0].shape[0]
    return pl.pallas_call(
        mixer_back_kernel,
        out_shape=(
            jax.ShapeDtypeStruct((rows, CONVED), F32),
            jax.ShapeDtypeStruct((rows, CONVED), BF),
            jax.ShapeDtypeStruct((8, CONVED), F32),
            jax.ShapeDtypeStruct((8, LANES), F32),
        ),
        in_specs=scalar_first(11),
        out_specs=tuple(whole_vmem(4)),
        scratch_shapes=[pltpu.VMEM((CHUNK + 8, CONVED), F32)] * 2,
        compiler_params=params(),
        cost_estimate=small_cost(),
    )(core, *own, layer["conv"], layer["cols"], layer["sel"], starts, grad_own, grad_recv)


def seen(core, part, rows, columns):
    row = lax.broadcasted_iota(jnp.int32, (rows, columns), 0) + part * rows
    col = lax.broadcasted_iota(jnp.int32, (rows, columns), 1)
    half = columns // 2
    query_at = (row // BLOCK * 2 + core) * BLOCK + row % BLOCK
    other = col // half
    key = col - other * half
    key_at = (key // BLOCK * 2 + jnp.where(other == 0, core, 1 - core)) * BLOCK + key % BLOCK
    return key_at <= query_at


def head_part(near, far, part):
    at = slice(part * HALF_HEAD, (part + 1) * HALF_HEAD)
    return jnp.concatenate([near[:, at], far[:, at]], axis=1)


def heads_of(maps_ref, far_ref, recv_maps_ref, recv_far_ref):
    near, far = maps_ref[:, LANES:], far_ref[:, 3 * LANES :]
    recv_near, recv_far = recv_far_ref[:, 3 * LANES :], recv_maps_ref[:, LANES:]
    keys, values = (
        jnp.concatenate([head_part(near, far, k), head_part(recv_near, recv_far, k)], axis=0)
        for k in (1, 2)
    )
    return head_part(near, far, 0), keys, values


def attend_kernel(
    core_ref, maps_ref, far_ref, recv_maps_ref, recv_far_ref, also_ref, out_ref, stat_ref
):
    core = core_ref[0]
    queries, keys, values = heads_of(maps_ref, far_ref, recv_maps_ref, recv_far_ref)
    for part in range(maps_ref.shape[0] // CHUNK):
        at = slice(part * CHUNK, (part + 1) * CHUNK)
        scores = dot_back(queries[at], keys) * RATIO
        scores = jnp.where(seen(core, part, *scores.shape), scores, -1e30)
        top = jnp.max(scores, axis=1, keepdims=True)
        grown = jnp.exp(scores - top)
        total = jnp.sum(grown, axis=1, keepdims=True)
        soft = grown / total
        out_ref[at, :] = dot_plain(soft.astype(BF), values).astype(BF)
        stat_ref[at, :] = jnp.broadcast_to(top + jnp.log(total), (CHUNK, LANES))


def attend(core, own, also):
    rows = own[0].shape[0]
    return pl.pallas_call(
        attend_kernel,
        out_shape=(
            jax.ShapeDtypeStruct((rows, ATTN_HEAD_SIZE), BF),
            jax.ShapeDtypeStruct((rows, LANES), F32),
        ),
        in_specs=scalar_first(4) + anywhere(1),
        out_specs=tuple(whole_vmem(2)),
        compiler_params=params(),
        cost_estimate=small_cost(),
    )(core, *own[1:], also)


def attend_back_kernel(
    core_ref,
    maps_ref,
    far_ref,
    recv_maps_ref,
    recv_far_ref,
    stat_ref,
    grad_ref,
    *refs,
):
    near_grad_ref, far_grad_ref, theirs_ref, total, query_total = refs[-5:]
    core = core_ref[0]
    queries, keys, values = heads_of(maps_ref, far_ref, recv_maps_ref, recv_far_ref)
    total[...] = jnp.zeros(total.shape, F32)
    half = maps_ref.shape[0]
    for part in range(half // CHUNK):
        at = slice(part * CHUNK, (part + 1) * CHUNK)
        query = queries[at]
        grad = grad_ref[at, :]
        scores = dot_back(query, keys) * RATIO
        visible = seen(core, part, *scores.shape)
        soft = jnp.where(visible, jnp.exp(scores - stat_ref[at, 0:1]), 0.0)
        grad_soft = dot_back(grad, values)
        row_total = jnp.sum(soft * grad_soft, axis=1, keepdims=True)
        grad_scores = (soft * (grad_soft - row_total)).astype(BF)
        query_total[at, :] = dot_plain(grad_scores, keys) * RATIO
        key_grad = dot_rows(grad_scores, query) * RATIO
        value_grad = dot_rows(soft.astype(BF), grad)
        total[...] += jnp.concatenate([key_grad, value_grad], axis=1)
    empty = jnp.zeros((half, HALF_HEAD), F32)
    mine, theirs = total[:half, :], total[half:, :]

    def cut(x, at):
        return x[:, at * HALF_HEAD : (at + 1) * HALF_HEAD]

    query = query_total[...]
    near_grad_ref[...] = jnp.concatenate([cut(query, 0), cut(mine, 0), cut(mine, 2), empty], axis=1)
    far_grad_ref[...] = jnp.concatenate([cut(query, 1), cut(mine, 1), cut(mine, 3), empty], axis=1)
    theirs_ref[:, :LANES] = jnp.concatenate(
        [empty, cut(theirs, 0), cut(theirs, 2), empty], axis=1
    ).astype(BF)
    theirs_ref[:, LANES:] = jnp.concatenate(
        [empty, cut(theirs, 1), cut(theirs, 3), empty], axis=1
    ).astype(BF)


def attend_back(core, own, stat, grad):
    rows = own[0].shape[0]
    return pl.pallas_call(
        attend_back_kernel,
        out_shape=(
            jax.ShapeDtypeStruct((rows, LANES), F32),
            jax.ShapeDtypeStruct((rows, LANES), F32),
            jax.ShapeDtypeStruct((rows, 2 * LANES), BF),
        ),
        in_specs=scalar_first(6),
        out_specs=tuple(whole_vmem(3)),
        scratch_shapes=[
            pltpu.VMEM((2 * rows, LANES), F32),
            pltpu.VMEM((rows, ATTN_HEAD_SIZE), F32),
        ],
        compiler_params=params(),
        cost_estimate=small_cost(),
    )(core, *own[1:], stat, grad)


def gather_later(rows):
    return lax.all_gather(rows, "shard", axis=0, tiled=True, axis_index_groups=same_core())


def collect_later(partial):
    return lax.psum_scatter(
        partial.astype(BF),
        "shard",
        scatter_dimension=0,
        tiled=True,
        axis_index_groups=same_core(),
    ).astype(F32)


def forward_mixer(x, unit, scale, own_unit, layer, core, also, row_weights):
    far = dot_plain(own_unit, layer["far"]).astype(BF)
    maps = dot_plain(own_unit, layer["near"][:, 2 * LANES :]).astype(BF)
    near = dot_plain(own_unit, layer["near"][:, : 2 * LANES]).astype(BF)
    own = (near, maps, far, swap_cores(maps), swap_cores(far))
    gate_raw = jnp.concatenate([near[:, :LANES], far[:, :LANES]], axis=1).astype(F32)
    mine, theirs, starts = mixer(core, own, layer)
    mixed = jnp.concatenate([mine, swap_cores(theirs)], axis=1).astype(F32)
    gated = mixed * jax.nn.silu(gate_raw)
    attended, stat = attend(core, own, own[0] if also is None else also)
    rows = row_weights(mine)
    squares = joined(gated * gated, layer["wide"])
    ssm_scale = lax.rsqrt(chip_sums(squares, attended) / INNER + EPSILON)
    mixer_low = (gated * ssm_scale * layer["gain"]).astype(BF)
    hidden = x + collect(dot_plain(mixer_low, rows["mamba"]) + dot_plain(attended, rows["out"]))
    kept = (
        unit,
        scale,
        own_unit,
        own,
        gate_raw,
        attended,
        stat,
        starts,
        mixed,
        gated,
        mixer_low,
        ssm_scale,
    )
    return hidden, kept, rows


def forward_wide(hidden, layer, rows):
    unit, scale = normalize(hidden)
    own_unit = spread(unit.astype(BF))
    near = dot_plain(own_unit, layer["wide"])
    far = dot_plain(own_unit, layer["wide_far"])
    gate_val = jnp.concatenate([near[:, :FF_CORE], far[:, :FF_CORE]], axis=1)
    up_val = jnp.concatenate([near[:, FF_CORE:], far[:, FF_CORE:]], axis=1)
    swish = (jax.nn.silu(gate_val) * up_val).astype(BF)
    return dot_plain(swish, rows["down"]), (unit, scale, own_unit, gate_val, up_val, swish)


def backward_wide(grad_out, grad_out_own, kept, layer, rows):
    unit, scale, own_unit, gate_val, up_val, swish = kept
    grad_swish = dot_back(grad_out_own, rows["down"])
    sig = jax.nn.sigmoid(gate_val)
    grad_gate = grad_swish * up_val * (sig * (1.0 + gate_val * (1.0 - sig)))
    grad_up = grad_swish * (gate_val * sig)
    grad_near = jnp.concatenate([grad_gate[:, :FF_CORE], grad_up[:, :FF_CORE]], axis=1).astype(BF)
    grad_far = jnp.concatenate([grad_gate[:, FF_CORE:], grad_up[:, FF_CORE:]], axis=1).astype(BF)
    grads = (
        dot_rows(own_unit, grad_near),
        dot_rows(own_unit, grad_far).astype(BF),
        dot_rows(swish, grad_out_own),
    )
    grad_unit = dot_back(grad_near, layer["wide"]) + dot_back(grad_far, layer["wide_far"])
    grad_unit = collect(grad_unit, *grads)
    grad_hidden = grad_out + normalize_back(unit, scale, grad_unit)
    return grad_hidden, *grads


def backward_mixer(grad_hidden, kept, layer, rows, core, reduce_rows, pending):
    (
        unit,
        scale,
        own_unit,
        own,
        gate_raw,
        attended,
        stat,
        starts,
        mixed,
        gated,
        mixer_low,
        ssm_scale,
    ) = kept
    grad_low = grad_hidden.astype(BF)
    grad_own = spread(grad_low)
    grad_mixer = dot_back(grad_own, rows["mamba"])
    grad_attended = dot_back(grad_own, rows["out"]).astype(BF)
    grad_scaled = grad_mixer * layer["gain"]
    near_heads, far_heads, heads_theirs = attend_back(core, own, stat, grad_attended)
    if reduce_rows is not None:
        grad_mamba, grad_out = dot_rows(mixer_low, grad_own), dot_rows(attended, grad_own)
        inner = chip_sums(grad_scaled * gated, near_heads, grad_mamba, grad_out)
    else:
        inner = chip_sums(grad_scaled * gated, near_heads)
    pull_back = ssm_scale * ssm_scale * ssm_scale * inner / INNER
    grad_gated = ssm_scale * grad_scaled - gated * pull_back
    sig = jax.nn.sigmoid(gate_raw)
    grad_mixed = (grad_gated * gate_raw * sig).astype(BF)
    grad_gate_raw = grad_gated * mixed * (sig * (1.0 + gate_raw * (1.0 - sig)))
    grad_recv = swap_cores(grad_mixed[:, LANES:])
    grad_gain = jnp.sum(grad_mixer * gated * ssm_scale, axis=0)
    mine, theirs, conv_grad, cols_grad = mixer_back(
        core, own, layer, starts, grad_mixed[:, :LANES], grad_recv
    )
    other = swap_cores(jnp.concatenate([theirs, heads_theirs], axis=1)).astype(F32)
    block = [slice(k * LANES, (k + 1) * LANES) for k in range(5)]
    if reduce_rows is not None:
        row_total = reduce_rows(grad_mamba, grad_out)
        mine = joined(mine, row_total)
    else:
        mine = joined(mine, pending)
    grad_near = jnp.concatenate(
        [
            grad_gate_raw[:, :LANES],
            mine[:, block[0]],
            mine[:, block[1]] + other[:, block[2]],
            near_heads + other[:, block[4]],
        ],
        axis=1,
    )
    grad_far = jnp.concatenate(
        [
            grad_gate_raw[:, LANES:],
            other[:, block[0]],
            mine[:, block[2]] + other[:, block[1]],
            far_heads + other[:, block[3]],
        ],
        axis=1,
    )
    grad_near, grad_far = grad_near.astype(BF), grad_far.astype(BF)
    near, far = dot_rows(own_unit, grad_near), dot_rows(own_unit, grad_far).astype(BF)
    if reduce_rows is None:
        low = joined(mixer_low, grad_near)
        grad_mamba = dot_rows(low, grad_own)
        grad_out = dot_rows(joined(attended, grad_near), grad_own)
        beside = near, far, grad_mamba, grad_out
        row_total = grad_mamba, grad_out
    else:
        beside = near, far
    grad_unit = dot_back(grad_near, layer["near"]) + dot_back(grad_far, layer["far"])
    grad_x = grad_hidden + normalize_back(unit, scale, collect(grad_unit, *beside))
    return grad_x, near, far, row_total, grad_gain, conv_grad, cols_grad


def section_pair(section, own, other):
    return jnp.where(section == 0, jnp.stack([own, other]), jnp.stack([other, own]))


def cut_in_kernel(w_ref, query_ref, key_ref, value_ref, gain_ref, conv_ref, out_ref):
    rows = w_ref.shape[0]
    gain = gain_ref[...]
    maps = 2 * INNER

    def piece(ref, at, width):
        return (ref[:, at : at + width].astype(F32) * gain).astype(BF)

    steps = piece(w_ref, maps + 2 * NS, NH)
    filler = jnp.zeros((rows, LANES - NARROW - NH), BF)
    rest = jnp.zeros((rows, LANES - 3 * HALF_HEAD), BF)
    for device in range(SHARDS):
        chip, core = device // CORES, device % CORES
        head = (chip // (CHIPS // KEY_VALUE_HEADS) * CORES + core) * HALF_HEAD
        cut = jnp.concatenate(
            [
                piece(w_ref, device * NARROW, NARROW),
                conv_ref[...],
                piece(w_ref, INNER + device * NARROW, NARROW),
                steps,
                filler,
                piece(w_ref, maps + core * NS, NS),
                piece(query_ref, device * HALF_HEAD, HALF_HEAD),
                piece(key_ref, head, HALF_HEAD),
                piece(value_ref, head, HALF_HEAD),
                rest,
            ],
            axis=1,
        )
        out_ref[device] = cut
        out_ref[SHARDS + device] = cut


def cut_wide_kernel(gate_ref, up_ref, gain_ref, out_ref):
    gain = gain_ref[...]
    for device in range(SHARDS):
        at = slice(device * FF_CORE, (device + 1) * FF_CORE)
        for k, ref in enumerate((gate_ref, up_ref)):
            cut = (ref[:, at].astype(F32) * gain).astype(BF)
            low = slice(k * FF_CORE, (k + 1) * FF_CORE)
            out_ref[device, :, low] = cut
            out_ref[SHARDS + device, :, low] = cut


def cut_call(kernel, columns, *operands):
    return pl.pallas_call(
        kernel,
        out_shape=jax.ShapeDtypeStruct((2 * SHARDS, operands[0].shape[0], columns), BF),
        in_specs=whole_vmem(len(operands)),
        out_specs=whole_vmem(1)[0],
        compiler_params=params(),
        cost_estimate=small_cost(),
    )(*operands)


def finish_kernel(in_width, total_ref, gain_ref, mid_ref, *refs):
    raw, outs, norms_ref = refs[:6], refs[6:12], refs[12]
    sums = []
    at = 0
    for k in range(6):
        width = raw[k].shape[1]
        part = slice(at, at + width)
        grad = total_ref[:, part].astype(F32)
        sums.append(jnp.sum(grad * raw[k][...].astype(F32), axis=1, keepdims=True))
        outs[k][...] = grad * (gain_ref if k < 4 else mid_ref)[...]
        at += in_width if k == 0 else width
    lane = lax.broadcasted_iota(jnp.int32, norms_ref.shape, 1)
    norm_in = sums[0] + sums[1] + sums[2] + sums[3]
    norms_ref[...] = jnp.where(lane == 0, norm_in, sums[4] + sums[5])


def finish(in_width, total, gain_in, gain_mid, raw):
    rows = total.shape[0]
    return pl.pallas_call(
        functools.partial(finish_kernel, in_width),
        out_shape=tuple(jax.ShapeDtypeStruct(w.shape, F32) for w in raw)
        + (jax.ShapeDtypeStruct((rows, LANES), F32),),
        in_specs=whole_vmem(9),
        out_specs=tuple(whole_vmem(7)),
        compiler_params=params(),
        cost_estimate=small_cost(),
    )(total, gain_in, gain_mid, *raw)


def body(
    inputs,
    cotangent,
    norm_in,
    w_in,
    conv_w,
    conv_b,
    dt_bias,
    a_log,
    skip_gain,
    norm_ssm,
    w_out,
    query_weight,
    key_weight,
    value_weight,
    output_weight,
    norm_mid,
    w_gate,
    w_up,
    w_down,
):
    place = lax.axis_index("shard")
    core = place % CORES
    core_word = core.reshape(1).astype(jnp.int32)
    section = lax.axis_index("section")
    reps = lax.axis_size("rep")
    local = inputs.shape[2]
    spare = LANES - NARROW

    gain_in = norm_in[0].astype(F32)[:, None]
    gain_mid = norm_mid[0].astype(F32)[:, None]

    own_input = lax.dynamic_index_in_dim(inputs[:, 0], section, 0, False).astype(F32)
    own_target = lax.dynamic_index_in_dim(cotangent[:, 0], section, 0, False)
    unit, scale = normalize(own_input)
    own_unit = spread(unit.astype(BF))
    conv_all = jnp.concatenate([conv_w[0], conv_b], axis=0)
    conv_count = conv_all.size
    conv_cols = jnp.concatenate(
        [conv_all.reshape(-1), jnp.zeros((spare * local - conv_count,), BF)]
    ).reshape(local, spare)
    cut = cut_call(
        cut_in_kernel,
        IN_COLS,
        w_in[0],
        query_weight[0],
        key_weight[0],
        value_weight[0],
        gain_in,
        conv_cols,
    )
    everywhere = ("section", "shard")
    met = lax.all_to_all(cut, everywhere, 0, 0, tiled=True)
    met = met.reshape(2, SHARDS, local, IN_COLS)
    conv_met = met[:, :, :, NARROW:LANES].reshape(2, SHARDS, spare * local)[:, :, :conv_count]
    conv_met = conv_met.reshape(2, SHARDS, CONV + 1, -1).transpose(0, 2, 1, 3)
    conv_met = conv_met.reshape(2, CONV + 1, INNER + 2 * NS).astype(F32)
    own_cols = met.reshape(2, SHARDS * local, IN_COLS)
    other_cols = swap_cores(own_cols)
    cut = cut_call(cut_wide_kernel, WIDE_COLS, w_gate[0], w_up[0], gain_mid)
    wide_cols = lax.all_to_all(cut, everywhere, 0, 0, tiled=True)
    wide_cols = wide_cols.reshape(2, SHARDS * local, WIDE_COLS)
    other_wide = swap_cores(wide_cols)

    def both_layers(own):
        return section_pair(section, own, swap_sections(own))

    raw_rows = jnp.concatenate([w_out[0], output_weight[0], w_down[0]], axis=0)
    raw_rows = joined(raw_rows, met)
    sent_rows = swap_sections(raw_rows)
    row_store = {}

    def rows_at(layer):
        def make(token):
            if not row_store:
                rows = section_pair(section, raw_rows, joined(sent_rows, token))
                row_store["pair"] = rows, swap_cores(rows)
            rows, others = (x[layer] for x in row_store["pair"])
            return {
                "mamba": jnp.concatenate([rows[:out_row], no_rows, others[:out_row], no_rows]),
                "out": jnp.concatenate([rows[out_row:down_row], others[out_row:down_row]]),
                "down": jnp.concatenate([rows[down_row:], others[down_row:]]),
            }

        return make

    out_row, down_row = NARROW, NARROW + HALF_HEAD
    per_head = jnp.concatenate([dt_bias[0], a_log[0], skip_gain[0], norm_ssm[0].astype(F32)])
    per_head = both_layers(per_head)
    own_gain = per_head[:, 3 * NH :]
    other_gain = swap_cores(own_gain)
    lane = lax.broadcasted_iota(jnp.int32, (NH, LANES), 1)
    head_of = jnp.where(lane < NARROW, (lane + place * NARROW) // HD, -1)
    member = (head_of == lax.broadcasted_iota(jnp.int32, (NH, LANES), 0)).astype(F32)
    sel = jnp.concatenate(
        [jnp.zeros((NARROW, LANES), F32), member, jnp.zeros((LANES - NARROW - NH, LANES), F32)]
    ).astype(BF)
    in_first = (head_of[0:1] == head_of[0:1, 0:1]).astype(F32)
    in_second = (head_of[0:1] == head_of[0:1, NARROW - 1 : NARROW]).astype(F32)

    def to_columns(values):
        return jnp.sum(values[:, None] * member, axis=0, keepdims=True)

    def padded(g):
        return jnp.concatenate([g, jnp.zeros((spare,), F32)])

    no_rows = jnp.zeros((spare, MODEL_WIDTH), BF)
    layers = []
    for layer in range(2):
        head_values = per_head[layer]
        cols = jnp.concatenate(
            [
                to_columns(head_values[:NH]),
                to_columns(jnp.exp(head_values[NH : 2 * NH])),
                to_columns(head_values[2 * NH : 3 * NH]),
                in_first,
                in_second,
                jnp.zeros((3, LANES), F32),
            ]
        )
        conv_own = jnp.concatenate(
            [
                lax.dynamic_slice_in_dim(conv_met[layer], place * NARROW, NARROW, axis=1),
                jnp.zeros((CONV + 1, spare), F32),
                by_place(core, conv_met[layer, :, INNER : INNER + NS], conv_met[layer, :, INNER + NS :], 1),
            ],
            axis=1,
        )
        layers.append(
            {
                "near": own_cols[layer],
                "far": other_cols[layer],
                "wide": wide_cols[layer],
                "wide_far": other_wide[layer],
                "conv": jnp.concatenate([conv_own, jnp.zeros((7 - CONV, CONVED), F32)]),
                "cols": cols,
                "sel": sel,
                "gain": jnp.concatenate([padded(own_gain[layer]), padded(other_gain[layer])])[None],
            }
        )

    x = own_input
    outs = []
    target_own = None
    kept_mixer, kept_wide, row_weights = [], [], []
    for layer in range(2):
        if layer == 1:
            unit, scale = normalize(x)
            own_unit = spread(unit.astype(BF))
        hidden, kept, rows = forward_mixer(
            x, unit, scale, own_unit, layers[layer], core_word, target_own, rows_at(layer)
        )
        if layer == 0:
            target_own = gather_later(joined(own_target, hidden))
        row_weights.append(rows)
        kept_mixer.append(kept)
        partial, kept = forward_wide(hidden, layers[layer], rows)
        kept_wide.append(kept)
        total = collect(partial) if layer == 0 else collect_later(partial)
        outs.append((hidden + total).astype(BF))
        x = outs[layer].astype(F32)

    def exchanged(first, second):
        own = jnp.where(section == 0, first, second)
        other = swap_sections(jnp.where(section == 0, second, first).astype(BF))
        return section_pair(section, own, other.astype(own.dtype))

    part = local // reps

    def by_parts(columns):
        cut = columns.reshape(SHARDS, reps, part, columns.shape[1])
        return cut.transpose(1, 0, 2, 3).reshape(reps * SHARDS, part, columns.shape[1])

    def over_all(sent):
        met = lax.all_to_all(sent, ("section", "rep", "shard"), 0, 0, tiled=True)
        met = met.reshape(2 * reps, SHARDS, part, sent.shape[2])
        return jnp.sum(met.astype(F32), axis=0)

    extra_width = -(-(conv_count + NARROW + 3 * NH) // (reps * part))
    in_width = -(-(2 * INNER + 2 * NS + NH + extra_width) // LANES) * LANES

    def to_all(rows, axes, count):
        copies = jnp.broadcast_to(rows[None], (count,) + rows.shape)
        met = lax.all_to_all(copies, axes, 0, 0, tiled=True)
        return met.reshape(count * rows.shape[0], rows.shape[1])

    def even(g):
        return g.transpose(1, 0, 2).reshape(part, -1)

    def by_key_head(g):
        groups = CHIPS // KEY_VALUE_HEADS
        g = jnp.sum(g.reshape(KEY_VALUE_HEADS, groups, CORES, part, -1), axis=1)
        return even(g.reshape(KEY_VALUE_HEADS * CORES, part, -1))

    def by_weight(total):
        maps = total[:, :, 2 * LANES : 3 * LANES].reshape(CHIPS, CORES, part, LANES)
        heads = [
            total[:, :, 3 * LANES + k * HALF_HEAD : 3 * LANES + (k + 1) * HALF_HEAD]
            for k in range(3)
        ]
        columns = [
            even(total[:, :, :NARROW]),
            even(total[:, :, LANES : LANES + NARROW]),
            even(jnp.sum(maps, axis=0)),
            jnp.sum(total[:, :, LANES + NARROW : LANES + NARROW + NH], axis=0),
            jnp.sum(total[:, :, NARROW : NARROW + extra_width], axis=0),
            jnp.zeros((part, in_width - 2 * INNER - 2 * NS - NH - extra_width), F32),
            even(heads[0]),
            by_key_head(heads[1]),
            by_key_head(heads[2]),
            even(total[:, :, IN_COLS : IN_COLS + FF_CORE]),
            even(total[:, :, IN_COLS + FF_CORE :]),
        ]
        return jnp.concatenate(columns, axis=1).astype(BF)

    def pair_total(near, far):
        return (near + swap_cores(far).astype(F32)).astype(BF)

    def small_parts(grad_gain, conv_grad, cols_grad):
        conv_grad = conv_grad[: CONV + 1]
        maps_grad = by_place(core, conv_grad[:, LANES : 2 * LANES], conv_grad[:, 2 * LANES :], 1)
        conv_grad = jnp.concatenate(
            [
                lax.dynamic_update_slice_in_dim(
                    jnp.zeros((CONV + 1, INNER), F32), conv_grad[:, :NARROW], place * NARROW, axis=1
                ),
                maps_grad,
            ],
            axis=1,
        )
        conv_grad = conv_grad.reshape(CONV + 1, SHARDS, -1).transpose(1, 0, 2).reshape(SHARDS, -1)
        gain_halves = by_place(core, grad_gain[:NARROW], grad_gain[LANES : LANES + NARROW], 0)
        gain_grad = lax.dynamic_update_slice_in_dim(
            jnp.zeros((INNER,), F32), gain_halves, (place // CORES) * CORES * NARROW, axis=0
        ).reshape(SHARDS, -1)
        head_grad = jnp.sum(cols_grad[:3, None, :] * member[None], axis=2).reshape(1, -1)
        extra = jnp.concatenate(
            [conv_grad, gain_grad, jnp.broadcast_to(head_grad, (SHARDS, 3 * NH))], axis=1
        )
        width = -(-extra.shape[1] // (reps * part))
        missing = reps * part * width - extra.shape[1]
        extra = jnp.concatenate([extra, jnp.zeros((SHARDS, missing), F32)], axis=1)
        extra = extra.reshape(SHARDS, reps, part, width).transpose(1, 0, 2, 3)
        return extra.reshape(reps * SHARDS, part, width).astype(BF)

    def with_small(sent, extra):
        room = spare - extra.shape[2]
        extra = jnp.pad(extra, ((0, 0), (0, 0), (0, room)))
        return jnp.concatenate([sent[:, :, :NARROW], extra, sent[:, :, LANES:]], axis=2)

    def rows_of(grad_mamba, grad_out, grad_down):
        mine = jnp.concatenate([grad_mamba[:NARROW], grad_out[:HALF_HEAD], grad_down[:FF_CORE]])
        theirs = jnp.concatenate(
            [grad_mamba[LANES : LANES + NARROW], grad_out[HALF_HEAD:], grad_down[FF_CORE:]]
        )
        return pair_total(mine, theirs.astype(BF))

    def reduce_rows(grad_mamba, grad_out):
        first_rows = rows_of(grad_mamba, grad_out, grad_down)
        met = lax.all_to_all(
            jnp.concatenate([first_rows, last_rows]), ("section", "rep"), 0, 0, tiled=True
        )
        return met

    sent = [None, None]
    grad = own_target.astype(F32)
    input_grads = [None, None]
    for layer in (1, 0):
        grad_own = target_own if layer == 1 else spread(grad.astype(BF))
        grad_hidden, grad_wide, grad_wide_far, grad_down = backward_wide(
            grad, grad_own, kept_wide[layer], layers[layer], row_weights[layer]
        )
        grad_x, grad_near, grad_far, row_total, *small = backward_mixer(
            grad_hidden,
            kept_mixer[layer],
            layers[layer],
            row_weights[layer],
            core_word,
            reduce_rows if layer == 0 else None,
            total,
        )
        if layer == 1:
            last_rows = rows_of(*row_total, grad_down)
        input_grads[layer] = grad_x
        grad = grad_x.astype(BF).astype(F32)
        columns = [pair_total(grad_near, grad_far), pair_total(grad_wide, grad_wide_far)]
        columns = jnp.concatenate(columns, axis=1)
        sent[layer] = with_small(by_parts(columns), small_parts(*small))

    section_out = exchanged(outs[0], joined(outs[1], grad_near))[None, :, None]
    input_grad = exchanged(*input_grads)[None, :, None]
    row_total = row_total.reshape(2 * reps, -1, MODEL_WIDTH).astype(F32)
    row_total = jnp.sum(row_total, axis=0).astype(BF)
    columns = by_weight(over_all(jnp.concatenate(sent)))
    totals = to_all(jnp.concatenate([columns, row_total.reshape(part, -1)], axis=1), "rep", reps)
    columns = totals[:, : columns.shape[1]]
    row_total = totals[:, columns.shape[1] :].reshape(-1, MODEL_WIDTH).astype(F32)
    used = 2 * INNER + 2 * NS + NH
    extra = columns[:, used : used + extra_width].astype(F32).reshape(-1)
    conv_total = extra[:conv_count].reshape(CONV + 1, -1)
    gain_total = extra[conv_count : conv_count + NARROW]
    head_total = extra[conv_count + NARROW : conv_count + NARROW + 3 * NH].reshape(3, NH)
    raw = [w[0] for w in (w_in, query_weight, key_weight, value_weight, w_gate, w_up)]
    *by_rows, norms = finish(in_width, totals, gain_in, gain_mid, raw)
    grad_norm_in, grad_norm_mid = norms[:, 0], norms[:, 1]
    return (
        section_out,
        input_grad,
        grad_norm_in[None],
        by_rows[0][None],
        conv_total[:CONV][None],
        conv_total[CONV][None],
        head_total[0][None],
        head_total[1][None],
        head_total[2][None],
        gain_total[None],
        row_total[:out_row][None],
        by_rows[1][None],
        by_rows[2][None],
        by_rows[3][None],
        row_total[out_row:down_row][None],
        grad_norm_mid[None],
        by_rows[4][None],
        by_rows[5][None],
        row_total[down_row:][None],
    )


def solution(mesh):
    return jax.shard_map(
        body,
        mesh=mesh,
        in_specs=(
            P(None, "rep", "shard", None),
            P(None, "rep", "shard", None),
            P("section", "shard"),
            P("section", "shard", None),
            P("section", None, "shard"),
            P("section", "shard"),
            P("section", None),
            P("section", None),
            P("section", None),
            P("section", "shard"),
            P("section", "shard", None),
            P("section", "shard", None),
            P("section", "shard", None),
            P("section", "shard", None),
            P("section", "shard", None),
            P("section", "shard"),
            P("section", "shard", None),
            P("section", "shard", None),
            P("section", "shard", None),
        ),
        out_specs=(
            P("section", None, "rep", "shard", None),
            P("section", None, "rep", "shard", None),
            P("section", "shard"),
            P("section", "shard", None),
            P("section", None, "shard"),
            P("section", "shard"),
            P("section", None),
            P("section", None),
            P("section", None),
            P("section", "shard"),
            P("section", "shard", None),
            P("section", "shard", None),
            P("section", "shard", None),
            P("section", "shard", None),
            P("section", "shard", None),
            P("section", "shard"),
            P("section", "shard", None),
            P("section", "shard", None),
            P("section", "shard", None),
        ),
        check_vma=False,
    )
```

```python
import functools

import jax
import jax.numpy as jnp
from jax import lax
from jax.experimental import pallas as pl
from jax.experimental.pallas import tpu as pltpu
from jax.sharding import PartitionSpec as P

MODEL_WIDTH = 1024
NH = 24
HD = 64
NS = 128
QUERY_HEADS = 8
KEY_VALUE_HEADS = 2
ATTN_HEAD_SIZE = 64
FF = 2048
CONV = 4
MB = 2

EPSILON = 1e-05

SHARDS = 16
CORES = 2
CHIPS = SHARDS // CORES
INNER = NH * HD
NARROW = INNER // SHARDS
LANES = 128
HALF_HEAD = ATTN_HEAD_SIZE // 2
IN_COLS = 4 * LANES
WIDE_COLS = 2 * LANES
CONVED = 3 * LANES
CHUNK = 128
BLOCK = 64
FF_CORE = FF // SHARDS
RATIO = ATTN_HEAD_SIZE ** (-0.5)

BF = jnp.bfloat16
F32 = jnp.float32


def dot_plain(former, latter):
    return jnp.dot(former, latter, preferred_element_type=F32)


def dot_rows(former, latter):
    return lax.dot_general(former, latter, (((0,), (0,)), ((), ())), preferred_element_type=F32)


def dot_back(former, latter):
    return lax.dot_general(former, latter, (((1,), (1,)), ((), ())), preferred_element_type=F32)


def exact(former, latter, dims):
    return lax.dot_general(
        former,
        latter,
        ((dims[:1], dims[1:]), ((), ())),
        precision=lax.Precision.HIGHEST,
        preferred_element_type=F32,
    )


def swap_cores(x):
    return lax.ppermute(x, "shard", [(i, i ^ 1) for i in range(SHARDS)])


def swap_sections(x):
    return lax.ppermute(x, "section", [(0, 1), (1, 0)])


def same_core():
    return [list(range(core, SHARDS, CORES)) for core in range(CORES)]


def joined(x, *met):
    zero = sum((m[(0,) * m.ndim] * 0).astype(F32) for m in met)
    return x + zero.astype(x.dtype)


def spread(rows):
    count, width = rows.shape
    copies = jnp.broadcast_to(rows[None], (CHIPS, count, width)).reshape(CHIPS * count, width)
    return lax.all_to_all(copies, "shard", 0, 0, axis_index_groups=same_core(), tiled=True)


def collect(partial, *beside):
    rows = partial.shape[0] // CHIPS
    met = lax.all_to_all(
        partial.astype(BF), "shard", 0, 0, axis_index_groups=same_core(), tiled=True
    )
    total = jnp.sum(met.reshape(CHIPS, rows, partial.shape[1]).astype(F32), axis=0)
    return joined(total, *beside) if beside else total


def chip_sums(x, *beside):
    ones = jnp.ones((8, x.shape[1]), F32)
    sums = exact(ones, x, (1, 1))
    copies = jnp.broadcast_to(sums[None], (CHIPS,) + sums.shape).reshape(8 * CHIPS, -1)
    met = lax.all_to_all(copies, "shard", 0, 0, axis_index_groups=same_core(), tiled=True)
    share = joined(jnp.full((8 * CHIPS, LANES), 0.125, F32), *beside)
    return exact(met, share, (0, 0))[:, :1]


def by_place(core, own, other, axis):
    return jnp.where(
        core == 0,
        jnp.concatenate([own, other], axis=axis),
        jnp.concatenate([other, own], axis=axis),
    )


def normalize(x):
    scale = lax.rsqrt(jnp.mean(x * x, axis=-1, keepdims=True) + EPSILON)
    return x * scale, scale


def normalize_back(unit, scale, grad):
    return scale * (grad - unit * jnp.mean(grad * unit, axis=-1, keepdims=True))


def whole_vmem(count):
    return [pl.BlockSpec(memory_space=pltpu.VMEM)] * count


def scalar_first(count):
    return [pl.BlockSpec(memory_space=pltpu.SMEM)] + whole_vmem(count)


def params():
    return pltpu.CompilerParams(vmem_limit_bytes=48 * 2**20)


def small_cost():
    return pl.CostEstimate(flops=10**6, bytes_accessed=10**4, transcendentals=0)


def softplus(v):
    return jnp.maximum(v, 0.0) + jnp.log1p(jnp.exp(-jnp.abs(v)))


def row_parts(refs, at):
    states, first, second = refs
    parts = [ref[at, low : low + LANES] for ref, low in (states, first, second)]
    return jnp.concatenate(parts, axis=1).astype(F32)


def sources(near_ref, maps_ref, far_ref, recv_maps_ref, recv_far_ref):
    own = ((near_ref, LANES), (maps_ref, 0), (far_ref, 2 * LANES))
    recv = ((recv_far_ref, LANES), (recv_far_ref, 2 * LANES), (recv_maps_ref, 0))
    return own, recv


def chunk_rows(core, own_refs, recv_refs, k):
    at = pl.ds(pl.multiple_of(k * BLOCK, BLOCK), BLOCK)
    own = row_parts(own_refs, at)
    recv = row_parts(recv_refs, at)
    return jnp.where(core == 0, own, recv), jnp.where(core == 0, recv, own)


def chunk_parts(core, ext, conv_ref, cols_ref, sel_ref):
    conv = conv_ref[CONV : CONV + 1, :]
    for j in range(CONV):
        start = 8 - (CONV - 1) + j
        conv = conv + conv_ref[j : j + 1, :] * ext[start : start + CHUNK, :]
    sig = 1.0 / (1.0 + jnp.exp(-conv))
    activated = conv * sig
    states_in = activated[:, 0:LANES]
    first, second = activated[:, LANES : 2 * LANES], activated[:, 2 * LANES :]
    input_map = jnp.where(core == 0, first, second)
    output_map = jnp.where(core == 0, second, first)
    raw = dot_plain(ext[8 : 8 + CHUNK, 0:LANES].astype(BF), sel_ref[...]) + cols_ref[0:1, :]
    step = softplus(raw)
    log_decay = -step * cols_ref[1:2, :]
    rows = lax.broadcasted_iota(jnp.int32, (CHUNK, CHUNK), 0)
    cols = lax.broadcasted_iota(jnp.int32, (CHUNK, CHUNK), 1)
    causal = cols <= rows
    lower = jnp.where(causal, 1.0, 0.0)
    cumulative = exact(lower, log_decay, (1, 0))
    turned = exact(log_decay, lower, (0, 1))
    weighted = states_in * step
    coupling = dot_back(output_map.astype(BF), input_map.astype(BF))
    within = []
    for lane in (0, NARROW - 1):
        gap = cumulative[:, lane : lane + 1] - turned[lane : lane + 1, :]
        within.append(jnp.where(causal, jnp.exp(jnp.where(causal, gap, 0.0)), 0.0))
    last = cumulative[CHUNK - 1 : CHUNK, :]
    tail = jnp.exp(last - cumulative)
    decay = jnp.exp(turned[:, CHUNK - 1 : CHUNK])
    return (
        conv,
        sig,
        states_in,
        input_map.astype(BF),
        output_map.astype(BF),
        raw,
        step,
        log_decay,
        lower,
        cumulative,
        weighted,
        coupling,
        within,
        last,
        tail,
        decay,
    )


def mixer_kernel(
    core_ref,
    near_ref,
    maps_ref,
    far_ref,
    recv_maps_ref,
    recv_far_ref,
    conv_ref,
    cols_ref,
    sel_ref,
    mine_ref,
    theirs_ref,
    starts_ref,
    ext,
):
    core = core_ref[0]
    own_refs, recv_refs = sources(near_ref, maps_ref, far_ref, recv_maps_ref, recv_far_ref)
    ext[0:8, :] = jnp.zeros((8, CONVED), F32)

    def chunk(k, state):
        first, second = chunk_rows(core, own_refs, recv_refs, k)
        ext[8 : 8 + BLOCK, :] = first
        ext[8 + BLOCK : 8 + CHUNK, :] = second
        (
            conv,
            sig,
            states_in,
            input_map,
            output_map,
            raw,
            step,
            log_decay,
            lower,
            cumulative,
            weighted,
            coupling,
            within,
            last,
            tail,
            decay,
        ) = chunk_parts(core, ext, conv_ref, cols_ref, sel_ref)
        starts_ref[k] = state
        mixed = dot_back(output_map, state.astype(BF)) * jnp.exp(cumulative)
        mixed = mixed + cols_ref[2:3, :] * states_in
        for head in range(2):
            mixed = mixed + dot_plain(
                (within[head] * coupling).astype(BF),
                (weighted * cols_ref[3 + head : 4 + head, :]).astype(BF),
            )
        state = decay * state + dot_rows((weighted * tail).astype(BF), input_map)
        at = pl.ds(pl.multiple_of(k * BLOCK, BLOCK), BLOCK)
        low, high = mixed[:BLOCK, :], mixed[BLOCK:, :]
        mine_ref[at, :] = jnp.where(core == 0, low, high).astype(BF)
        theirs_ref[at, :] = jnp.where(core == 0, high, low).astype(BF)
        ext[0:8, :] = ext[CHUNK : CHUNK + 8, :]
        return state

    lax.fori_loop(0, CHIPS, chunk, jnp.zeros((LANES, NS), F32), unroll=4)


def anywhere(count):
    return [pl.BlockSpec(memory_space=pl.ANY)] * count


def mixer(core, own, layer):
    rows = own[0].shape[0]
    return pl.pallas_call(
        mixer_kernel,
        out_shape=(
            jax.ShapeDtypeStruct((rows, LANES), BF),
            jax.ShapeDtypeStruct((rows, LANES), BF),
            jax.ShapeDtypeStruct((CHIPS, LANES, NS), F32),
        ),
        in_specs=scalar_first(8),
        out_specs=tuple(whole_vmem(3)),
        scratch_shapes=[pltpu.VMEM((CHUNK + 8, CONVED), F32)],
        compiler_params=params(),
        cost_estimate=small_cost(),
    )(core, *own, layer["conv"], layer["cols"], layer["sel"])


def mixer_back_kernel(
    core_ref,
    near_ref,
    maps_ref,
    far_ref,
    recv_maps_ref,
    recv_far_ref,
    conv_ref,
    cols_ref,
    sel_ref,
    starts_ref,
    grad_own_ref,
    grad_recv_ref,
    *refs,
):
    mine_ref, theirs_ref, conv_grad_ref, cols_grad_ref, ext, later = refs[-6:]
    core = core_ref[0]
    own_refs, recv_refs = sources(near_ref, maps_ref, far_ref, recv_maps_ref, recv_far_ref)
    later[...] = jnp.zeros((CHUNK + 8, CONVED), F32)
    conv_grad_ref[...] = jnp.zeros((8, CONVED), F32)
    cols_grad_ref[...] = jnp.zeros((8, LANES), F32)
    ones = jnp.ones((CHUNK, LANES), BF)
    lanes = lax.broadcasted_iota(jnp.int32, (CHUNK, LANES), 1)

    def chunk(turn, grad_state):
        k = CHIPS - 1 - turn
        first, second = chunk_rows(core, own_refs, recv_refs, k)
        ext[8 : 8 + BLOCK, :] = first
        ext[8 + BLOCK : 8 + CHUNK, :] = second
        before = jnp.maximum(k - 1, 0)
        at_end = pl.ds(pl.multiple_of(before * BLOCK + BLOCK - 16, 16), 16)
        own_end = row_parts(own_refs, at_end)
        recv_end = row_parts(recv_refs, at_end)
        end = jnp.where(core == 0, recv_end, own_end)[8:16, :]
        ext[0:8, :] = jnp.where(k > 0, end, 0.0)
        (
            conv,
            sig,
            states_in,
            input_map,
            output_map,
            raw,
            step,
            log_decay,
            lower,
            cumulative,
            weighted,
            coupling,
            within,
            last,
            tail,
            decay,
        ) = chunk_parts(core, ext, conv_ref, cols_ref, sel_ref)
        start = starts_ref[k]
        start_low = start.astype(BF)
        at = pl.ds(pl.multiple_of(k * BLOCK, BLOCK), BLOCK)
        grad_mine = grad_own_ref[at, :].astype(F32)
        grad_theirs = grad_recv_ref[at, :].astype(F32)
        grad = jnp.concatenate(
            [
                jnp.where(core == 0, grad_mine, grad_theirs),
                jnp.where(core == 0, grad_theirs, grad_mine),
            ],
            axis=0,
        )
        grad_states = cols_ref[2:3, :] * grad
        grad_skip = jnp.sum(grad * states_in, axis=0, keepdims=True)
        grown = grad * jnp.exp(cumulative)
        grown_low = grown.astype(BF)
        grad_out_map = dot_plain(grown_low, start_low)
        grad_start = dot_rows(grown_low, output_map)
        grad_cum = grown * dot_back(output_map, start_low)
        grad_coupling = jnp.zeros((CHUNK, CHUNK), F32)
        grad_weighted = jnp.zeros((CHUNK, LANES), F32)
        for head in range(2):
            member = cols_ref[3 + head : 4 + head, :]
            grad_head = (grad * member).astype(BF)
            grad_mixing = dot_back(grad_head, weighted.astype(BF))
            mixing = within[head] * coupling
            grad_weighted = grad_weighted + dot_rows(mixing.astype(BF), grad_head)
            grad_coupling = grad_coupling + grad_mixing * within[head]
            pairs = (grad_mixing * mixing).astype(BF)
            change = dot_plain(pairs, ones) - dot_rows(pairs, ones)
            grad_cum = grad_cum + jnp.where(lanes == head * (NARROW - 1), change, 0.0)
        coupling_low = grad_coupling.astype(BF)
        grad_out_map = grad_out_map + dot_plain(coupling_low, input_map)
        grad_in_map = dot_rows(coupling_low, output_map)
        state_low = grad_state.astype(BF)
        tailed = weighted * tail
        grad_in_map = grad_in_map + dot_plain(tailed.astype(BF), state_low)
        reach = dot_back(input_map, state_low)
        grad_weighted = grad_weighted + reach * tail
        moved = reach * tailed
        grad_cum = grad_cum - moved
        kept = exact(jnp.ones((8, NS), F32), grad_state * start, (1, 1))[0:1, :]
        grad_last = jnp.sum(moved, axis=0, keepdims=True) + kept * jnp.exp(last)
        grad_log = exact(lower, grad_cum, (0, 0)) + grad_last
        grad_step = grad_weighted * states_in - cols_ref[1:2, :] * grad_log
        grad_states = grad_states + grad_weighted * step
        grad_raw = grad_step / (1.0 + jnp.exp(-raw))
        cols_grad_ref[0:1, :] += jnp.sum(grad_raw, axis=0, keepdims=True)
        cols_grad_ref[1:2, :] += jnp.sum(grad_log * log_decay, axis=0, keepdims=True)
        cols_grad_ref[2:3, :] += grad_skip
        grad_dt = exact(grad_raw, sel_ref[...].astype(F32), (1, 1))
        slope = sig * (1.0 + conv * (1.0 - sig))
        grad_first = jnp.where(core == 0, grad_in_map, grad_out_map)
        grad_second = jnp.where(core == 0, grad_out_map, grad_in_map)
        grad_conv = jnp.concatenate([grad_states, grad_first, grad_second], axis=1) * slope
        later[CHUNK : CHUNK + 8, :] = later[0:8, :]
        later[0:CHUNK, :] = grad_conv
        conv_grad_ref[CONV : CONV + 1, :] += jnp.sum(grad_conv, axis=0, keepdims=True)
        grad_in = jnp.zeros((CHUNK, CONVED), F32)
        for j in range(CONV):
            low = 8 - (CONV - 1) + j
            conv_grad_ref[j : j + 1, :] += jnp.sum(
                grad_conv * ext[low : low + CHUNK, :], axis=0, keepdims=True
            )
            ahead = CONV - 1 - j
            grad_in = grad_in + conv_ref[j : j + 1, :] * later[ahead : ahead + CHUNK, :]
        grad_in = jnp.concatenate([grad_in[:, 0:LANES] + grad_dt, grad_in[:, LANES:]], axis=1)
        low, high = grad_in[:BLOCK, :], grad_in[BLOCK:, :]
        mine_ref[at, :] = jnp.where(core == 0, low, high)
        theirs_ref[at, :] = jnp.where(core == 0, high, low).astype(BF)
        return decay * grad_state + grad_start

    lax.fori_loop(0, CHIPS, chunk, jnp.zeros((LANES, NS), F32), unroll=4)


def mixer_back(core, own, layer, starts, grad_own, grad_recv):
    rows = own[0].shape[0]
    return pl.pallas_call(
        mixer_back_kernel,
        out_shape=(
            jax.ShapeDtypeStruct((rows, CONVED), F32),
            jax.ShapeDtypeStruct((rows, CONVED), BF),
            jax.ShapeDtypeStruct((8, CONVED), F32),
            jax.ShapeDtypeStruct((8, LANES), F32),
        ),
        in_specs=scalar_first(11),
        out_specs=tuple(whole_vmem(4)),
        scratch_shapes=[pltpu.VMEM((CHUNK + 8, CONVED), F32)] * 2,
        compiler_params=params(),
        cost_estimate=small_cost(),
    )(core, *own, layer["conv"], layer["cols"], layer["sel"], starts, grad_own, grad_recv)


def seen(core, part, rows, columns):
    row = lax.broadcasted_iota(jnp.int32, (rows, columns), 0) + part * rows
    col = lax.broadcasted_iota(jnp.int32, (rows, columns), 1)
    half = columns // 2
    query_at = (row // BLOCK * 2 + core) * BLOCK + row % BLOCK
    other = col // half
    key = col - other * half
    key_at = (key // BLOCK * 2 + jnp.where(other == 0, core, 1 - core)) * BLOCK + key % BLOCK
    return key_at <= query_at


def head_part(near, far, part):
    at = slice(part * HALF_HEAD, (part + 1) * HALF_HEAD)
    return jnp.concatenate([near[:, at], far[:, at]], axis=1)


def heads_of(maps_ref, far_ref, recv_maps_ref, recv_far_ref):
    near, far = maps_ref[:, LANES:], far_ref[:, 3 * LANES :]
    recv_near, recv_far = recv_far_ref[:, 3 * LANES :], recv_maps_ref[:, LANES:]
    keys, values = (
        jnp.concatenate([head_part(near, far, k), head_part(recv_near, recv_far, k)], axis=0)
        for k in (1, 2)
    )
    return head_part(near, far, 0), keys, values


def attend_kernel(
    core_ref, maps_ref, far_ref, recv_maps_ref, recv_far_ref, also_ref, out_ref, stat_ref
):
    core = core_ref[0]
    queries, keys, values = heads_of(maps_ref, far_ref, recv_maps_ref, recv_far_ref)
    for part in range(maps_ref.shape[0] // CHUNK):
        at = slice(part * CHUNK, (part + 1) * CHUNK)
        scores = dot_back(queries[at], keys) * RATIO
        scores = jnp.where(seen(core, part, *scores.shape), scores, -1e30)
        top = jnp.max(scores, axis=1, keepdims=True)
        grown = jnp.exp(scores - top)
        total = jnp.sum(grown, axis=1, keepdims=True)
        soft = grown / total
        out_ref[at, :] = dot_plain(soft.astype(BF), values).astype(BF)
        stat_ref[at, :] = jnp.broadcast_to(top + jnp.log(total), (CHUNK, LANES))


def attend(core, own, also):
    rows = own[0].shape[0]
    return pl.pallas_call(
        attend_kernel,
        out_shape=(
            jax.ShapeDtypeStruct((rows, ATTN_HEAD_SIZE), BF),
            jax.ShapeDtypeStruct((rows, LANES), F32),
        ),
        in_specs=scalar_first(4) + anywhere(1),
        out_specs=tuple(whole_vmem(2)),
        compiler_params=params(),
        cost_estimate=small_cost(),
    )(core, *own[1:], also)


def attend_back_kernel(
    core_ref,
    maps_ref,
    far_ref,
    recv_maps_ref,
    recv_far_ref,
    stat_ref,
    grad_ref,
    *refs,
):
    near_grad_ref, far_grad_ref, theirs_ref, total, query_total = refs[-5:]
    core = core_ref[0]
    queries, keys, values = heads_of(maps_ref, far_ref, recv_maps_ref, recv_far_ref)
    total[...] = jnp.zeros(total.shape, F32)
    half = maps_ref.shape[0]
    for part in range(half // CHUNK):
        at = slice(part * CHUNK, (part + 1) * CHUNK)
        query = queries[at]
        grad = grad_ref[at, :]
        scores = dot_back(query, keys) * RATIO
        visible = seen(core, part, *scores.shape)
        soft = jnp.where(visible, jnp.exp(scores - stat_ref[at, 0:1]), 0.0)
        grad_soft = dot_back(grad, values)
        row_total = jnp.sum(soft * grad_soft, axis=1, keepdims=True)
        grad_scores = (soft * (grad_soft - row_total)).astype(BF)
        query_total[at, :] = dot_plain(grad_scores, keys) * RATIO
        key_grad = dot_rows(grad_scores, query) * RATIO
        value_grad = dot_rows(soft.astype(BF), grad)
        total[...] += jnp.concatenate([key_grad, value_grad], axis=1)
    empty = jnp.zeros((half, HALF_HEAD), F32)
    mine, theirs = total[:half, :], total[half:, :]

    def cut(x, at):
        return x[:, at * HALF_HEAD : (at + 1) * HALF_HEAD]

    query = query_total[...]
    near_grad_ref[...] = jnp.concatenate([cut(query, 0), cut(mine, 0), cut(mine, 2), empty], axis=1)
    far_grad_ref[...] = jnp.concatenate([cut(query, 1), cut(mine, 1), cut(mine, 3), empty], axis=1)
    theirs_ref[:, :LANES] = jnp.concatenate(
        [empty, cut(theirs, 0), cut(theirs, 2), empty], axis=1
    ).astype(BF)
    theirs_ref[:, LANES:] = jnp.concatenate(
        [empty, cut(theirs, 1), cut(theirs, 3), empty], axis=1
    ).astype(BF)


def attend_back(core, own, stat, grad):
    rows = own[0].shape[0]
    return pl.pallas_call(
        attend_back_kernel,
        out_shape=(
            jax.ShapeDtypeStruct((rows, LANES), F32),
            jax.ShapeDtypeStruct((rows, LANES), F32),
            jax.ShapeDtypeStruct((rows, 2 * LANES), BF),
        ),
        in_specs=scalar_first(6),
        out_specs=tuple(whole_vmem(3)),
        scratch_shapes=[
            pltpu.VMEM((2 * rows, LANES), F32),
            pltpu.VMEM((rows, ATTN_HEAD_SIZE), F32),
        ],
        compiler_params=params(),
        cost_estimate=small_cost(),
    )(core, *own[1:], stat, grad)


def gather_later(rows):
    return lax.all_gather(rows, "shard", axis=0, tiled=True, axis_index_groups=same_core())


def collect_later(partial):
    return lax.psum_scatter(
        partial.astype(BF),
        "shard",
        scatter_dimension=0,
        tiled=True,
        axis_index_groups=same_core(),
    ).astype(F32)


def forward_mixer(x, unit, scale, own_unit, layer, core, also, row_weights):
    far = dot_plain(own_unit, layer["far"]).astype(BF)
    maps = dot_plain(own_unit, layer["near"][:, 2 * LANES :]).astype(BF)
    near = dot_plain(own_unit, layer["near"][:, : 2 * LANES]).astype(BF)
    own = (near, maps, far, swap_cores(maps), swap_cores(far))
    gate_raw = jnp.concatenate([near[:, :LANES], far[:, :LANES]], axis=1).astype(F32)
    mine, theirs, starts = mixer(core, own, layer)
    mixed = jnp.concatenate([mine, swap_cores(theirs)], axis=1).astype(F32)
    gated = mixed * jax.nn.silu(gate_raw)
    attended, stat = attend(core, own, own[0])
    rows = row_weights(mine)
    squares = joined(gated * gated, layer["wide"])
    ssm_scale = lax.rsqrt(chip_sums(squares, attended) / INNER + EPSILON)
    mixer_low = (gated * ssm_scale * layer["gain"]).astype(BF)
    partial = dot_plain(mixer_low, rows["mamba"]) + dot_plain(attended, rows["out"])
    hidden = x + collect(partial, *also)
    kept = (
        unit,
        scale,
        own_unit,
        own,
        gate_raw,
        attended,
        stat,
        starts,
        mixed,
        gated,
        mixer_low,
        ssm_scale,
    )
    return hidden, kept, rows


def forward_wide(hidden, layer, rows):
    unit, scale = normalize(hidden)
    own_unit = spread(unit.astype(BF))
    near = dot_plain(own_unit, layer["wide"])
    far = dot_plain(own_unit, layer["wide_far"])
    gate_val = jnp.concatenate([near[:, :FF_CORE], far[:, :FF_CORE]], axis=1)
    up_val = jnp.concatenate([near[:, FF_CORE:], far[:, FF_CORE:]], axis=1)
    swish = (jax.nn.silu(gate_val) * up_val).astype(BF)
    return dot_plain(swish, rows["down"]), (unit, scale, own_unit, gate_val, up_val, swish)


def backward_wide(grad_out, grad_out_own, kept, layer, rows):
    unit, scale, own_unit, gate_val, up_val, swish = kept
    grad_swish = dot_back(grad_out_own, rows["down"])
    sig = jax.nn.sigmoid(gate_val)
    grad_gate = grad_swish * up_val * (sig * (1.0 + gate_val * (1.0 - sig)))
    grad_up = grad_swish * (gate_val * sig)
    grad_near = jnp.concatenate([grad_gate[:, :FF_CORE], grad_up[:, :FF_CORE]], axis=1).astype(BF)
    grad_far = jnp.concatenate([grad_gate[:, FF_CORE:], grad_up[:, FF_CORE:]], axis=1).astype(BF)
    grads = (
        dot_rows(own_unit, grad_near),
        dot_rows(own_unit, grad_far).astype(BF),
        dot_rows(swish, grad_out_own),
    )
    grad_unit = dot_back(grad_near, layer["wide"]) + dot_back(grad_far, layer["wide_far"])
    grad_unit = collect(grad_unit, *grads)
    grad_hidden = grad_out + normalize_back(unit, scale, grad_unit)
    return grad_hidden, *grads


def backward_mixer(grad_hidden, kept, layer, rows, core, reduce_rows, pending):
    (
        unit,
        scale,
        own_unit,
        own,
        gate_raw,
        attended,
        stat,
        starts,
        mixed,
        gated,
        mixer_low,
        ssm_scale,
    ) = kept
    grad_low = grad_hidden.astype(BF)
    grad_own = spread(grad_low)
    grad_mixer = dot_back(grad_own, rows["mamba"])
    grad_attended = dot_back(grad_own, rows["out"]).astype(BF)
    grad_scaled = grad_mixer * layer["gain"]
    near_heads, far_heads, heads_theirs = attend_back(core, own, stat, grad_attended)
    if reduce_rows is not None:
        grad_mamba, grad_out = dot_rows(mixer_low, grad_own), dot_rows(attended, grad_own)
        inner = chip_sums(grad_scaled * gated, near_heads, grad_mamba, grad_out)
    else:
        inner = chip_sums(grad_scaled * gated, near_heads)
    pull_back = ssm_scale * ssm_scale * ssm_scale * inner / INNER
    grad_gated = ssm_scale * grad_scaled - gated * pull_back
    sig = jax.nn.sigmoid(gate_raw)
    grad_mixed = (grad_gated * gate_raw * sig).astype(BF)
    grad_gate_raw = grad_gated * mixed * (sig * (1.0 + gate_raw * (1.0 - sig)))
    grad_recv = swap_cores(grad_mixed[:, LANES:])
    grad_gain = jnp.sum(grad_mixer * gated * ssm_scale, axis=0)
    mine, theirs, conv_grad, cols_grad = mixer_back(
        core, own, layer, starts, grad_mixed[:, :LANES], grad_recv
    )
    other = swap_cores(jnp.concatenate([theirs, heads_theirs], axis=1)).astype(F32)
    block = [slice(k * LANES, (k + 1) * LANES) for k in range(5)]
    if reduce_rows is not None:
        row_total = reduce_rows(grad_mamba, grad_out)
        mine = joined(mine, row_total)
    else:
        mine = joined(mine, pending)
    grad_near = jnp.concatenate(
        [
            grad_gate_raw[:, :LANES],
            mine[:, block[0]],
            mine[:, block[1]] + other[:, block[2]],
            near_heads + other[:, block[4]],
        ],
        axis=1,
    )
    grad_far = jnp.concatenate(
        [
            grad_gate_raw[:, LANES:],
            other[:, block[0]],
            mine[:, block[2]] + other[:, block[1]],
            far_heads + other[:, block[3]],
        ],
        axis=1,
    )
    grad_near, grad_far = grad_near.astype(BF), grad_far.astype(BF)
    near, far = dot_rows(own_unit, grad_near), dot_rows(own_unit, grad_far).astype(BF)
    if reduce_rows is None:
        low = joined(mixer_low, grad_near)
        grad_mamba = dot_rows(low, grad_own)
        grad_out = dot_rows(joined(attended, grad_near), grad_own)
        beside = near, far, grad_mamba, grad_out
        row_total = grad_mamba, grad_out
    else:
        beside = near, far
    grad_unit = dot_back(grad_near, layer["near"]) + dot_back(grad_far, layer["far"])
    grad_x = grad_hidden + normalize_back(unit, scale, collect(grad_unit, *beside))
    return grad_x, near, far, row_total, grad_gain, conv_grad, cols_grad


def section_pair(section, own, other):
    return jnp.where(section == 0, jnp.stack([own, other]), jnp.stack([other, own]))


def cut_in_kernel(w_ref, query_ref, key_ref, value_ref, gain_ref, conv_ref, out_ref):
    rows = w_ref.shape[0]
    gain = gain_ref[...]
    maps = 2 * INNER

    def piece(ref, at, width):
        return (ref[:, at : at + width].astype(F32) * gain).astype(BF)

    steps = piece(w_ref, maps + 2 * NS, NH)
    filler = jnp.zeros((rows, LANES - NARROW - NH), BF)
    rest = jnp.zeros((rows, LANES - 3 * HALF_HEAD), BF)
    for device in range(SHARDS):
        chip, core = device // CORES, device % CORES
        head = (chip // (CHIPS // KEY_VALUE_HEADS) * CORES + core) * HALF_HEAD
        cut = jnp.concatenate(
            [
                piece(w_ref, device * NARROW, NARROW),
                conv_ref[...],
                piece(w_ref, INNER + device * NARROW, NARROW),
                steps,
                filler,
                piece(w_ref, maps + core * NS, NS),
                piece(query_ref, device * HALF_HEAD, HALF_HEAD),
                piece(key_ref, head, HALF_HEAD),
                piece(value_ref, head, HALF_HEAD),
                rest,
            ],
            axis=1,
        )
        out_ref[device] = cut
        out_ref[SHARDS + device] = cut


def cut_wide_kernel(gate_ref, up_ref, gain_ref, out_ref):
    gain = gain_ref[...]
    for device in range(SHARDS):
        at = slice(device * FF_CORE, (device + 1) * FF_CORE)
        for k, ref in enumerate((gate_ref, up_ref)):
            cut = (ref[:, at].astype(F32) * gain).astype(BF)
            low = slice(k * FF_CORE, (k + 1) * FF_CORE)
            out_ref[device, :, low] = cut
            out_ref[SHARDS + device, :, low] = cut


def cut_call(kernel, columns, *operands):
    return pl.pallas_call(
        kernel,
        out_shape=jax.ShapeDtypeStruct((2 * SHARDS, operands[0].shape[0], columns), BF),
        in_specs=whole_vmem(len(operands)),
        out_specs=whole_vmem(1)[0],
        compiler_params=params(),
        cost_estimate=small_cost(),
    )(*operands)


def finish_kernel(in_width, total_ref, gain_ref, mid_ref, *refs):
    raw, outs, norms_ref = refs[:6], refs[6:12], refs[12]
    sums = []
    at = 0
    for k in range(6):
        width = raw[k].shape[1]
        part = slice(at, at + width)
        grad = total_ref[:, part].astype(F32)
        sums.append(jnp.sum(grad * raw[k][...].astype(F32), axis=1, keepdims=True))
        outs[k][...] = grad * (gain_ref if k < 4 else mid_ref)[...]
        at += in_width if k == 0 else width
    lane = lax.broadcasted_iota(jnp.int32, norms_ref.shape, 1)
    norm_in = sums[0] + sums[1] + sums[2] + sums[3]
    norms_ref[...] = jnp.where(lane == 0, norm_in, sums[4] + sums[5])


def finish(in_width, total, gain_in, gain_mid, raw):
    rows = total.shape[0]
    return pl.pallas_call(
        functools.partial(finish_kernel, in_width),
        out_shape=tuple(jax.ShapeDtypeStruct(w.shape, F32) for w in raw)
        + (jax.ShapeDtypeStruct((rows, LANES), F32),),
        in_specs=whole_vmem(9),
        out_specs=tuple(whole_vmem(7)),
        compiler_params=params(),
        cost_estimate=small_cost(),
    )(total, gain_in, gain_mid, *raw)


def body(
    inputs,
    cotangent,
    norm_in,
    w_in,
    conv_w,
    conv_b,
    dt_bias,
    a_log,
    skip_gain,
    norm_ssm,
    w_out,
    query_weight,
    key_weight,
    value_weight,
    output_weight,
    norm_mid,
    w_gate,
    w_up,
    w_down,
):
    place = lax.axis_index("shard")
    core = place % CORES
    core_word = core.reshape(1).astype(jnp.int32)
    section = lax.axis_index("section")
    reps = lax.axis_size("rep")
    local = inputs.shape[2]
    spare = LANES - NARROW

    gain_in = norm_in[0].astype(F32)[:, None]
    gain_mid = norm_mid[0].astype(F32)[:, None]

    own_input = lax.dynamic_index_in_dim(inputs[:, 0], section, 0, False).astype(F32)
    own_target = lax.dynamic_index_in_dim(cotangent[:, 0], section, 0, False)
    unit, scale = normalize(own_input)
    own_unit = spread(unit.astype(BF))
    conv_all = jnp.concatenate([conv_w[0], conv_b], axis=0)
    conv_count = conv_all.size
    conv_cols = jnp.concatenate(
        [conv_all.reshape(-1), jnp.zeros((spare * local - conv_count,), BF)]
    ).reshape(local, spare)
    cut = cut_call(
        cut_in_kernel,
        IN_COLS,
        w_in[0],
        query_weight[0],
        key_weight[0],
        value_weight[0],
        gain_in,
        conv_cols,
    )
    everywhere = ("section", "shard")
    met = lax.all_to_all(cut, everywhere, 0, 0, tiled=True)
    met = met.reshape(2, SHARDS, local, IN_COLS)
    conv_met = met[:, :, :, NARROW:LANES].reshape(2, SHARDS, spare * local)[:, :, :conv_count]
    conv_met = conv_met.reshape(2, SHARDS, CONV + 1, -1).transpose(0, 2, 1, 3)
    conv_met = conv_met.reshape(2, CONV + 1, INNER + 2 * NS).astype(F32)
    own_cols = met.reshape(2, SHARDS * local, IN_COLS)
    other_cols = swap_cores(own_cols)
    cut = cut_call(cut_wide_kernel, WIDE_COLS, w_gate[0], w_up[0], gain_mid)
    wide_cols = lax.all_to_all(cut, everywhere, 0, 0, tiled=True)
    wide_cols = wide_cols.reshape(2, SHARDS * local, WIDE_COLS)
    other_wide = swap_cores(wide_cols)

    def both_layers(own):
        return section_pair(section, own, swap_sections(own))

    raw_rows = jnp.concatenate([w_out[0], output_weight[0], w_down[0]], axis=0)
    raw_rows = joined(raw_rows, met)
    sent_rows = swap_sections(raw_rows)
    row_store = {}

    def rows_at(layer):
        def make(token):
            if not row_store:
                rows = section_pair(section, raw_rows, joined(sent_rows, token))
                row_store["pair"] = rows, swap_cores(rows)
            rows, others = (x[layer] for x in row_store["pair"])
            return {
                "mamba": jnp.concatenate([rows[:out_row], no_rows, others[:out_row], no_rows]),
                "out": jnp.concatenate([rows[out_row:down_row], others[out_row:down_row]]),
                "down": jnp.concatenate([rows[down_row:], others[down_row:]]),
            }

        return make

    out_row, down_row = NARROW, NARROW + HALF_HEAD
    per_head = jnp.concatenate([dt_bias[0], a_log[0], skip_gain[0], norm_ssm[0].astype(F32)])
    per_head = both_layers(per_head)
    own_gain = per_head[:, 3 * NH :]
    other_gain = swap_cores(own_gain)
    lane = lax.broadcasted_iota(jnp.int32, (NH, LANES), 1)
    head_of = jnp.where(lane < NARROW, (lane + place * NARROW) // HD, -1)
    member = (head_of == lax.broadcasted_iota(jnp.int32, (NH, LANES), 0)).astype(F32)
    sel = jnp.concatenate(
        [jnp.zeros((NARROW, LANES), F32), member, jnp.zeros((LANES - NARROW - NH, LANES), F32)]
    ).astype(BF)
    in_first = (head_of[0:1] == head_of[0:1, 0:1]).astype(F32)
    in_second = (head_of[0:1] == head_of[0:1, NARROW - 1 : NARROW]).astype(F32)

    def to_columns(values):
        return jnp.sum(values[:, None] * member, axis=0, keepdims=True)

    def padded(g):
        return jnp.concatenate([g, jnp.zeros((spare,), F32)])

    no_rows = jnp.zeros((spare, MODEL_WIDTH), BF)
    layers = []
    for layer in range(2):
        head_values = per_head[layer]
        cols = jnp.concatenate(
            [
                to_columns(head_values[:NH]),
                to_columns(jnp.exp(head_values[NH : 2 * NH])),
                to_columns(head_values[2 * NH : 3 * NH]),
                in_first,
                in_second,
                jnp.zeros((3, LANES), F32),
            ]
        )
        conv_own = jnp.concatenate(
            [
                lax.dynamic_slice_in_dim(conv_met[layer], place * NARROW, NARROW, axis=1),
                jnp.zeros((CONV + 1, spare), F32),
                by_place(core, conv_met[layer, :, INNER : INNER + NS], conv_met[layer, :, INNER + NS :], 1),
            ],
            axis=1,
        )
        layers.append(
            {
                "near": own_cols[layer],
                "far": other_cols[layer],
                "wide": wide_cols[layer],
                "wide_far": other_wide[layer],
                "conv": jnp.concatenate([conv_own, jnp.zeros((7 - CONV, CONVED), F32)]),
                "cols": cols,
                "sel": sel,
                "gain": jnp.concatenate([padded(own_gain[layer]), padded(other_gain[layer])])[None],
            }
        )

    x = own_input
    outs = []
    also = ()
    kept_mixer, kept_wide, row_weights = [], [], []
    for layer in range(2):
        if layer == 1:
            unit, scale = normalize(x)
            own_unit = spread(unit.astype(BF))
        hidden, kept, rows = forward_mixer(
            x, unit, scale, own_unit, layers[layer], core_word, also, rows_at(layer)
        )
        if layer == 0:
            target_own = gather_later(joined(own_target, hidden))
            also = (target_own,)
        row_weights.append(rows)
        kept_mixer.append(kept)
        partial, kept = forward_wide(hidden, layers[layer], rows)
        kept_wide.append(kept)
        total = collect(partial) if layer == 0 else collect_later(partial)
        outs.append((hidden + total).astype(BF))
        x = outs[layer].astype(F32)

    def exchanged(first, second):
        own = jnp.where(section == 0, first, second)
        other = swap_sections(jnp.where(section == 0, second, first).astype(BF))
        return section_pair(section, own, other.astype(own.dtype))

    part = local // reps

    def by_parts(columns):
        cut = columns.reshape(SHARDS, reps, part, columns.shape[1])
        return cut.transpose(1, 0, 2, 3).reshape(reps * SHARDS, part, columns.shape[1])

    def over_all(sent):
        met = lax.all_to_all(sent, ("section", "rep", "shard"), 0, 0, tiled=True)
        met = met.reshape(2 * reps, SHARDS, part, sent.shape[2])
        return jnp.sum(met.astype(F32), axis=0)

    extra_width = -(-(conv_count + NARROW + 3 * NH) // (reps * part))
    in_width = -(-(2 * INNER + 2 * NS + NH + extra_width) // LANES) * LANES

    def to_all(rows, axes, count):
        copies = jnp.broadcast_to(rows[None], (count,) + rows.shape)
        met = lax.all_to_all(copies, axes, 0, 0, tiled=True)
        return met.reshape(count * rows.shape[0], rows.shape[1])

    def even(g):
        return g.transpose(1, 0, 2).reshape(part, -1)

    def by_key_head(g):
        groups = CHIPS // KEY_VALUE_HEADS
        g = jnp.sum(g.reshape(KEY_VALUE_HEADS, groups, CORES, part, -1), axis=1)
        return even(g.reshape(KEY_VALUE_HEADS * CORES, part, -1))

    def by_weight(total):
        maps = total[:, :, 2 * LANES : 3 * LANES].reshape(CHIPS, CORES, part, LANES)
        heads = [
            total[:, :, 3 * LANES + k * HALF_HEAD : 3 * LANES + (k + 1) * HALF_HEAD]
            for k in range(3)
        ]
        columns = [
            even(total[:, :, :NARROW]),
            even(total[:, :, LANES : LANES + NARROW]),
            even(jnp.sum(maps, axis=0)),
            jnp.sum(total[:, :, LANES + NARROW : LANES + NARROW + NH], axis=0),
            jnp.sum(total[:, :, NARROW : NARROW + extra_width], axis=0),
            jnp.zeros((part, in_width - 2 * INNER - 2 * NS - NH - extra_width), F32),
            even(heads[0]),
            by_key_head(heads[1]),
            by_key_head(heads[2]),
            even(total[:, :, IN_COLS : IN_COLS + FF_CORE]),
            even(total[:, :, IN_COLS + FF_CORE :]),
        ]
        return jnp.concatenate(columns, axis=1).astype(BF)

    def pair_total(near, far):
        return (near + swap_cores(far).astype(F32)).astype(BF)

    def small_parts(grad_gain, conv_grad, cols_grad):
        conv_grad = conv_grad[: CONV + 1]
        maps_grad = by_place(core, conv_grad[:, LANES : 2 * LANES], conv_grad[:, 2 * LANES :], 1)
        conv_grad = jnp.concatenate(
            [
                lax.dynamic_update_slice_in_dim(
                    jnp.zeros((CONV + 1, INNER), F32), conv_grad[:, :NARROW], place * NARROW, axis=1
                ),
                maps_grad,
            ],
            axis=1,
        )
        conv_grad = conv_grad.reshape(CONV + 1, SHARDS, -1).transpose(1, 0, 2).reshape(SHARDS, -1)
        gain_halves = by_place(core, grad_gain[:NARROW], grad_gain[LANES : LANES + NARROW], 0)
        gain_grad = lax.dynamic_update_slice_in_dim(
            jnp.zeros((INNER,), F32), gain_halves, (place // CORES) * CORES * NARROW, axis=0
        ).reshape(SHARDS, -1)
        head_grad = jnp.sum(cols_grad[:3, None, :] * member[None], axis=2).reshape(1, -1)
        extra = jnp.concatenate(
            [conv_grad, gain_grad, jnp.broadcast_to(head_grad, (SHARDS, 3 * NH))], axis=1
        )
        width = -(-extra.shape[1] // (reps * part))
        missing = reps * part * width - extra.shape[1]
        extra = jnp.concatenate([extra, jnp.zeros((SHARDS, missing), F32)], axis=1)
        extra = extra.reshape(SHARDS, reps, part, width).transpose(1, 0, 2, 3)
        return extra.reshape(reps * SHARDS, part, width).astype(BF)

    def with_small(sent, extra):
        room = spare - extra.shape[2]
        extra = jnp.pad(extra, ((0, 0), (0, 0), (0, room)))
        return jnp.concatenate([sent[:, :, :NARROW], extra, sent[:, :, LANES:]], axis=2)

    def rows_of(grad_mamba, grad_out, grad_down):
        mine = jnp.concatenate([grad_mamba[:NARROW], grad_out[:HALF_HEAD], grad_down[:FF_CORE]])
        theirs = jnp.concatenate(
            [grad_mamba[LANES : LANES + NARROW], grad_out[HALF_HEAD:], grad_down[FF_CORE:]]
        )
        return pair_total(mine, theirs.astype(BF))

    def reduce_rows(grad_mamba, grad_out):
        first_rows = rows_of(grad_mamba, grad_out, grad_down)
        met = lax.all_to_all(
            jnp.concatenate([first_rows, last_rows]), ("section", "rep"), 0, 0, tiled=True
        )
        return met

    sent = [None, None]
    grad = own_target.astype(F32)
    input_grads = [None, None]
    for layer in (1, 0):
        grad_own = target_own if layer == 1 else spread(grad.astype(BF))
        grad_hidden, grad_wide, grad_wide_far, grad_down = backward_wide(
            grad, grad_own, kept_wide[layer], layers[layer], row_weights[layer]
        )
        grad_x, grad_near, grad_far, row_total, *small = backward_mixer(
            grad_hidden,
            kept_mixer[layer],
            layers[layer],
            row_weights[layer],
            core_word,
            reduce_rows if layer == 0 else None,
            total,
        )
        if layer == 1:
            last_rows = rows_of(*row_total, grad_down)
        input_grads[layer] = grad_x
        grad = grad_x.astype(BF).astype(F32)
        columns = [pair_total(grad_near, grad_far), pair_total(grad_wide, grad_wide_far)]
        columns = jnp.concatenate(columns, axis=1)
        sent[layer] = with_small(by_parts(columns), small_parts(*small))

    section_out = exchanged(outs[0], joined(outs[1], grad_near))[None, :, None]
    input_grad = exchanged(*input_grads)[None, :, None]
    row_total = row_total.reshape(2 * reps, -1, MODEL_WIDTH).astype(F32)
    row_total = jnp.sum(row_total, axis=0).astype(BF)
    columns = by_weight(over_all(jnp.concatenate(sent)))
    totals = to_all(jnp.concatenate([columns, row_total.reshape(part, -1)], axis=1), "rep", reps)
    columns = totals[:, : columns.shape[1]]
    row_total = totals[:, columns.shape[1] :].reshape(-1, MODEL_WIDTH).astype(F32)
    used = 2 * INNER + 2 * NS + NH
    extra = columns[:, used : used + extra_width].astype(F32).reshape(-1)
    conv_total = extra[:conv_count].reshape(CONV + 1, -1)
    gain_total = extra[conv_count : conv_count + NARROW]
    head_total = extra[conv_count + NARROW : conv_count + NARROW + 3 * NH].reshape(3, NH)
    raw = [w[0] for w in (w_in, query_weight, key_weight, value_weight, w_gate, w_up)]
    *by_rows, norms = finish(in_width, totals, gain_in, gain_mid, raw)
    grad_norm_in, grad_norm_mid = norms[:, 0], norms[:, 1]
    return (
        section_out,
        input_grad,
        grad_norm_in[None],
        by_rows[0][None],
        conv_total[:CONV][None],
        conv_total[CONV][None],
        head_total[0][None],
        head_total[1][None],
        head_total[2][None],
        gain_total[None],
        row_total[:out_row][None],
        by_rows[1][None],
        by_rows[2][None],
        by_rows[3][None],
        row_total[out_row:down_row][None],
        grad_norm_mid[None],
        by_rows[4][None],
        by_rows[5][None],
        row_total[down_row:][None],
    )


def solution(mesh):
    return jax.shard_map(
        body,
        mesh=mesh,
        in_specs=(
            P(None, "rep", "shard", None),
            P(None, "rep", "shard", None),
            P("section", "shard"),
            P("section", "shard", None),
            P("section", None, "shard"),
            P("section", "shard"),
            P("section", None),
            P("section", None),
            P("section", None),
            P("section", "shard"),
            P("section", "shard", None),
            P("section", "shard", None),
            P("section", "shard", None),
            P("section", "shard", None),
            P("section", "shard", None),
            P("section", "shard"),
            P("section", "shard", None),
            P("section", "shard", None),
            P("section", "shard", None),
        ),
        out_specs=(
            P("section", None, "rep", "shard", None),
            P("section", None, "rep", "shard", None),
            P("section", "shard"),
            P("section", "shard", None),
            P("section", None, "shard"),
            P("section", "shard"),
            P("section", None),
            P("section", None),
            P("section", None),
            P("section", "shard"),
            P("section", "shard", None),
            P("section", "shard", None),
            P("section", "shard", None),
            P("section", "shard", None),
            P("section", "shard", None),
            P("section", "shard"),
            P("section", "shard", None),
            P("section", "shard", None),
            P("section", "shard", None),
        ),
        check_vma=False,
    )
```
